32 devices in a mesh: dp: 8 (over y, x, core), tensor: 4 (over z).
Axes of the slice: x: 2, y: 2, z: 4, core: 2. Of those that a mesh axis runs over, the one named last changes fastest.
Arguments:
- layer_input: bfloat16 [32768, 1024], P('dp', 'tensor'), may hold values from -6 to 6
- out_cotangent: bfloat16 [32768, 1024], P('dp', 'tensor'), may hold values from -6 to 6
- norm_gains: float32 [2, 1024], P(None, 'tensor'), may hold values from 0.5 to 1.5
- proj_weight: bfloat16 [4, 1024, 1024], P(None, None, 'tensor'), may hold values from -0.1875 to 0.1875
- beta_weight: bfloat16 [1024, 8], P(None, 'tensor'), may hold values from -0.1875 to 0.1875
- conv_weight: float32 [3, 4, 1024], P(None, None, 'tensor'), may hold values from -0.6 to 0.6
- head_gain: float32 [128], replicated, may hold values from 0.5 to 1.5
- out_weight: bfloat16 [1024, 1024], P('tensor'), may hold values from -0.1875 to 0.1875
- mlp_weight: bfloat16 [2, 1024, 2816], P(None, None, 'tensor'), may hold values from -0.1875 to 0.1875
- down_weight: bfloat16 [2816, 1024], P('tensor'), may hold values from -0.109375 to 0.109375
- seq_lengths: int32 [32], replicated, may hold values from 64 to 2048, as said below
- seq_order: int32 [32], replicated, may hold values from 0 to 31, as said below
Outputs:
- layer_output: bfloat16 [32768, 1024], P('dp', 'tensor')
- input_grad: bfloat16 [32768, 1024], P('dp', 'tensor')
- grad_norm_gains: float32 [2, 1024], P(None, 'tensor')
- grad_proj: float32 [4, 1024, 1024], P(None, None, 'tensor')
- grad_beta: float32 [1024, 8], P(None, 'tensor')
- grad_conv: float32 [3, 4, 1024], P(None, None, 'tensor')
- grad_head_gain: float32 [128], replicated
- grad_out: float32 [1024, 1024], P('tensor')
- grad_mlp: float32 [2, 1024, 2816], P(None, None, 'tensor')
- grad_down: float32 [2816, 1024], P('tensor')
The draws below stay inside these ranges and needn't reach their ends.
Inputs may be any that keep to these rules, and one draw needn't show every extreme that they name: `seq_lengths`: each length is a multiple of 64. Taking the sequences in the order of seq_order, each consecutive run of 4 of them (the first, the second and so on) sums to 4096 tokens and holds one sequence of exactly 2048 tokens. `seq_order`: each sequence index appears once; entries j * 4 to (j + 1) * 4 - 1 list the sequences dealt to data group j.
All inputs are finite; a program needn't handle non-finite values.
Results may differ from the reference program's by a relative error of at most 0.011.
Values may be sent and summed in bfloat16 or wider, within the bound.
No kernel may reach another device: no remote copies, remote signals or barrier semaphores. Data moves between devices by JAX's collectives and lax.ppermute only.
A program may use at most 448 MiB of HBM per device.

```python
import jax
import jax.numpy as jnp
from jax import lax

D = 1024
HEADS = 8
HEAD_DIM = 128
FF = 2816
CONV = 4
BLOCK = 64
SEQ_GRP = 4
TOK_DEV = 4096
SEQS = 32
TOKENS = 32768
N_DP = 8


def deal_plan(key):
    group_count = SEQS // SEQ_GRP
    half_blocks = TOK_DEV // (2 * BLOCK)
    key_cut, key_mix, key_order = jax.random.split(key, 3)

    def one_group(cut_key, mix_key):
        chosen = jnp.sort(jax.random.permutation(cut_key, half_blocks - 1)[:SEQ_GRP - 2]).astype(jnp.int32)
        bounds = jnp.concatenate([jnp.full((1,), -1, jnp.int32), chosen, jnp.full((1,), half_blocks - 1, jnp.int32)])
        pieces = bounds[1:] - bounds[:-1]
        counts = jnp.concatenate([jnp.full((1,), half_blocks, jnp.int32), pieces])
        return counts[jax.random.permutation(mix_key, SEQ_GRP)]
    blocks_each = jax.vmap(one_group)(jax.random.split(key_cut, group_count), jax.random.split(key_mix, group_count))
    dealt_len = (blocks_each * BLOCK).reshape(-1).astype(jnp.int32)
    seq_order = jax.random.permutation(key_order, SEQS).astype(jnp.int32)
    seq_lengths = jnp.zeros((SEQS,), jnp.int32).at[seq_order].set(dealt_len)
    return (seq_lengths, seq_order)


def draw_seq_lengths(key, part):
    return deal_plan(jax.random.fold_in(key, 11))[0]


def draw_seq_order(key, part):
    return deal_plan(jax.random.fold_in(key, 11))[1]


def levels(stream_key, extent, shards, least, largest):
    level, own = 1.0, jax.random.fold_in(stream_key, 6)
    for dim, parts in shards:
        steps = jnp.exp(jax.random.uniform(jax.random.fold_in(own, dim), (parts,), jnp.float32, least / len(shards), largest / len(shards)))
        level = level * jnp.repeat(steps, extent[dim] // parts).reshape([-1 if axis == dim else 1 for axis in range(len(extent))])
    return level


def centred(stream_key, extent, width, most, cuts=(), held_as=jnp.bfloat16):
    values = width * jax.random.normal(stream_key, extent, jnp.float32)
    if cuts:
        values = values * levels(stream_key, extent, cuts, -0.22, 0.18)
    return jnp.clip(values, -most, most).astype(held_as)


def setup_inputs(seed: int = 0) -> dict:
    seeds = jax.random.split(jax.random.key(seed), 13)
    return {
        "layer_input": centred(seeds[0], (TOKENS, D), 1.0, 6.0, ((0, 8), (1, 4))),
        "out_cotangent": centred(seeds[1], (TOKENS, D), 1.0, 6.0, ((0, 8), (1, 4))),
        "norm_gains": jnp.clip(1.0 + 0.1 * jax.random.normal(seeds[2], (2, D), jnp.float32), 0.5, 1.5),
        "proj_weight": centred(seeds[3], (4, D, D), D ** -0.5, 0.1875, ((2, 4),)),
        "beta_weight": centred(seeds[4], (D, HEADS), D ** -0.5, 0.1875, ((1, 4),)),
        "conv_weight": jnp.clip(jax.random.uniform(seeds[5], (3, CONV, D), jnp.float32, -0.6, 0.6) * levels(seeds[5], (3, CONV, D), ((2, 4),), -0.4, 0.0), -0.6, 0.6),
        "head_gain": jnp.clip(1.0 + 0.1 * jax.random.normal(seeds[6], (HEAD_DIM,), jnp.float32), 0.5, 1.5),
        "out_weight": centred(seeds[7], (D, D), D ** -0.5, 0.1875, ((0, 4),)),
        "mlp_weight": centred(seeds[8], (2, D, FF), D ** -0.5, 0.1875, ((2, 4),)),
        "down_weight": centred(seeds[9], (FF, D), FF ** -0.5, 0.109375, ((0, 4),)),
        "seq_lengths": draw_seq_lengths(jax.random.fold_in(seeds[12], 71), 0),
        "seq_order": draw_seq_order(jax.random.fold_in(seeds[12], 71), 0),
    }


norm_eps = 1e-06
highest = lax.Precision.HIGHEST

@jax.custom_vjp
def low(v):
    return lax.optimization_barrier(v.astype(jnp.bfloat16)).astype(jnp.float32)

@jax.custom_vjp
def low_back(v):
    return v

def low_keep(v):
    return (low(v), None)

def low_pass(kept, grad):
    return (grad,)

def back_keep(v):
    return (v, None)

def back_low(kept, grad):
    return (low(grad),)
low.defvjp(low_keep, low_pass)
low_back.defvjp(back_keep, back_low)

def route_maps(seq_lengths, seq_order):
    seq_count = seq_lengths.shape[0]
    indices = jnp.arange(seq_count, dtype=jnp.int32)
    given_start = (jnp.cumsum(seq_lengths) - seq_lengths).astype(jnp.int32)
    chosen = seq_order[:, None] == indices[None, :]
    dealt_len = lax.optimization_barrier(jnp.sum(jnp.where(chosen, seq_lengths[None, :], 0), axis=1)).astype(jnp.int32)
    dealt_src = lax.optimization_barrier(jnp.sum(jnp.where(chosen, given_start[None, :], 0), axis=1)).astype(jnp.int32)
    dealt_start = (jnp.cumsum(dealt_len) - dealt_len).astype(jnp.int32)
    return (dealt_len, dealt_src, dealt_start)

def locate(places, dealt_len, dealt_src, dealt_start):
    inside = (places[:, None] >= dealt_start[None, :]) & (places[:, None] < (dealt_start + dealt_len)[None, :])
    source = places + lax.optimization_barrier(jnp.sum(jnp.where(inside, (dealt_src - dealt_start)[None, :], 0), axis=1)).astype(jnp.int32)
    position = places - lax.optimization_barrier(jnp.sum(jnp.where(inside, dealt_start[None, :], 0), axis=1)).astype(jnp.int32)
    return (source.astype(jnp.int32), position.astype(jnp.int32))

def unit_rows(values):
    return values * lax.rsqrt(lax.optimization_barrier(jnp.sum(jnp.square(values), axis=-1, keepdims=True)) + norm_eps)

def delta_rule(queries, key_rows, values, beta_gate, position):
    row_count, head_count, head_dim = queries.shape
    blocks = row_count // BLOCK

    def to_blocks(array_in):
        return jnp.transpose(array_in.reshape(blocks, BLOCK, head_count, array_in.shape[-1]), (0, 2, 1, 3))
    query_blocks = to_blocks(queries)
    key_blocks = to_blocks(key_rows)
    value_blocks = to_blocks(values)
    beta_blocks = to_blocks(beta_gate[:, :, None])
    keep_state = jnp.where(position.reshape(blocks, BLOCK)[:, 0] > 0, 1.0, 0.0).astype(jnp.float32)
    strict = jnp.tril(jnp.ones((BLOCK, BLOCK), jnp.float32), -1)
    causal = jnp.tril(jnp.ones((BLOCK, BLOCK), jnp.float32))
    key_gram = jnp.einsum('bhid,bhjd->bhij', key_blocks, key_blocks, precision=highest)
    system = jnp.eye(BLOCK, dtype=jnp.float32) + strict * beta_blocks * key_gram
    weighted = lax.linalg.triangular_solve(system, beta_blocks * key_blocks, left_side=True, lower=True, unit_diagonal=True)
    updates = lax.linalg.triangular_solve(system, beta_blocks * value_blocks, left_side=True, lower=True, unit_diagonal=True)
    scores = causal * jnp.einsum('bhid,bhjd->bhij', query_blocks, key_blocks, precision=highest)

    def advance(carried, packed):
        query_now, key_now, weighted_now, updates_now, scores_now, keep_now = packed
        begun = carried * keep_now
        corrected = updates_now - jnp.einsum('hid,hde->hie', weighted_now, begun, precision=highest)
        output = jnp.einsum('hid,hde->hie', query_now, begun, precision=highest)
        output = output + jnp.einsum('hij,hje->hie', scores_now, corrected, precision=highest)
        return (begun + jnp.einsum('hid,hie->hde', key_now, corrected, precision=highest), output)
    initial = jnp.zeros((head_count, head_dim, values.shape[-1]), jnp.float32)
    final_state, outputs = lax.scan(jax.checkpoint(advance), initial, (query_blocks, key_blocks, weighted, updates, scores, keep_state))
    return jnp.transpose(outputs, (0, 2, 1, 3)).reshape(row_count, head_count, values.shape[-1])

def mixer_core(qkv_pre, gate_pre, beta_pre, head_gain, conv_weight, position):
    tap_count = conv_weight.shape[1]
    row_count = gate_pre.shape[0]
    head_count = beta_pre.shape[1]
    head_dim = head_gain.shape[0]
    mixed = jnp.zeros_like(qkv_pre)
    for tap_index in range(tap_count):
        behind = tap_count - 1 - tap_index
        shifted = jnp.pad(qkv_pre, ((0, 0), (behind, 0), (0, 0)))[:, :row_count, :]
        usable = jnp.where(position >= behind, 1.0, 0.0).astype(jnp.float32)
        mixed = mixed + conv_weight[:, tap_index, :][:, None, :] * shifted * usable[None, :, None]
    active = jax.nn.silu(mixed).reshape(3, row_count, head_count, head_dim)
    queries = unit_rows(active[0]) * head_dim ** (-0.5)
    key_rows = unit_rows(active[1])
    outputs = delta_rule(queries, key_rows, active[2], jax.nn.sigmoid(beta_pre), position)
    normed = outputs * lax.rsqrt(lax.optimization_barrier(jnp.mean(jnp.square(outputs), axis=-1, keepdims=True)) + norm_eps) * head_gain
    return normed.reshape(row_count, head_count * head_dim) * jax.nn.silu(gate_pre)

def rms_scale(values):
    return lax.rsqrt(lax.optimization_barrier(jnp.mean(jnp.square(values), axis=-1, keepdims=True)) + norm_eps)

def block_forward(weights, rows_in, position):
    gains, projection, beta_proj, conv_taps, gain_head, output_proj, mlp_proj, down_proj = weights
    normed = low(rows_in * rms_scale(rows_in) * gains[0])
    projected = low_back(jnp.einsum('td,kde->kte', normed, projection, precision=highest))
    beta_pre = low_back(jnp.dot(normed, beta_proj, precision=highest))
    gated = mixer_core(projected[:3], projected[3], beta_pre, gain_head, conv_taps, position)
    mixed = low_back(jnp.dot(low(gated), output_proj, precision=highest))
    middle = rows_in + mixed
    normed_mid = low(middle * rms_scale(middle) * gains[1])
    gate_up = low_back(jnp.einsum('td,kdf->ktf', normed_mid, mlp_proj, precision=highest))
    hidden = low(jax.nn.silu(gate_up[0]) * gate_up[1])
    return middle + jnp.dot(hidden, down_proj, precision=highest)

def reference(layer_input, out_cotangent, norm_gains, proj_weight, beta_weight, conv_weight, head_gain, out_weight, mlp_weight, down_weight, seq_lengths, seq_order):
    total_rows = layer_input.shape[0]
    dealt_len, dealt_src, dealt_start = route_maps(seq_lengths, seq_order)
    source, position = locate(jnp.arange(total_rows, dtype=jnp.int32), dealt_len, dealt_src, dealt_start)
    dealt_in = layer_input.astype(jnp.float32)[source]
    dealt_cot = out_cotangent.astype(jnp.float32)[source]
    weights = (norm_gains, proj_weight.astype(jnp.float32), beta_weight.astype(jnp.float32), conv_weight, head_gain, out_weight.astype(jnp.float32), mlp_weight.astype(jnp.float32), down_weight.astype(jnp.float32))
    grouped_pos = position.reshape(N_DP, TOK_DEV)
    run_block = jax.checkpoint(block_forward)

    def forward(params_in, rows_in):

        def one_group(carried, packed):
            return (carried, run_block(params_in, packed[0], packed[1]))
        unused, outputs = lax.scan(one_group, jnp.zeros((), jnp.float32), (rows_in.reshape(N_DP, TOK_DEV, -1), grouped_pos))
        return outputs.reshape(total_rows, -1)
    result, pullback = jax.vjp(forward, weights, dealt_in)
    grads, grad_rows = pullback(dealt_cot)
    layer_output = jnp.zeros_like(result).at[source].set(result).astype(jnp.bfloat16)
    input_grad = jnp.zeros_like(grad_rows).at[source].set(grad_rows).astype(jnp.bfloat16)
    return (layer_output, input_grad, grads[0], grads[1], grads[2], grads[3], grads[4], grads[5], grads[6], grads[7])
```

```python
import functools

import jax
import jax.numpy as jnp
from jax import lax
from jax.experimental import pallas as pl
from jax.experimental.pallas import tpu as pltpu
from jax.sharding import Mesh, PartitionSpec as P

CH = 128
HALF = 64
HD = 128
TAPS = 4
EPS = 1e-6
f32, bf16 = jnp.float32, jnp.bfloat16


def mm(a, b, ca=1, cb=0):
    return lax.dot_general(
        a.astype(bf16), b.astype(bf16), (((ca,), (cb,)), ((), ())), preferred_element_type=f32
    )


def nt(a, b):
    return mm(a, b, 1, 1)


def grid_ids():
    row = lax.broadcasted_iota(jnp.int32, (CH, CH), 0)
    col = lax.broadcasted_iota(jnp.int32, (CH, CH), 1)
    return row, col


def inverse(systems):
    row, col = grid_ids()
    eye = jnp.where(row == col, 1.0, 0.0)
    pair = (row // 2 == col // 2) & (row > col)
    found = [eye - jnp.where(pair, a, 0.0) for a in systems]
    size = 2
    while size < CH:
        inside = (
            (row // (2 * size) == col // (2 * size))
            & ((row // size) % 2 == 1)
            & ((col // size) % 2 == 0)
        )
        right = [mm(jnp.where(inside, a, 0.0), t) for a, t in zip(systems, found)]
        found = [t - mm(t, r) for t, r in zip(found, right)]
        size *= 2
    return found


def behind(rows, before, open0, open1):
    return (
        jnp.concatenate([before * open0, rows[:HALF]], axis=0),
        jnp.concatenate([rows[HALF - 8 : HALF] * open1, rows[HALF:]], axis=0),
    )


def shift_down(halves, s):
    return jnp.concatenate([h[8 - s : 8 - s + HALF] for h in halves], axis=0)


def shift_up(halves, s):
    return jnp.concatenate([h[s : s + HALF] for h in halves], axis=0)


def head(x, h):
    return x[:, h * HD : (h + 1) * HD]


def convolve(rows, before, taps, open0, open1):
    halves = behind(rows, before, open0, open1)
    mixed = taps[TAPS - 1 : TAPS] * rows
    for s in range(1, TAPS):
        mixed = mixed + taps[TAPS - 1 - s : TAPS - s] * shift_down(halves, s)
    return mixed


def unit(z):
    return lax.rsqrt(jnp.sum(z * z, axis=1, keepdims=True) + EPS)


def forward_kernel(
    starts, proj, before, beta_in, conv, gain, gated_out, s_out, t_out, e_out, o_out, state, *, heads
):
    i = pl.program_id(0)

    @pl.when(i == 0)
    def _():
        state[...] = jnp.zeros_like(state)

    open0 = 1.0 - starts[2 * i].astype(f32)
    open1 = 1.0 - starts[2 * i + 1].astype(f32)
    row, col = grid_ids()
    r1 = lax.broadcasted_iota(jnp.int32, (CH, 1), 0)
    sees = jnp.where(r1 < HALF, 1.0, open1)
    lasts = jnp.where(r1 < HALF, open1, 1.0)
    joined = jnp.where((row >= HALF) & (col < HALF), open1, 1.0)
    causal = jnp.where(row >= col, joined, 0.0)
    strict = jnp.where(row > col, joined, 0.0)

    acts = []
    for k in range(3):
        mixed = convolve(proj[k], before[k], conv[k], open0, open1)
        acts.append(mixed * jax.nn.sigmoid(mixed))
    beta = jax.nn.sigmoid(beta_in[...])
    gate = proj[3]
    gate = gate * jax.nn.sigmoid(gate)

    q, k, v, b, grams, scores = [], [], [], [], [], []
    for h in range(heads):
        qa, ka = head(acts[0], h), head(acts[1], h)
        q.append(qa * (unit(qa) * HD**-0.5))
        k.append(ka * unit(ka))
        v.append(head(acts[2], h))
        b.append(beta[:, h : h + 1])
        both = nt(jnp.concatenate([k[h], q[h]], axis=0), k[h])
        grams.append(strict * both[:CH])
        scores.append(causal * both[CH:])
    solved = inverse([b[h] * grams[h] for h in range(heads)])
    for h in range(heads):
        begun = state[h] * open0
        seen = mm(jnp.concatenate([sees * k[h], sees * q[h]], axis=0), begun)
        rest = v[h] - seen[:CH]
        delta = mm(solved[h], b[h] * rest)
        err = rest - mm(grams[h], delta)
        delta = b[h] * err
        out = seen[CH:] + mm(scores[h], delta)
        state[h] = open1 * begun + mm(jnp.transpose(lasts * k[h]), delta)
        s_out[0, h] = begun.astype(s_out.dtype)
        t_out[0, h] = jnp.transpose(solved[h]).astype(t_out.dtype)
        e_out[:, h * HD : (h + 1) * HD] = err.astype(e_out.dtype)
        o_out[:, h * HD : (h + 1) * HD] = out.astype(o_out.dtype)
        rho = lax.rsqrt(jnp.mean(out * out, axis=1, keepdims=True) + EPS)
        gated_out[:, h * HD : (h + 1) * HD] = (out * rho * gain[...] * head(gate, h)).astype(
            gated_out.dtype
        )


def backward_kernel(
    starts,
    proj,
    before,
    beta_in,
    conv,
    gain,
    s_in,
    t_in,
    e_in,
    o_in,
    gg_in,
    gpre,
    gbeta,
    gconv,
    ggain,
    dstate,
    after,
    *,
    heads,
    blocks,
):
    step = pl.program_id(0)
    i = blocks - 1 - step

    @pl.when(step == 0)
    def _():
        dstate[...] = jnp.zeros_like(dstate)
        after[...] = jnp.zeros_like(after)
        gconv[...] = jnp.zeros_like(gconv)
        ggain[...] = jnp.zeros_like(ggain)

    open0 = 1.0 - starts[2 * i].astype(f32)
    open1 = 1.0 - starts[2 * i + 1].astype(f32)
    open2 = 1.0 - starts[2 * i + 2].astype(f32)
    row, col = grid_ids()
    r1 = lax.broadcasted_iota(jnp.int32, (CH, 1), 0)
    sees = jnp.where(r1 < HALF, 1.0, open1)
    lasts = jnp.where(r1 < HALF, open1, 1.0)
    joined = jnp.where((row >= HALF) & (col < HALF), open1, 1.0)
    causal = jnp.where(row >= col, joined, 0.0)
    strict = jnp.where(row > col, joined, 0.0)
    joined_t = jnp.where((col >= HALF) & (row < HALF), open1, 1.0)
    causal_t = jnp.where(col >= row, joined_t, 0.0)
    strict_t = jnp.where(col > row, joined_t, 0.0)

    mixed, acts, sig = [], [], []
    for k in range(3):
        mixed.append(convolve(proj[k], before[k], conv[k], open0, open1))
        sig.append(jax.nn.sigmoid(mixed[k]))
        acts.append(mixed[k] * sig[k])
    beta = jax.nn.sigmoid(beta_in[...])
    gate = proj[3]
    sg = jax.nn.sigmoid(gate)
    silu_gate = gate * sg
    gain_row = gain[...]

    dacts = [[], [], []]
    dbetas = []
    total_gain = jnp.zeros((1, HD), f32)
    for h in range(heads):
        lanes = slice(h * HD, (h + 1) * HD)
        qa, ka = head(acts[0], h), head(acts[1], h)
        rq, rk = unit(qa), unit(ka)
        q, k = qa * (rq * HD**-0.5), ka * rk
        b = beta[:, h : h + 1]
        out = o_in[:, lanes].astype(f32)
        gg = gg_in[:, lanes].astype(f32)
        rho = lax.rsqrt(jnp.mean(out * out, axis=1, keepdims=True) + EPS)
        unit_out = out * rho
        g, s = head(gate, h), head(sg, h)
        gpre[3, :, lanes] = (gg * (unit_out * gain_row) * s * (1.0 + g * (1.0 - s))).astype(gpre.dtype)
        dn = gg * head(silu_gate, h)
        total_gain = total_gain + jnp.sum(dn * unit_out, axis=0, keepdims=True)
        dn = dn * gain_row
        do = rho * dn - unit_out * (rho * jnp.mean(dn * unit_out, axis=1, keepdims=True))

        begun = s_in[0, h]
        ds = dstate[h]
        err = e_in[:, lanes].astype(f32)
        delta = b * err
        scores_t = causal_t * nt(k, q)
        ddelta = mm(scores_t, do) + mm(lasts * k, ds)
        dx = mm(t_in[0, h], ddelta)
        dr = b * dx
        dbetas.append(jnp.sum(dx * err, axis=1, keepdims=True))
        both = jnp.concatenate([do, dr], axis=0)
        pair = nt(both, delta)
        pair_t = nt(delta, both)
        dp = causal * pair[:CH]
        dp_t = causal_t * pair_t[:, :CH]
        w = strict * pair[CH:] + strict_t * pair_t[:, CH:]
        through = nt(both, begun)
        from_k = mm(jnp.concatenate([dp, w], axis=0), k)
        dq = sees * through[:CH] + from_k[:CH]
        dk = lasts * nt(delta, ds) - sees * through[CH:] + mm(dp_t, q) - from_k[CH:]
        turned = jnp.transpose(jnp.concatenate([sees * q, -sees * k], axis=0))
        dstate[h] = open0 * (open1 * ds + mm(turned, both))

        dq = dq * HD**-0.5
        dacts[0].append(rq * dq - qa * (rq * rq * rq * jnp.sum(qa * dq, axis=1, keepdims=True)))
        dacts[1].append(rk * dk - ka * (rk * rk * rk * jnp.sum(ka * dk, axis=1, keepdims=True)))
        dacts[2].append(dr)
    ggain[...] += total_gain
    gbeta[...] = jnp.concatenate(dbetas, axis=1) * beta * (1.0 - beta)
    for k in range(3):
        dact = jnp.concatenate(dacts[k], axis=1)
        dmix = dact * sig[k] * (1.0 + mixed[k] * (1.0 - sig[k]))
        pre = behind(proj[k], before[k], open0, open1)
        nxt = (
            jnp.concatenate([dmix[:HALF], dmix[HALF : HALF + 8] * open1], axis=0),
            jnp.concatenate([dmix[HALF:], after[k] * open2], axis=0),
        )
        dpre = conv[k, TAPS - 1 : TAPS] * dmix
        gconv[k, TAPS - 1 : TAPS] += jnp.sum(dmix * proj[k], axis=0, keepdims=True)
        for s in range(1, TAPS):
            dpre = dpre + conv[k, TAPS - 1 - s : TAPS - s] * shift_up(nxt, s)
            gconv[k, TAPS - 1 - s : TAPS - s] += jnp.sum(
                dmix * shift_down(pre, s), axis=0, keepdims=True
            )
        after[k] = dmix[:8]
        gpre[k] = dpre.astype(gpre.dtype)


def mixer_forward(starts, proj, beta_pre, conv, gain):
    rows, width = proj.shape[1:]
    heads = width // HD
    blocks = rows // CH
    per = CH // 8
    at = lambda i, s: lax.rem(i + s[2 * blocks + 1], blocks)
    prior = lambda i, s: at(jnp.maximum(i - 1, 0), s) * per + per - 1
    return pl.pallas_call(
        functools.partial(forward_kernel, heads=heads),
        grid_spec=pltpu.PrefetchScalarGridSpec(
            num_scalar_prefetch=1,
            grid=(blocks,),
            in_specs=[
                pl.BlockSpec((4, CH, width), lambda i, s: (0, at(i, s), 0)),
                pl.BlockSpec((4, 8, width), lambda i, s: (0, prior(i, s), 0)),
                pl.BlockSpec((CH, heads), lambda i, s: (at(i, s), 0)),
                pl.BlockSpec((3, TAPS, width), lambda i, s: (0, 0, 0)),
                pl.BlockSpec((1, HD), lambda i, s: (0, 0)),
            ],
            out_specs=[
                pl.BlockSpec((CH, width), lambda i, s: (at(i, s), 0)),
                pl.BlockSpec((1, heads, HD, HD), lambda i, s: (i, 0, 0, 0)),
                pl.BlockSpec((1, heads, CH, CH), lambda i, s: (i, 0, 0, 0)),
                pl.BlockSpec((CH, width), lambda i, s: (i, 0)),
                pl.BlockSpec((CH, width), lambda i, s: (i, 0)),
            ],
            scratch_shapes=[pltpu.VMEM((heads, HD, HD), f32)],
        ),
        out_shape=[
            jax.ShapeDtypeStruct((rows, width), bf16),
            jax.ShapeDtypeStruct((blocks, heads, HD, HD), bf16),
            jax.ShapeDtypeStruct((blocks, heads, CH, CH), bf16),
            jax.ShapeDtypeStruct((rows, width), f32),
            jax.ShapeDtypeStruct((rows, width), f32),
        ],
        compiler_params=pltpu.CompilerParams(vmem_limit_bytes=56 * 1024 * 1024),
    )(starts, proj, proj, beta_pre, conv, gain)


def mixer_backward(starts, proj, beta_pre, conv, gain, saved, grad_gated):
    rows, width = proj.shape[1:]
    heads = width // HD
    blocks = rows // CH
    per = CH // 8
    back = lambda i: blocks - 1 - i
    at = lambda i, s: lax.rem(back(i) + s[2 * blocks + 1], blocks)
    prior = lambda i, s: at(jnp.minimum(i + 1, blocks - 1), s) * per + per - 1
    return pl.pallas_call(
        functools.partial(backward_kernel, heads=heads, blocks=blocks),
        grid_spec=pltpu.PrefetchScalarGridSpec(
            num_scalar_prefetch=1,
            grid=(blocks,),
            in_specs=[
                pl.BlockSpec((4, CH, width), lambda i, s: (0, at(i, s), 0)),
                pl.BlockSpec((4, 8, width), lambda i, s: (0, prior(i, s), 0)),
                pl.BlockSpec((CH, heads), lambda i, s: (at(i, s), 0)),
                pl.BlockSpec((3, TAPS, width), lambda i, s: (0, 0, 0)),
                pl.BlockSpec((1, HD), lambda i, s: (0, 0)),
                pl.BlockSpec((1, heads, HD, HD), lambda i, s: (back(i), 0, 0, 0)),
                pl.BlockSpec((1, heads, CH, CH), lambda i, s: (back(i), 0, 0, 0)),
                pl.BlockSpec((CH, width), lambda i, s: (back(i), 0)),
                pl.BlockSpec((CH, width), lambda i, s: (back(i), 0)),
                pl.BlockSpec((CH, width), lambda i, s: (at(i, s), 0)),
            ],
            out_specs=[
                pl.BlockSpec((4, CH, width), lambda i, s: (0, at(i, s), 0)),
                pl.BlockSpec((CH, heads), lambda i, s: (at(i, s), 0)),
                pl.BlockSpec((3, TAPS, width), lambda i, s: (0, 0, 0)),
                pl.BlockSpec((1, HD), lambda i, s: (0, 0)),
            ],
            scratch_shapes=[pltpu.VMEM((heads, HD, HD), f32), pltpu.VMEM((3, 8, width), f32)],
        ),
        out_shape=[
            jax.ShapeDtypeStruct((4, rows, width), bf16),
            jax.ShapeDtypeStruct((rows, heads), f32),
            jax.ShapeDtypeStruct((3, TAPS, width), f32),
            jax.ShapeDtypeStruct((1, HD), f32),
        ],
        compiler_params=pltpu.CompilerParams(vmem_limit_bytes=56 * 1024 * 1024),
    )(starts, proj, proj, beta_pre, conv, gain, *saved, grad_gated)


BLOCK = 64
EVERY = ("chip", "core", "tensor")
GROUPS = ("chip", "core")


def per_match(places, starts, lengths, values):
    inside = (places[:, None] >= starts[None, :]) & (places[:, None] < (starts + lengths)[None, :])
    return jnp.sum(jnp.where(inside, values[None, :], 0), axis=1)


def total_before(counts):
    size = counts.shape[-1]
    earlier = jnp.tri(size, k=-1, dtype=jnp.int32)
    return jnp.sum(counts[..., None, :] * earlier, axis=-1)


def gather_kernel(index, source, target):
    def move(j, carried):
        target[j] = source[index[j]]
        return carried

    lax.fori_loop(0, target.shape[0], move, 0, unroll=8)


def reorder(blocks, index):
    count, unit, _ = blocks.shape
    if unit % 8:
        chosen = (index[:, None] == jnp.arange(count, dtype=jnp.int32)[None, :]).astype(blocks.dtype)
        return jnp.einsum("ab,buc->auc", chosen, blocks)
    whole = pl.BlockSpec(blocks.shape, lambda i, s: (0, 0, 0))
    return pl.pallas_call(
        gather_kernel,
        grid_spec=pltpu.PrefetchScalarGridSpec(
            num_scalar_prefetch=1, grid=(1,), in_specs=[whole], out_specs=whole
        ),
        out_shape=jax.ShapeDtypeStruct(blocks.shape, blocks.dtype),
        compiler_params=pltpu.CompilerParams(vmem_limit_bytes=32 * 1024 * 1024),
    )(index, blocks)


def routing(seq_lengths, seq_order, groups, rows, depth):
    count = seq_lengths.shape[0]
    per_group = count // groups
    half = rows // (2 * BLOCK)
    part = half // 2
    total = groups * rows // BLOCK
    lengths = seq_lengths // BLOCK
    given = total_before(lengths)
    chosen = seq_order[:, None] == jnp.arange(count, dtype=jnp.int32)[None, :]
    dealt_len = jnp.sum(jnp.where(chosen, lengths[None, :], 0), axis=1)
    dealt_src = jnp.sum(jnp.where(chosen, given[None, :], 0), axis=1)
    by_group = dealt_len.reshape(groups, per_group)
    is_long = by_group == half
    short = jnp.where(is_long, 0, by_group)
    inner = jnp.where(is_long, 0, half + total_before(short))
    base = jnp.arange(groups, dtype=jnp.int32)[:, None] * (2 * half)
    placed = (base + inner).reshape(-1)
    order = jnp.arange(total, dtype=jnp.int32)
    piece, offset = order // part, order % part
    chip, core, plane = piece // (2 * depth), (piece // depth) % 2, piece % depth
    places = (chip * depth + plane) * half + core * part + offset
    take = places + per_match(places, placed, dealt_len, dealt_src - placed)
    goes = order + per_match(order, dealt_src, dealt_len, placed - dealt_src)
    unit, within = goes // half, goes % half
    back = (((unit // depth) * 2 + within // part) * depth + unit % depth) * part + within % part
    own = lax.axis_index("chip") * depth + lax.axis_index("tensor")
    own_places = own * half + jnp.arange(half, dtype=jnp.int32)
    begins = jnp.any(own_places[:, None] == placed[None, :], axis=1).astype(jnp.int32)
    shift = lax.axis_index("core") * (half // 4)
    marks = jnp.concatenate([begins, jnp.ones((1,), jnp.int32), shift.astype(jnp.int32)[None]])
    return take, back, marks


def route_in(values, take, groups):
    rows, columns = values.shape
    blocks, unit = rows // BLOCK, BLOCK // groups
    spread = jnp.swapaxes(values.reshape(blocks, groups, unit, columns), 0, 1)
    spread = lax.all_to_all(spread, GROUPS, 0, 0, tiled=True)
    picked = reorder(spread.reshape(blocks * groups, unit, columns), take)
    depth = lax.axis_size("tensor")
    part = blocks * groups // (groups * depth)
    routed = lax.all_to_all(picked.reshape(groups * depth, part, unit, columns), EVERY, 0, 0, tiled=True)
    routed = routed.reshape(groups, depth, part, unit, columns).transpose(2, 0, 3, 1, 4)
    return routed.reshape(part * BLOCK, depth * columns)


def route_out(values, back, groups):
    rows, width = values.shape
    depth = lax.axis_size("tensor")
    part, unit, columns = rows // BLOCK, BLOCK // groups, width // depth
    parted = values.reshape(part, groups, unit, depth, columns).transpose(1, 3, 0, 2, 4)
    parted = parted.reshape(groups * depth, part, unit, columns)
    held = lax.all_to_all(parted, EVERY, 0, 0, tiled=True)
    held = reorder(held.reshape(groups * depth * part, unit, columns), back)
    blocks = depth * part
    home = lax.all_to_all(held.reshape(groups, blocks, unit, columns), GROUPS, 0, 0, tiled=True)
    return jnp.swapaxes(home, 0, 1).reshape(blocks * BLOCK, columns)


def swap(values):
    return lax.ppermute(values, "core", [(0, 1), (1, 0)])


def dot(a, b):
    return jnp.dot(a, b, preferred_element_type=f32)


def norm_back(values, scale, gain, grad_normed, width):
    weighted = gain * grad_normed
    along = jnp.sum(weighted * values, axis=1, keepdims=True)
    grad_values = scale * weighted - values * (scale * scale * scale) * along / width
    return grad_values, jnp.sum(grad_normed * values * scale, axis=0)


def reduce_parts(parts, chips, depth):
    _, _, rows, columns = parts.shape
    summed = lax.psum_scatter(parts.reshape(chips * depth * rows, columns), "chip", scatter_dimension=0, tiled=True)
    summed = lax.psum_scatter(summed, "tensor", scatter_dimension=0, tiled=True)
    full = lax.all_gather(summed, GROUPS, axis=0)
    return full.reshape(chips, 2, rows, columns).astype(f32)


def on_device(
    layer_input,
    out_cotangent,
    norm_gains,
    proj_weight,
    beta_weight,
    conv_weight,
    head_gain,
    out_weight,
    mlp_weight,
    down_weight,
    seq_lengths,
    seq_order,
):
    rows, columns = layer_input.shape
    depth = lax.axis_size("tensor")
    chips = lax.axis_size("chip")
    groups = 2 * chips
    width = columns * depth
    own_rows = rows // 4
    core = lax.axis_index("core")

    def mine(array, axis):
        size = array.shape[axis] // 2
        return jnp.where(
            core == 0,
            lax.slice_in_dim(array, 0, size, axis=axis),
            lax.slice_in_dim(array, size, 2 * size, axis=axis),
        )

    take, back, marks = routing(seq_lengths, seq_order, groups, rows, depth)
    rows_own = route_in(layer_input, take, groups)

    hidden_half = down_weight.shape[0] // 2
    padded = -(-hidden_half // 128) * 128
    extra = padded - hidden_half
    proj = lax.all_gather(mine(proj_weight, 2), "tensor", axis=2, tiled=True)
    small = jnp.concatenate(
        [
            mine(beta_weight, 1).astype(f32).reshape(-1),
            norm_gains.reshape(-1),
            mine(conv_weight, 2).reshape(-1),
        ]
    )
    small = lax.all_gather(small, "tensor", axis=0)
    beta_proj = small[:, :width].T.astype(bf16)
    gains = small[:, width : width + 2 * columns].reshape(depth, 2, columns)
    gains = jnp.swapaxes(gains, 0, 1).reshape(2, width)
    conv = small[:, width + 2 * columns :].reshape(depth, 3, TAPS, HD)
    conv = conv.transpose(1, 2, 0, 3).reshape(3, TAPS, depth * HD)
    out_proj = lax.all_gather(mine(out_weight, 0), "tensor", axis=0, tiled=True)
    mlp_half = jnp.pad(mine(mlp_weight, 2), ((0, 0), (0, 0), (0, extra)))
    mlp = lax.all_gather(mlp_half, "tensor", axis=2, tiled=True)
    down_half = jnp.pad(mine(down_weight, 0), ((0, extra), (0, 0)))
    down = lax.all_gather(down_half, "tensor", axis=0, tiled=True)

    low = jnp.concatenate([rows_own, swap(rows_own)], axis=0)
    all_rows = low.astype(f32)
    scale_all = lax.rsqrt(jnp.mean(jnp.square(all_rows), axis=1, keepdims=True) + EPS)
    normed = (all_rows * scale_all * gains[0]).astype(bf16)
    projected = jnp.einsum("td,kde->kte", normed, proj, preferred_element_type=f32)
    beta_pre = dot(normed, beta_proj)
    gain_row = head_gain[None, :]
    gated, *saved = mixer_forward(marks, projected, beta_pre, conv, gain_row)

    cot_own = route_in(out_cotangent, take, groups)
    cot = jnp.concatenate([cot_own, swap(cot_own)], axis=0)

    rows_f = rows_own.astype(f32)
    scale_in = scale_all[:own_rows]
    mixed = swap(dot(gated[own_rows:], out_proj).astype(bf16))
    middle = rows_f + dot(gated[:own_rows], out_proj) + mixed.astype(f32)
    scale_mid = lax.rsqrt(jnp.mean(jnp.square(middle), axis=1, keepdims=True) + EPS)
    normed_mid_own = (middle * scale_mid * gains[1]).astype(bf16)
    normed_mid = jnp.concatenate([normed_mid_own, swap(normed_mid_own)], axis=0)

    gate_up = jnp.einsum("td,kdf->ktf", normed_mid, mlp, preferred_element_type=f32)
    sigmoid_gate = jax.nn.sigmoid(gate_up[0])
    activated = gate_up[0] * sigmoid_gate
    hidden = (activated * gate_up[1]).astype(bf16)
    lower = swap(dot(hidden[own_rows:], down).astype(bf16))
    total = middle + dot(hidden[:own_rows], down) + lower.astype(f32)
    layer_output = route_out(total.astype(bf16), back, groups)

    grad_hidden = jnp.einsum("td,fd->tf", cot, down, preferred_element_type=f32)
    grad_gate = grad_hidden * gate_up[1] * sigmoid_gate * (1.0 + gate_up[0] * (1.0 - sigmoid_gate))
    grad_gate_up = jnp.stack([grad_gate, grad_hidden * activated]).astype(bf16)
    from_mlp = lambda part: jnp.einsum("ktf,kdf->td", part, mlp, preferred_element_type=f32)
    came = swap(from_mlp(grad_gate_up[:, own_rows:]).astype(bf16))
    grad_normed_mid = from_mlp(grad_gate_up[:, :own_rows]) + came.astype(f32)
    mid_back, grad_gain_mid = norm_back(middle, scale_mid, gains[1], grad_normed_mid, width)
    grad_middle = cot_own.astype(f32) + mid_back
    grad_mix_own = grad_middle.astype(bf16)
    grad_mix = jnp.concatenate([grad_mix_own, swap(grad_mix_own)], axis=0)
    grad_gated = jnp.einsum("td,ed->te", grad_mix, out_proj, preferred_element_type=f32)

    grad_down = jnp.einsum("tf,td->fd", hidden, cot, preferred_element_type=f32).astype(bf16)
    grad_mlp = jnp.einsum("td,ktf->kdf", normed_mid, grad_gate_up, preferred_element_type=f32).astype(bf16)
    grad_out = jnp.einsum("te,td->ed", gated, grad_mix, preferred_element_type=f32).astype(bf16)

    grad_pre, grad_beta_pre, grad_conv, grad_head = mixer_backward(
        marks, projected, beta_pre, conv, gain_row, saved, grad_gated
    )
    grad_beta_low = grad_beta_pre.astype(bf16)

    def from_proj(part):
        term = jnp.einsum("kte,kde->td", grad_pre[:, part], proj, preferred_element_type=f32)
        return term + jnp.einsum("th,dh->td", grad_beta_low[part], beta_proj, preferred_element_type=f32)

    came = swap(from_proj(slice(own_rows, None)).astype(bf16))
    grad_normed = from_proj(slice(0, own_rows)) + came.astype(f32)
    in_back, grad_gain_in = norm_back(rows_f, scale_in, gains[0], grad_normed, width)
    grad_input = (grad_middle + in_back).astype(bf16)
    input_grad = route_out(grad_input, back, groups)
    grad_proj = jnp.einsum("td,kte->kde", normed, grad_pre, preferred_element_type=f32)
    grad_beta = jnp.einsum("td,th->hd", normed, grad_beta_low, preferred_element_type=f32)

    down_parts = jnp.swapaxes(grad_down.reshape(depth, chips, padded // chips, width), 0, 1)
    down_full = reduce_parts(down_parts, chips, depth)
    down_full = jnp.swapaxes(down_full, 0, 1).reshape(2, padded, width)
    grad_down_out = down_full[:, :hidden_half].reshape(2 * hidden_half, width)

    mlp_parts = grad_mlp.reshape(chips, 2 * width // chips, depth, padded)
    mlp_full = reduce_parts(jnp.swapaxes(mlp_parts, 1, 2), chips, depth)
    mlp_full = mlp_full[:, :, :, :hidden_half].transpose(0, 2, 1, 3)
    grad_mlp_out = mlp_full.reshape(2, width, 2 * hidden_half)

    out_parts = jnp.swapaxes(grad_out.reshape(depth, chips, HD // chips, width), 0, 1)
    out_full = reduce_parts(out_parts, chips, depth)
    grad_out_out = jnp.swapaxes(out_full, 0, 1).reshape(2 * HD, width)

    proj_rows = proj.shape[0] * width
    proj_parts = grad_proj.astype(bf16).reshape(chips, proj_rows // chips, depth, HD)
    proj_parts = jnp.swapaxes(proj_parts, 1, 2)
    gain_parts = jnp.stack([grad_gain_in, grad_gain_mid]).reshape(2, depth, columns)
    small_parts = jnp.concatenate(
        [
            jnp.swapaxes(gain_parts, 0, 1).reshape(depth, -1),
            grad_beta,
            grad_conv.reshape(3 * TAPS, depth, HD).transpose(1, 0, 2).reshape(depth, -1),
            jnp.broadcast_to(grad_head, (depth, HD)),
        ],
        axis=1,
    )
    small_count = small_parts.shape[1]
    lines = -(-small_count // (HD * 8 * chips)) * 8
    small_parts = jnp.pad(small_parts, ((0, 0), (0, lines * chips * HD - small_count)))
    small_parts = small_parts.astype(bf16).reshape(depth, chips, lines, HD)
    joined = jnp.concatenate([proj_parts, jnp.swapaxes(small_parts, 0, 1)], axis=2)
    proj_full = reduce_parts(joined, chips, depth)
    grad_proj_out = proj_full[:, :, :-lines].transpose(0, 2, 1, 3).reshape(proj.shape[0], width, 2 * HD)
    small_full = jnp.swapaxes(proj_full[:, :, -lines:], 0, 1).reshape(2, -1)
    size = 2 * columns
    grad_gains = (small_full[0, :size] + small_full[1, :size]).reshape(2, columns)
    grad_beta_out = small_full[:, size : size + width].T
    size = size + width
    conv_size = 3 * TAPS * HD
    grad_conv_out = small_full[:, size : size + conv_size].reshape(2, 3, TAPS, HD)
    grad_conv_out = grad_conv_out.transpose(1, 2, 0, 3).reshape(3, TAPS, 2 * HD)
    size = size + conv_size
    grad_head_out = small_full[0, size : size + HD] + small_full[1, size : size + HD]
    return (
        layer_output,
        input_grad,
        grad_gains,
        grad_proj_out,
        grad_beta_out,
        grad_conv_out,
        grad_head_out,
        grad_out_out,
        grad_mlp_out,
        grad_down_out,
    )


def solution(mesh):
    devices = mesh.devices
    chips = devices.shape[0] // 2
    fine = Mesh(devices.reshape(chips, 2, devices.shape[1]), EVERY)
    return jax.shard_map(
        on_device,
        mesh=fine,
        in_specs=(
            P(GROUPS, "tensor"),
            P(GROUPS, "tensor"),
            P(None, "tensor"),
            P(None, None, "tensor"),
            P(None, "tensor"),
            P(None, None, "tensor"),
            P(),
            P("tensor", None),
            P(None, None, "tensor"),
            P("tensor", None),
            P(),
            P(),
        ),
        out_specs=(
            P(GROUPS, "tensor"),
            P(GROUPS, "tensor"),
            P(None, "tensor"),
            P(None, None, "tensor"),
            P(None, "tensor"),
            P(None, None, "tensor"),
            P(),
            P("tensor", None),
            P(None, None, "tensor"),
            P("tensor", None),
        ),
        check_vma=False,
    )
```

```python
import functools

import jax
import jax.numpy as jnp
from jax import lax
from jax.experimental import pallas as pl
from jax.experimental.pallas import tpu as pltpu
from jax.sharding import Mesh, PartitionSpec as P

CH = 128
SUB = 2
STEP = CH * SUB
HALF = 64
HD = 128
TAPS = 4
EPS = 1e-6
f32, bf16 = jnp.float32, jnp.bfloat16


def mm(a, b, ca=1, cb=0):
    return lax.dot_general(
        a.astype(bf16), b.astype(bf16), (((ca,), (cb,)), ((), ())), preferred_element_type=f32
    )


def nt(a, b):
    return mm(a, b, 1, 1)


def grid_ids():
    row = lax.broadcasted_iota(jnp.int32, (CH, CH), 0)
    col = lax.broadcasted_iota(jnp.int32, (CH, CH), 1)
    return row, col


def inverse(systems):
    row, col = grid_ids()
    eye = jnp.where(row == col, 1.0, 0.0)
    pair = (row // 2 == col // 2) & (row > col)
    found = [eye - jnp.where(pair, a, 0.0) for a in systems]
    size = 2
    while size < CH:
        inside = (
            (row // (2 * size) == col // (2 * size))
            & ((row // size) % 2 == 1)
            & ((col // size) % 2 == 0)
        )
        right = [mm(jnp.where(inside, a, 0.0), t) for a, t in zip(systems, found)]
        found = [t - mm(t, r) for t, r in zip(found, right)]
        size *= 2
    return found


def behind(rows, before, opens):
    halves = []
    for n, is_open in enumerate(opens):
        prior = before if n == 0 else rows[n * HALF - 8 : n * HALF]
        halves.append(jnp.concatenate([prior * is_open, rows[n * HALF : (n + 1) * HALF]], axis=0))
    return halves


def ahead(rows, after, opens):
    halves = []
    for n in range(len(opens) - 1):
        next_rows = after if n == len(opens) - 2 else rows[(n + 1) * HALF : (n + 1) * HALF + 8]
        halves.append(
            jnp.concatenate([rows[n * HALF : (n + 1) * HALF], next_rows * opens[n + 1]], axis=0)
        )
    return halves


def shift_down(halves, s):
    return jnp.concatenate([h[8 - s : 8 - s + HALF] for h in halves], axis=0)


def shift_up(halves, s):
    return jnp.concatenate([h[s : s + HALF] for h in halves], axis=0)


def head(x, h):
    return x[:, h * HD : (h + 1) * HD]


def convolve(rows, halves, taps):
    mixed = taps[TAPS - 1 : TAPS] * rows
    for s in range(1, TAPS):
        mixed = mixed + taps[TAPS - 1 - s : TAPS - s] * shift_down(halves, s)
    return mixed


def unit(z):
    return lax.rsqrt(jnp.sum(z * z, axis=1, keepdims=True) + EPS)


def chunk_masks(open1):
    row, col = grid_ids()
    r1 = lax.broadcasted_iota(jnp.int32, (CH, 1), 0)
    sees = jnp.where(r1 < HALF, 1.0, open1)
    lasts = jnp.where(r1 < HALF, open1, 1.0)
    joined = jnp.where((row >= HALF) & (col < HALF), open1, 1.0)
    return row, col, sees, lasts, joined


def forward_kernel(
    starts, proj, before, conv, gain, gated_out, s_out, t_out, e_out, o_out, state, *, heads
):
    i = pl.program_id(0)
    width = heads * HD

    @pl.when(i == 0)
    def _():
        state[...] = jnp.zeros_like(state)

    opens = [1.0 - starts[2 * SUB * i + n].astype(f32) for n in range(2 * SUB)]
    acts = []
    for k in range(3):
        rows = proj[:, k * width : (k + 1) * width]
        mixed = convolve(rows, behind(rows, before[:, k * width : (k + 1) * width], opens), conv[k])
        acts.append(mixed * jax.nn.sigmoid(mixed))
    beta = jax.nn.sigmoid(proj[:, 4 * width : 4 * width + heads])

    pairs = [(c, h) for c in range(SUB) for h in range(heads)]
    masks = [chunk_masks(opens[2 * c + 1]) for c in range(SUB)]
    q, k, v, b, grams, scores = {}, {}, {}, {}, {}, {}
    for h in range(heads):
        qa, ka, va = (head(acts[n], h) for n in range(3))
        qa = qa * (unit(qa) * HD**-0.5)
        ka = ka * unit(ka)
        for c in range(SUB):
            lines = slice(c * CH, (c + 1) * CH)
            q[c, h], k[c, h], v[c, h] = qa[lines], ka[lines], va[lines]
            b[c, h] = beta[lines, h : h + 1]
            row, col, sees, lasts, joined = masks[c]
            both = nt(jnp.concatenate([k[c, h], q[c, h]], axis=0), k[c, h])
            grams[c, h] = jnp.where(row > col, joined, 0.0) * both[:CH]
            scores[c, h] = jnp.where(row >= col, joined, 0.0) * both[CH:]
    solved = dict(zip(pairs, inverse([b[p] * grams[p] for p in pairs])))
    for c, h in pairs:
        row, col, sees, lasts, joined = masks[c]
        p = (c, h)
        begun = state[h] * opens[2 * c]
        seen = mm(jnp.concatenate([sees * k[p], sees * q[p]], axis=0), begun)
        rest = v[p] - seen[:CH]
        delta = mm(solved[p], b[p] * rest)
        err = rest - mm(grams[p], delta)
        delta = b[p] * err
        out = seen[CH:] + mm(scores[p], delta)
        state[h] = opens[2 * c + 1] * begun + mm(jnp.transpose(lasts * k[p]), delta)
        s_out[c, h] = begun.astype(s_out.dtype)
        t_out[c, h] = jnp.transpose(solved[p]).astype(t_out.dtype)
        at = (slice(c * CH, (c + 1) * CH), slice(h * HD, (h + 1) * HD))
        e_out[at] = err.astype(e_out.dtype)
        o_out[at] = out.astype(o_out.dtype)
        rho = lax.rsqrt(jnp.mean(out * out, axis=1, keepdims=True) + EPS)
        gate = proj[at[0], 3 * width + h * HD : 3 * width + (h + 1) * HD]
        gate = gate * jax.nn.sigmoid(gate)
        gated_out[at] = (out * rho * gain[...] * gate).astype(gated_out.dtype)


def backward_kernel(
    starts,
    proj,
    before,
    conv,
    gain,
    s_in,
    t_in,
    e_in,
    o_in,
    gg_in,
    gpre,
    gconv,
    ggain,
    dstate,
    after,
    *,
    heads,
    blocks,
):
    step = pl.program_id(0)
    i = blocks - 1 - step
    width = heads * HD

    @pl.when(step == 0)
    def _():
        dstate[...] = jnp.zeros_like(dstate)
        after[...] = jnp.zeros_like(after)
        gconv[...] = jnp.zeros_like(gconv)
        ggain[...] = jnp.zeros_like(ggain)

    opens = [1.0 - starts[2 * SUB * i + n].astype(f32) for n in range(2 * SUB + 1)]
    mixed, acts, sig, halves = [], [], [], []
    for k in range(3):
        rows = proj[:, k * width : (k + 1) * width]
        halves.append(behind(rows, before[:, k * width : (k + 1) * width], opens[:-1]))
        mixed.append(convolve(rows, halves[k], conv[k]))
        sig.append(jax.nn.sigmoid(mixed[k]))
        acts.append(mixed[k] * sig[k])
    beta = jax.nn.sigmoid(proj[:, 4 * width : 4 * width + heads])
    gain_row = gain[...]

    total_gain = jnp.zeros((1, HD), f32)
    dos, grads, dbetas = {}, {}, {}
    for h in range(heads):
        lanes = slice(h * HD, (h + 1) * HD)
        wide = slice(3 * width + h * HD, 3 * width + (h + 1) * HD)
        out = o_in[:, lanes].astype(f32)
        gg = gg_in[:, lanes].astype(f32)
        rho = lax.rsqrt(jnp.mean(out * out, axis=1, keepdims=True) + EPS)
        unit_out = out * rho
        g = proj[:, wide]
        s = jax.nn.sigmoid(g)
        gpre[:, wide] = (gg * (unit_out * gain_row) * s * (1.0 + g * (1.0 - s))).astype(gpre.dtype)
        dn = gg * (g * s)
        total_gain = total_gain + jnp.sum(dn * unit_out, axis=0, keepdims=True)
        dn = dn * gain_row
        dos[h] = rho * dn - unit_out * (rho * jnp.mean(dn * unit_out, axis=1, keepdims=True))
    ggain[...] += total_gain

    for c in reversed(range(SUB)):
        row, col, sees, lasts, joined = chunk_masks(opens[2 * c + 1])
        joined_t = jnp.where((col >= HALF) & (row < HALF), opens[2 * c + 1], 1.0)
        causal = jnp.where(row >= col, joined, 0.0)
        strict = jnp.where(row > col, joined, 0.0)
        causal_t = jnp.where(col >= row, joined_t, 0.0)
        strict_t = jnp.where(col > row, joined_t, 0.0)
        lines = slice(c * CH, (c + 1) * CH)
        for h in range(heads):
            lanes = slice(h * HD, (h + 1) * HD)
            qa, ka = acts[0][lines, lanes], acts[1][lines, lanes]
            rq, rk = unit(qa), unit(ka)
            q, k = qa * (rq * HD**-0.5), ka * rk
            b = beta[lines, h : h + 1]
            do = dos[h][lines]
            begun = s_in[c, h]
            ds = dstate[h]
            err = e_in[lines, lanes].astype(f32)
            delta = b * err
            scores_t = causal_t * nt(k, q)
            ddelta = mm(scores_t, do) + mm(lasts * k, ds)
            dx = mm(t_in[c, h], ddelta)
            dr = b * dx
            dbetas[c, h] = jnp.sum(dx * err, axis=1, keepdims=True)
            both = jnp.concatenate([do, dr], axis=0)
            pair = nt(both, delta)
            pair_t = nt(delta, both)
            dp = causal * pair[:CH]
            dp_t = causal_t * pair_t[:, :CH]
            w = strict * pair[CH:] + strict_t * pair_t[:, CH:]
            through = nt(both, begun)
            from_k = mm(jnp.concatenate([dp, w], axis=0), k)
            dq = sees * through[:CH] + from_k[:CH]
            dk = lasts * nt(delta, ds) - sees * through[CH:] + mm(dp_t, q) - from_k[CH:]
            turned = jnp.transpose(jnp.concatenate([sees * q, -sees * k], axis=0))
            dstate[h] = opens[2 * c] * (opens[2 * c + 1] * ds + mm(turned, both))
            dq = dq * HD**-0.5
            grads[0, c, h] = rq * dq - qa * (rq * rq * rq * jnp.sum(qa * dq, axis=1, keepdims=True))
            grads[1, c, h] = rk * dk - ka * (rk * rk * rk * jnp.sum(ka * dk, axis=1, keepdims=True))
            grads[2, c, h] = dr
    dbeta = jnp.concatenate(
        [jnp.concatenate([dbetas[c, h] for h in range(heads)], axis=1) for c in range(SUB)], axis=0
    )
    dbeta = dbeta * beta * (1.0 - beta)
    dbeta = jnp.concatenate([dbeta, jnp.zeros((STEP, HD - heads), f32)], axis=1)
    gpre[:, 4 * width :] = dbeta.astype(gpre.dtype)
    for k in range(3):
        dact = jnp.concatenate(
            [jnp.concatenate([grads[k, c, h] for h in range(heads)], axis=1) for c in range(SUB)], axis=0
        )
        dmix = dact * sig[k] * (1.0 + mixed[k] * (1.0 - sig[k]))
        nxt = ahead(dmix, after[k], opens)
        dpre = conv[k, TAPS - 1 : TAPS] * dmix
        gconv[k, TAPS - 1 : TAPS] += jnp.sum(
            dmix * proj[:, k * width : (k + 1) * width], axis=0, keepdims=True
        )
        for s in range(1, TAPS):
            dpre = dpre + conv[k, TAPS - 1 - s : TAPS - s] * shift_up(nxt, s)
            gconv[k, TAPS - 1 - s : TAPS - s] += jnp.sum(
                dmix * shift_down(halves[k], s), axis=0, keepdims=True
            )
        after[k] = dmix[:8]
        gpre[:, k * width : (k + 1) * width] = dpre.astype(gpre.dtype)


def core_work(rows, width):
    return pl.CostEstimate(
        flops=60_000 * rows * width, transcendentals=8 * rows * width, bytes_accessed=200 * rows * width
    )


def mixer_forward(starts, proj, conv, gain):
    rows, full = proj.shape
    width = conv.shape[2]
    heads = width // HD
    blocks = rows // STEP
    chunks = blocks * SUB
    per = STEP // 8
    at = lambda i, s: lax.rem(i + s[2 * chunks + 1] * (blocks // 2), blocks)
    prior = lambda i, s: at(jnp.maximum(i - 1, 0), s) * per + per - 1
    return pl.pallas_call(
        functools.partial(forward_kernel, heads=heads),
        grid_spec=pltpu.PrefetchScalarGridSpec(
            num_scalar_prefetch=1,
            grid=(blocks,),
            in_specs=[
                pl.BlockSpec((STEP, full), lambda i, s: (at(i, s), 0)),
                pl.BlockSpec((8, 3 * width), lambda i, s: (prior(i, s), 0)),
                pl.BlockSpec((3, TAPS, width), lambda i, s: (0, 0, 0)),
                pl.BlockSpec((1, HD), lambda i, s: (0, 0)),
            ],
            out_specs=[
                pl.BlockSpec((STEP, width), lambda i, s: (at(i, s), 0)),
                pl.BlockSpec((SUB, heads, HD, HD), lambda i, s: (i, 0, 0, 0)),
                pl.BlockSpec((SUB, heads, CH, CH), lambda i, s: (i, 0, 0, 0)),
                pl.BlockSpec((STEP, width), lambda i, s: (i, 0)),
                pl.BlockSpec((STEP, width), lambda i, s: (i, 0)),
            ],
            scratch_shapes=[pltpu.VMEM((heads, HD, HD), f32)],
        ),
        out_shape=[
            jax.ShapeDtypeStruct((rows, width), bf16),
            jax.ShapeDtypeStruct((chunks, heads, HD, HD), bf16),
            jax.ShapeDtypeStruct((chunks, heads, CH, CH), bf16),
            jax.ShapeDtypeStruct((rows, width), f32),
            jax.ShapeDtypeStruct((rows, width), f32),
        ],
        compiler_params=pltpu.CompilerParams(vmem_limit_bytes=56 * 1024 * 1024),
        cost_estimate=core_work(rows, width),
    )(starts, proj, proj, conv, gain)


def mixer_backward(starts, proj, conv, gain, saved, grad_gated):
    rows, full = proj.shape
    width = conv.shape[2]
    heads = width // HD
    blocks = rows // STEP
    chunks = blocks * SUB
    per = STEP // 8
    back = lambda i: blocks - 1 - i
    at = lambda i, s: lax.rem(back(i) + s[2 * chunks + 1] * (blocks // 2), blocks)
    prior = lambda i, s: at(jnp.minimum(i + 1, blocks - 1), s) * per + per - 1
    return pl.pallas_call(
        functools.partial(backward_kernel, heads=heads, blocks=blocks),
        grid_spec=pltpu.PrefetchScalarGridSpec(
            num_scalar_prefetch=1,
            grid=(blocks,),
            in_specs=[
                pl.BlockSpec((STEP, full), lambda i, s: (at(i, s), 0)),
                pl.BlockSpec((8, 3 * width), lambda i, s: (prior(i, s), 0)),
                pl.BlockSpec((3, TAPS, width), lambda i, s: (0, 0, 0)),
                pl.BlockSpec((1, HD), lambda i, s: (0, 0)),
                pl.BlockSpec((SUB, heads, HD, HD), lambda i, s: (back(i), 0, 0, 0)),
                pl.BlockSpec((SUB, heads, CH, CH), lambda i, s: (back(i), 0, 0, 0)),
                pl.BlockSpec((STEP, width), lambda i, s: (back(i), 0)),
                pl.BlockSpec((STEP, width), lambda i, s: (back(i), 0)),
                pl.BlockSpec((STEP, width), lambda i, s: (at(i, s), 0)),
            ],
            out_specs=[
                pl.BlockSpec((STEP, full), lambda i, s: (at(i, s), 0)),
                pl.BlockSpec((3, TAPS, width), lambda i, s: (0, 0, 0)),
                pl.BlockSpec((1, HD), lambda i, s: (0, 0)),
            ],
            scratch_shapes=[pltpu.VMEM((heads, HD, HD), f32), pltpu.VMEM((3, 8, width), f32)],
        ),
        out_shape=[
            jax.ShapeDtypeStruct((rows, full), bf16),
            jax.ShapeDtypeStruct((3, TAPS, width), f32),
            jax.ShapeDtypeStruct((1, HD), f32),
        ],
        compiler_params=pltpu.CompilerParams(vmem_limit_bytes=56 * 1024 * 1024),
        cost_estimate=core_work(rows, width),
    )(starts, proj, proj, conv, gain, *saved, grad_gated)


BLOCK = 64
EVERY = ("chip", "core", "tensor")
GROUPS = ("chip", "core")


def per_match(places, starts, lengths, values):
    inside = (places[:, None] >= starts[None, :]) & (places[:, None] < (starts + lengths)[None, :])
    return jnp.sum(jnp.where(inside, values[None, :], 0), axis=1)


def total_before(counts):
    size = counts.shape[-1]
    earlier = jnp.tri(size, k=-1, dtype=jnp.int32)
    return jnp.sum(counts[..., None, :] * earlier, axis=-1)


def gather_kernel(index, source, target):
    def move(j, carried):
        target[j] = source[index[j]]
        return carried

    lax.fori_loop(0, target.shape[0], move, 0, unroll=8)


def reorder(blocks, index):
    count, unit, _ = blocks.shape
    if unit % 8:
        chosen = (index[:, None] == jnp.arange(count, dtype=jnp.int32)[None, :]).astype(blocks.dtype)
        return jnp.einsum("ab,buc->auc", chosen, blocks)
    whole = pl.BlockSpec(blocks.shape, lambda i, s: (0, 0, 0))
    return pl.pallas_call(
        gather_kernel,
        grid_spec=pltpu.PrefetchScalarGridSpec(
            num_scalar_prefetch=1, grid=(1,), in_specs=[whole], out_specs=whole
        ),
        out_shape=jax.ShapeDtypeStruct(blocks.shape, blocks.dtype),
        compiler_params=pltpu.CompilerParams(vmem_limit_bytes=32 * 1024 * 1024),
    )(index, blocks)


def routing(seq_lengths, seq_order, groups, rows, depth):
    count = seq_lengths.shape[0]
    per_group = count // groups
    half = rows // (2 * BLOCK)
    part = half // 2
    total = groups * rows // BLOCK
    lengths = seq_lengths // BLOCK
    given = total_before(lengths)
    chosen = seq_order[:, None] == jnp.arange(count, dtype=jnp.int32)[None, :]
    dealt_len = jnp.sum(jnp.where(chosen, lengths[None, :], 0), axis=1)
    dealt_src = jnp.sum(jnp.where(chosen, given[None, :], 0), axis=1)
    by_group = dealt_len.reshape(groups, per_group)
    is_long = by_group == half
    short = jnp.where(is_long, 0, by_group)
    inner = jnp.where(is_long, 0, half + total_before(short))
    base = jnp.arange(groups, dtype=jnp.int32)[:, None] * (2 * half)
    placed = (base + inner).reshape(-1)
    order = jnp.arange(total, dtype=jnp.int32)
    piece, offset = order // part, order % part
    chip, core, plane = piece // (2 * depth), (piece // depth) % 2, piece % depth
    places = (chip * depth + plane) * half + core * part + offset
    take = places + per_match(places, placed, dealt_len, dealt_src - placed)
    goes = order + per_match(order, dealt_src, dealt_len, placed - dealt_src)
    unit, within = goes // half, goes % half
    back = (((unit // depth) * 2 + within // part) * depth + unit % depth) * part + within % part
    own = lax.axis_index("chip") * depth + lax.axis_index("tensor")
    own_places = own * half + jnp.arange(half, dtype=jnp.int32)
    begins = jnp.any(own_places[:, None] == placed[None, :], axis=1).astype(jnp.int32)
    core = lax.axis_index("core").astype(jnp.int32)
    marks = jnp.concatenate([begins, jnp.ones((1,), jnp.int32), core[None]])
    return take, back, marks


def deal(values, groups):
    rows, columns = values.shape
    blocks, unit = rows // BLOCK, BLOCK // groups
    return jnp.swapaxes(values.reshape(blocks, groups, unit, columns), 0, 1)


def spread(dealt):
    groups, blocks, unit, columns = dealt.shape
    dealt = lax.all_to_all(dealt, GROUPS, 0, 0, tiled=True)
    return dealt.reshape(blocks * groups, unit, columns)


def deliver(picked):
    blocks, unit, columns = picked.shape
    depth = lax.axis_size("tensor")
    groups = lax.axis_size("core") * lax.axis_size("chip")
    part = blocks // (groups * depth)
    routed = lax.all_to_all(picked.reshape(groups * depth, part, unit, columns), EVERY, 0, 0, tiled=True)
    routed = routed.reshape(groups, depth, part, unit, columns).transpose(2, 0, 3, 1, 4)
    return routed.reshape(part * BLOCK, depth * columns)


def collect(values, groups):
    rows, width = values.shape
    depth = lax.axis_size("tensor")
    part, unit, columns = rows // BLOCK, BLOCK // groups, width // depth
    parted = values.reshape(part, groups, unit, depth, columns).transpose(1, 3, 0, 2, 4)
    held = lax.all_to_all(parted.reshape(groups * depth, part, unit, columns), EVERY, 0, 0, tiled=True)
    return held.reshape(groups * depth * part, unit, columns)


def bring_home(held, groups):
    count, unit, columns = held.shape
    blocks = count // groups
    home = lax.all_to_all(held.reshape(groups, blocks, unit, columns), GROUPS, 0, 0, tiled=True)
    return jnp.swapaxes(home, 0, 1).reshape(blocks * BLOCK, columns)


def tie(*values):
    return lax.optimization_barrier(values)


def swap(values):
    return lax.ppermute(values, "core", [(0, 1), (1, 0)])


def dot(a, b):
    return jnp.dot(a, b, preferred_element_type=f32)


def norm_back(values, scale, gain, grad_normed, width):
    weighted = gain * grad_normed
    along = jnp.sum(weighted * values, axis=1, keepdims=True)
    grad_values = scale * weighted - values * (scale * scale * scale) * along / width
    return grad_values, jnp.sum(grad_normed * values * scale, axis=0)


ROOM = pltpu.CompilerParams(vmem_limit_bytes=48 * 1024 * 1024)


def moved(*arrays):
    size = sum(a.size * a.dtype.itemsize for a in arrays)
    return pl.CostEstimate(flops=0, transcendentals=0, bytes_accessed=size)


def shape_of(shape, dtype=bf16):
    return jax.ShapeDtypeStruct(shape, dtype)


def whole(shape):
    return pl.BlockSpec(shape, lambda *i: (0,) * len(shape))


def columns_at(place, size):
    return pl.ds(pl.multiple_of(place * size, 128), size)


def mixer_weights_kernel(source, beta, target):
    depth, _, width = source.shape[1:]
    lines = target.shape[0]
    kinds = (target.shape[1] - width) // (depth * width)
    for z in range(depth):
        for k in range(kinds):
            lane = (k * depth + z) * width
            target[:, lane : lane + width] = source[0, z, k * lines : (k + 1) * lines]
    target[:, kinds * depth * width :] = beta[...]


def mixer_weights(parts, beta, kinds):
    chips, depth, _, width = parts.shape
    rows = beta.shape[0]
    wide = kinds * depth * width + width
    return pl.pallas_call(
        mixer_weights_kernel,
        grid=(chips,),
        in_specs=[
            pl.BlockSpec((1, depth, kinds * rows // chips, width), lambda i: (i, 0, 0, 0)),
            pl.BlockSpec((rows // chips, width), lambda i: (i, 0)),
        ],
        out_specs=pl.BlockSpec((rows // chips, wide), lambda i: (i, 0)),
        out_shape=shape_of((rows, wide)),
        compiler_params=ROOM,
        cost_estimate=moved(parts, parts),
    )(parts, beta)


def ff_weights_kernel(source, target):
    depth = source.shape[1]
    kinds, lines = target.shape[0], target.shape[1] // depth
    for z in range(depth):
        for k in range(kinds):
            target[k, z * lines : (z + 1) * lines] = source[0, z, k * lines : (k + 1) * lines]


def ff_weights(parts, kinds):
    chips, depth, lines, width = parts.shape
    lines = lines // kinds
    if chips != 4:
        apart = parts.reshape(chips, depth, kinds, lines, width)
        return apart.transpose(2, 1, 3, 0, 4).reshape(kinds, depth * lines, chips * width)
    return pl.pallas_call(
        ff_weights_kernel,
        grid=(chips,),
        in_specs=[pl.BlockSpec((1, depth, kinds * lines, width), lambda i: (i, 0, 0, 0))],
        out_specs=pl.BlockSpec((kinds, depth * lines, width), lambda i: (0, 0, i)),
        out_shape=shape_of((kinds, depth * lines, chips * width)),
        compiler_params=ROOM,
        cost_estimate=moved(parts, parts),
    )(parts)


def place_kernel(order, *refs):
    target = refs[-1]
    for k, slot in enumerate(refs[:-1]):
        target[order[k]] = slot[...]


def place(slots, order):
    count, (rows, width) = len(slots), slots[0].shape
    return pl.pallas_call(
        place_kernel,
        grid_spec=pltpu.PrefetchScalarGridSpec(
            num_scalar_prefetch=1,
            grid=(1,),
            in_specs=[whole((rows, width))] * count,
            out_specs=whole((count, rows, width)),
        ),
        out_shape=shape_of((count, rows, width)),
        compiler_params=ROOM,
        cost_estimate=moved(*slots, *slots),
    )(order, *slots)


def place_rows_kernel(order, *refs, depth):
    first, second = refs[-2:]
    one, two = first.shape[0] // depth, second.shape[0] // depth
    for k, slot in enumerate(refs[:-2]):
        columns = columns_at(order[k], slot.shape[1])
        for z in range(depth):
            line = z * (one + two)
            first[z * one : (z + 1) * one, columns] = slot[line : line + one]
            second[z * two : (z + 1) * two, columns] = slot[line + one : line + one + two]


def place_rows(slots, order, depth, size):
    count, (rows, width) = len(slots), slots[0].shape
    outs = [(depth * size, count * width), (rows - depth * size, count * width)]
    return pl.pallas_call(
        functools.partial(place_rows_kernel, depth=depth),
        grid_spec=pltpu.PrefetchScalarGridSpec(
            num_scalar_prefetch=1,
            grid=(1,),
            in_specs=[whole((rows, width))] * count,
            out_specs=[whole(o) for o in outs],
        ),
        out_shape=[shape_of(o) for o in outs],
        compiler_params=ROOM,
        cost_estimate=moved(*slots, *slots),
    )(order, *slots)


def split_ff_kernel(pair, single, target):
    depth = target.shape[1]
    lines = single.shape[0] // depth
    for z in range(depth):
        part = slice(z * lines, (z + 1) * lines)
        target[0, z, :lines] = pair[0, part]
        target[0, z, lines : 2 * lines] = pair[1, part]
        target[0, z, 2 * lines :] = single[part]


def split_ff(pair, single, depth):
    rows, width = single.shape[0], single.shape[1] // 4
    shape = (depth, 3 * rows // depth, width)
    return pl.pallas_call(
        split_ff_kernel,
        grid=(4,),
        in_specs=[
            pl.BlockSpec((2, rows, width), lambda i: (0, 0, i)),
            pl.BlockSpec((rows, width), lambda i: (0, i)),
        ],
        out_specs=pl.BlockSpec((1,) + shape, lambda i: (i, 0, 0, 0)),
        out_shape=shape_of((4,) + shape),
        compiler_params=ROOM,
        cost_estimate=moved(pair, pair, single, single),
    )(pair, single)


def tn(a, b):
    return mm(a, b, 0, 0)


FREE = pl.CostEstimate(flops=0, transcendentals=0, bytes_accessed=0)
WIDE_ROOM = pltpu.CompilerParams(vmem_limit_bytes=56 * 1024 * 1024)


def mixer_grads_kernel(
    near, normed, grad_pre, grad_mix, gated, proj, gains, gain_mid, conv, grad_head, *targets, kinds
):
    step = pl.program_id(0)
    chip = near[step]
    depth, _, width = targets[0].shape
    lines = normed.shape[1]
    wide = depth * width
    total = jnp.zeros((lines, 1), f32)
    parts = []
    for n in range(kinds + 1):
        lanes = slice(n * wide, n * wide + (wide if n < kinds else width))
        part = tn(normed[...], grad_pre[:, lanes])
        total = total + jnp.sum(part * proj[:, lanes].astype(f32), axis=1, keepdims=True)
        parts.append(part)
    out = tn(grad_mix[...], gated[...])
    lane = lax.broadcasted_iota(jnp.int32, (lines, width), 1)
    turned = jnp.transpose(jnp.where(lane == depth, total, parts[kinds]))
    gain_in = turned[depth : depth + 1] / gains[0:1]
    blank = jnp.zeros((1, width), f32)

    def in_lines(row, keep):
        row = row * keep
        return [row[:, n * width : (n + 1) * width] for n in range(lines // width)]

    for k, target in enumerate(targets):

        @pl.when(step == k)
        def _():
            for z in range(depth):
                lanes = slice(z * width, (z + 1) * width)
                for n in range(kinds):
                    target[z, n * lines : (n + 1) * lines] = parts[n][:, lanes].astype(bf16)
                target[z, kinds * lines : (kinds + 1) * lines] = out[:, lanes].astype(bf16)
                here = jnp.where(chip == z, 1.0, 0.0)
                small = in_lines(turned[z : z + 1], 1.0) + in_lines(gain_in, here) + in_lines(gain_mid[0:1], here)
                small.append(conv[chip, :, lanes])
                small.append(grad_head[...] * jnp.where(chip == 0, 1.0, 0.0))
                count = 3 * (lines // width) + conv.shape[1] + 1
                small += [blank] * (16 - count)
                target[z, (kinds + 1) * lines :] = jnp.concatenate(small, axis=0).astype(bf16)


def mixer_grads(normed, grad_pre, grad_mix, gated, proj, gains, gain_mid, conv, grad_head, near, depth, kinds):
    rows, width = normed.shape
    lines = width // 4
    shape = (depth, (kinds + 1) * lines + 16, HD)
    column = lambda a: pl.BlockSpec((a.shape[0], lines), lambda i, s: (0, s[i]))
    conv = conv.reshape(4, -1, depth * HD)
    return pl.pallas_call(
        functools.partial(mixer_grads_kernel, kinds=kinds),
        grid_spec=pltpu.PrefetchScalarGridSpec(
            num_scalar_prefetch=1,
            grid=(4,),
            in_specs=[
                column(normed),
                whole(grad_pre.shape),
                column(grad_mix),
                whole(gated.shape),
                pl.BlockSpec((lines, proj.shape[1]), lambda i, s: (s[i], 0)),
                column(gains),
                column(gain_mid),
                whole(conv.shape),
                whole(grad_head.shape),
            ],
            out_specs=[whole(shape)] * 4,
        ),
        out_shape=[shape_of(shape)] * 4,
        compiler_params=WIDE_ROOM,
        cost_estimate=pl.CostEstimate(flops=40_000_000_000, transcendentals=0, bytes_accessed=100_000_000),
    )(near, normed, grad_pre, grad_mix, gated, proj, gains, gain_mid, conv, grad_head)


def send_back_kernel(grad_pre, proj, target):
    target[...] = nt(grad_pre[...], proj[...]).astype(target.dtype)


def send_back(grad_pre, proj):
    rows, wide = grad_pre.shape
    width = proj.shape[0]
    block, steps = 256, rows // 512
    return pl.pallas_call(
        send_back_kernel,
        grid=(steps,),
        in_specs=[pl.BlockSpec((block, wide), lambda i: (steps + i, 0)), whole(proj.shape)],
        out_specs=pl.BlockSpec((block, width), lambda i: (i, 0)),
        out_shape=shape_of((rows // 2, width)),
        compiler_params=WIDE_ROOM,
        cost_estimate=FREE,
    )(grad_pre, proj)


def keep_back_kernel(grad_pre, proj, came, values, gain, grad_middle, target):
    grad_normed = nt(grad_pre[...], proj[...]) + came[...].astype(f32)
    rows = values[...].astype(f32)
    scale = lax.rsqrt(jnp.mean(rows * rows, axis=1, keepdims=True) + EPS)
    weighted = gain[...] * grad_normed
    along = jnp.mean(weighted * rows, axis=1, keepdims=True)
    grad = scale * weighted - rows * (scale * scale * scale * along)
    target[...] = (grad_middle[...] + grad).astype(target.dtype)


def keep_back(grad_pre, proj, came, values, gain, grad_middle):
    rows, wide = grad_pre.shape
    width = proj.shape[0]
    block = 256
    line = lambda w: pl.BlockSpec((block, w), lambda i: (i, 0))
    return pl.pallas_call(
        keep_back_kernel,
        grid=(rows // 512,),
        in_specs=[
            line(wide),
            whole(proj.shape),
            line(width),
            line(width),
            whole(gain.shape),
            line(width),
        ],
        out_specs=line(width),
        out_shape=shape_of((rows // 2, width)),
        compiler_params=WIDE_ROOM,
        cost_estimate=FREE,
    )(grad_pre, proj, came, values, gain, grad_middle)


def add_kernel(ahead, *refs):
    for j, target in enumerate(refs[-4:]):
        total = refs[0][ahead[j]].astype(f32)
        for source in refs[1:-4]:
            total = total + source[ahead[j]].astype(f32)
        target[...] = total.astype(bf16)


def add_parts(parts, ahead):
    depth, rows, width = parts[0].shape
    steps = 2
    block = rows // steps
    return pl.pallas_call(
        add_kernel,
        grid_spec=pltpu.PrefetchScalarGridSpec(
            num_scalar_prefetch=1,
            grid=(steps,),
            in_specs=[pl.BlockSpec((depth, block, width), lambda i, s: (0, i, 0))] * len(parts),
            out_specs=[pl.BlockSpec((block, width), lambda i, s: (i, 0))] * 4,
        ),
        out_shape=[shape_of((rows, width))] * 4,
        compiler_params=ROOM,
        cost_estimate=moved(*parts, parts[0]),
    )(ahead, *parts)


def join_ff_kernel(where, own, other, pair, single):
    lines = single.shape[0] // 2
    for side, slot in enumerate((own, other)):
        core = where[4] if side == 0 else 1 - where[4]
        rows = pl.ds(pl.multiple_of(core * lines, 8), lines)
        pair[0, rows] = slot[0, :lines].astype(f32)
        pair[1, rows] = slot[0, lines : 2 * lines].astype(f32)
        single[rows] = slot[0, 2 * lines :].astype(f32)


def join_ff(own, other, where):
    _, lines, width = own.shape
    rows = 2 * lines // 3
    piece = pl.BlockSpec((1, lines, width), lambda i, s: (i, 0, 0))
    return pl.pallas_call(
        join_ff_kernel,
        grid_spec=pltpu.PrefetchScalarGridSpec(
            num_scalar_prefetch=1,
            grid=(4,),
            in_specs=[piece, piece],
            out_specs=[
                pl.BlockSpec((2, rows, width), lambda i, s: (0, 0, i)),
                pl.BlockSpec((rows, width), lambda i, s: (0, i)),
            ],
        ),
        out_shape=[shape_of((2, rows, 4 * width), f32), shape_of((rows, 4 * width), f32)],
        compiler_params=ROOM,
        cost_estimate=moved(*[own] * 6),
    )(where, own, other)


def join_mixer_kernel(where, *refs):
    proj, out, small = refs[-3:]
    kinds = proj.shape[0]
    lines, width = proj.shape[1] // 4, proj.shape[2] // 2
    for k in range(4):
        mine, theirs = refs[k][...].astype(f32), refs[4 + k][...].astype(f32)
        first = jnp.where(where[4] == 0, mine, theirs)
        second = jnp.where(where[4] == 0, theirs, mine)
        rows = pl.ds(pl.multiple_of(where[k] * lines, 128), lines)
        for n in range(kinds):
            proj[n, rows, :width] = first[n * lines : (n + 1) * lines]
            proj[n, rows, width:] = second[n * lines : (n + 1) * lines]
        line = kinds * lines
        out[:width, columns_at(where[k], lines)] = jnp.transpose(first[line : line + lines])
        out[width:, columns_at(where[k], lines)] = jnp.transpose(second[line : line + lines])
        small[0, where[k]] = first[line + lines :]
        small[1, where[k]] = second[line + lines :]


def join_mixer(own, other, where, kinds, lines):
    rows, width = own[0].shape
    rest = rows - (kinds + 1) * lines
    outs = [(kinds, 4 * lines, 2 * width), (2 * width, 4 * lines), (2, 4, rest, width)]
    return pl.pallas_call(
        join_mixer_kernel,
        grid_spec=pltpu.PrefetchScalarGridSpec(
            num_scalar_prefetch=1,
            grid=(1,),
            in_specs=[whole((rows, width))] * 8,
            out_specs=[whole(o) for o in outs],
        ),
        out_shape=[shape_of(o, f32) for o in outs],
        compiler_params=ROOM,
        cost_estimate=moved(*[*own] * 6),
    )(where, *own, *other)


def ff_kernel(rows, cot, pair, down, hidden, grads):
    size = down.shape[0]
    for start in range(0, size, 512):
        part = slice(start, min(start + 512, size))
        gate = nt(rows[...], pair[0, part])
        up = nt(rows[...], pair[1, part])
        back = nt(cot[...], down[part])
        sig = jax.nn.sigmoid(gate)
        act = gate * sig
        hidden[:, part] = (act * up).astype(hidden.dtype)
        grads[0, :, part] = (back * up * (sig * (1.0 + gate * (1.0 - sig)))).astype(grads.dtype)
        grads[1, :, part] = (back * act).astype(grads.dtype)


def feed_forward(rows, cot, pair, down):
    count, width = rows.shape
    size = down.shape[0]
    block = 256
    line = lambda w: pl.BlockSpec((block, w), lambda i: (i, 0))
    return pl.pallas_call(
        ff_kernel,
        grid=(count // block,),
        in_specs=[line(width), line(width), whole(pair.shape), whole(down.shape)],
        out_specs=[line(size), pl.BlockSpec((2, block, size), lambda i: (0, i, 0))],
        out_shape=[shape_of((count, size)), shape_of((2, count, size))],
        compiler_params=pltpu.CompilerParams(vmem_limit_bytes=56 * 1024 * 1024),
        cost_estimate=pl.CostEstimate(
            flops=6 * count * width * size, transcendentals=count * size, bytes_accessed=40_000_000
        ),
    )(rows, cot, pair, down)


def to_near(slots):
    return [slots[0]] + [
        lax.ppermute(slots[k], "chip", [(i, i ^ k) for i in range(4)]) for k in range(1, len(slots))
    ]


def to_ahead(slots):
    count = len(slots)
    return [slots[0]] + [
        lax.ppermute(slots[j], "tensor", [(i, (i + j) % count) for i in range(count)])
        for j in range(1, count)
    ]


def total_of(sums):
    return sum(s.astype(f32) for s in sums).astype(bf16)


def sum_scattered(parts, chips, depth):
    flat = parts.reshape(-1, parts.shape[-1])
    summed = lax.psum_scatter(flat, "chip", scatter_dimension=0, tiled=True)
    return lax.psum_scatter(summed, "tensor", scatter_dimension=0, tiled=True)


def reduce_parts(parts, chips, depth):
    _, _, rows, columns = parts.shape
    full = lax.all_gather(sum_scattered(parts, chips, depth), GROUPS, axis=0)
    return full.reshape(chips, 2, rows, columns).astype(f32)


def cut(array, chips, axis):
    size = array.shape[axis] // chips
    return lax.dynamic_slice_in_dim(array, lax.axis_index("chip") * size, size, axis)


def on_device(
    layer_input,
    out_cotangent,
    norm_gains,
    proj_weight,
    beta_weight,
    conv_weight,
    head_gain,
    out_weight,
    mlp_weight,
    down_weight,
    seq_lengths,
    seq_order,
):
    rows, columns = layer_input.shape
    depth = lax.axis_size("tensor")
    chips = lax.axis_size("chip")
    groups = 2 * chips
    width = columns * depth
    own_rows = rows // 4
    core = lax.axis_index("core")

    def mine(array, axis):
        size = array.shape[axis] // 2
        return jnp.where(
            core == 0,
            lax.slice_in_dim(array, 0, size, axis=axis),
            lax.slice_in_dim(array, size, 2 * size, axis=axis),
        )

    chip, plane = lax.axis_index("chip"), lax.axis_index("tensor")
    few = chips == 4
    planes_behind = lax.rem(plane + depth - jnp.arange(depth, dtype=jnp.int32), depth)
    planes_ahead = lax.rem(plane + jnp.arange(depth, dtype=jnp.int32), depth)
    near = chip ^ jnp.arange(4, dtype=jnp.int32)
    where = jnp.concatenate([near, core[None]])
    everywhere = ("chip", "tensor")
    kinds = proj_weight.shape[0]
    heads_wide = depth * HD
    lines = width // chips
    hidden_half = down_weight.shape[0] // 2

    take, back, marks = routing(seq_lengths, seq_order, groups, rows, depth)
    layer_input, proj_weight = tie(deal(layer_input, groups), proj_weight)
    dealt_in = spread(layer_input)
    mixer_half = [cut(mine(proj_weight, 2), chips, 1).reshape(-1, HD)]
    small_wide = jnp.concatenate([norm_gains.reshape(-1), mine(conv_weight, 2).reshape(-1)])
    high = lax.reduce_precision(small_wide, 8, 7)
    middle_term = lax.reduce_precision(small_wide - high, 8, 7)
    low_term = small_wide - high - middle_term
    small = [mine(beta_weight, 1).reshape(-1)] + [t.astype(bf16) for t in (high, middle_term, low_term)]
    small = jnp.concatenate(small).reshape(-1, HD)
    small_rows = small.shape[0]
    small_piece = -(-small_rows // (16 * chips)) * 16
    small = jnp.pad(small, ((0, small_piece * chips - small_rows), (0, 0)))
    mixer_half = jnp.concatenate(mixer_half + [cut(small, chips, 0)], axis=0)
    mixer_parts = lax.all_gather(mixer_half, everywhere, axis=0).reshape(chips, depth, -1, HD)
    small = jnp.swapaxes(mixer_parts[:, :, -small_piece:], 0, 1).reshape(depth, -1)
    wide_size = small_wide.shape[0]
    beta_proj = jnp.pad(small[:, :width].T, ((0, 0), (0, HD - depth)))
    high, middle_term, low_term = (
        small[:, width + n * wide_size : width + (n + 1) * wide_size].astype(f32) for n in range(3)
    )
    small_wide = high + (middle_term + low_term)
    gains = small_wide[:, : 2 * columns].reshape(depth, 2, columns)
    gains = jnp.swapaxes(gains, 0, 1).reshape(2, width)
    conv = small_wide[:, 2 * columns :].reshape(depth, 3, TAPS, HD)
    conv = conv.transpose(1, 2, 0, 3).reshape(3, TAPS, heads_wide)
    proj = mixer_weights(mixer_parts, beta_proj, kinds)
    down_half = cut(jnp.concatenate([mine(down_weight, 0), mine(out_weight, 0)], axis=0), chips, 1)
    down_slots = to_ahead([down_half] * depth) if few else [down_half]
    dealt_in, down_slots = tie(dealt_in, down_slots)
    rows_own = deliver(reorder(dealt_in, take))
    rows_own, out_cotangent = tie(rows_own, out_cotangent)
    dealt_cot = spread(deal(out_cotangent, groups))
    pair_half = cut(mine(jnp.swapaxes(mlp_weight, 1, 2), 1), chips, 2)
    pair_parts = lax.all_gather(pair_half.reshape(2 * hidden_half, -1), everywhere, axis=0)

    low = jnp.concatenate([rows_own, swap(rows_own)], axis=0)
    all_rows = low.astype(f32)
    scale_all = lax.rsqrt(jnp.mean(jnp.square(all_rows), axis=1, keepdims=True) + EPS)
    normed = (all_rows * scale_all * gains[0]).astype(bf16)
    projected = dot(normed, proj)
    gain_row = head_gain[None, :]

    projected, dealt_cot = tie(projected, dealt_cot)
    picked_cot = reorder(dealt_cot, take)
    down_plane = place(down_slots, planes_behind) if few else down_slots[0]
    projected, picked_cot, down_plane = tie(projected, picked_cot, down_plane)
    cot_own = deliver(picked_cot)
    if few:
        down_slots = to_near([down_plane.reshape(depth * (hidden_half + HD), -1)] * 4)
    else:
        down_slots = lax.all_gather(down_plane, everywhere, axis=0)
    gated, *saved = mixer_forward(marks, projected, conv, gain_row)
    gated, down_slots = tie(gated, down_slots)
    if few:
        down, out_proj = place_rows(down_slots, near, depth, hidden_half)
    else:
        down = down_slots.reshape(chips, depth, hidden_half + HD, -1).transpose(1, 2, 0, 3)
        down = down.reshape(depth, hidden_half + HD, width)
        out_proj = down[:, hidden_half:].reshape(heads_wide, width)
        down = down[:, :hidden_half].reshape(depth * hidden_half, width)

    rows_f = rows_own.astype(f32)
    scale_in = scale_all[:own_rows]
    out_of = lambda part: dot(part, out_proj)
    mixed = swap(out_of(gated[own_rows:]).astype(bf16))
    middle = rows_f + out_of(gated[:own_rows]) + mixed.astype(f32)
    scale_mid = lax.rsqrt(jnp.mean(jnp.square(middle), axis=1, keepdims=True) + EPS)
    normed_mid_own = (middle * scale_mid * gains[1]).astype(bf16)
    normed_mid_own, cot_own = tie(normed_mid_own, cot_own)
    cot = jnp.concatenate([cot_own, swap(cot_own)], axis=0)
    normed_mid = jnp.concatenate([normed_mid_own, swap(normed_mid_own)], axis=0)

    pair = ff_weights(pair_parts.reshape(chips, depth, 2 * hidden_half, -1), 2)
    hidden, grad_gate_up = feed_forward(normed_mid, cot, pair, down)

    grad_pair = jnp.einsum("ktf,td->kfd", grad_gate_up, normed_mid, preferred_element_type=f32).astype(bf16)
    grad_down = jnp.einsum("tf,td->fd", hidden, cot, preferred_element_type=f32).astype(bf16)
    if few:
        ff_terms = split_ff(grad_pair, grad_down, depth)
        grad_gate_up, hidden, ff_terms = tie(grad_gate_up, hidden, ff_terms)
        ff_chip = lax.psum_scatter(ff_terms.reshape(-1, lines), "chip", scatter_dimension=0, tiled=True)

    lower = swap(dot(hidden[own_rows:], down).astype(bf16))
    total = middle + dot(hidden[:own_rows], down) + lower.astype(f32)
    total_low, grad_gate_up = tie(total.astype(bf16), grad_gate_up)
    held_out = collect(total_low, groups)
    from_mlp = lambda part: jnp.einsum("ktf,kfd->td", part, pair, preferred_element_type=f32)
    came = swap(from_mlp(grad_gate_up[:, own_rows:]).astype(bf16))
    grad_normed_mid = from_mlp(grad_gate_up[:, :own_rows]) + came.astype(f32)
    mid_back, grad_gain_mid = norm_back(middle, scale_mid, gains[1], grad_normed_mid, width)
    grad_middle = cot_own.astype(f32) + mid_back
    grad_mix_own = grad_middle.astype(bf16)
    (grad_mix,) = tie(jnp.concatenate([grad_mix_own, swap(grad_mix_own)], axis=0))
    grad_gated = jnp.einsum("td,ed->te", grad_mix, out_proj, preferred_element_type=f32)
    grad_pre, grad_conv, grad_head = mixer_backward(marks, projected, conv, gain_row, saved, grad_gated)
    if few:
        grad_pre, held_out, ff_chip = tie(grad_pre, held_out, ff_chip)
        ff_own = lax.psum_scatter(ff_chip, "tensor", scatter_dimension=0, tiled=True)

    came = swap(send_back(grad_pre, proj))
    grad_input = keep_back(grad_pre, proj, came, rows_own, gains[0:1], grad_middle)
    grad_input, grad_pre, grad_mix = tie(grad_input, grad_pre, grad_mix)
    held_grad = collect(grad_input, groups)

    if few:
        mixer_terms = mixer_grads(
            normed,
            grad_pre,
            grad_mix,
            gated,
            proj,
            gains,
            grad_gain_mid[None],
            grad_conv,
            grad_head,
            near,
            depth,
            kinds,
        )
        _, ff_own = tie(mixer_terms[0], ff_own)
        mixer_terms, ff_own = tie(to_near(mixer_terms), lax.all_gather(ff_own, "chip", axis=0))
        sums, ff_other = tie(to_ahead(add_parts(mixer_terms, planes_ahead)), swap(ff_own))
        mixer_own = to_near([total_of(sums)] * 4)
        mixer_sums = mixer_own, [swap(s) for s in mixer_own]
        grad_pair_out, grad_down_out = join_ff(ff_own, ff_other, where)
    held_grad, held_out = tie(held_grad, held_out)
    both = jnp.concatenate([reorder(held_out, back), reorder(held_grad, back)], axis=2)
    both = bring_home(both, groups)
    layer_output, input_grad = both[:, :columns], both[:, columns:]
    if few:
        grad_proj_out, grad_out_out, small_sums = join_mixer(*mixer_sums, where, kinds, lines)
        across = lines // HD
        beta_sums = small_sums[:, :, :across].reshape(2, width)
        gain_sums = jnp.sum(small_sums[:, :, across : 3 * across], axis=1).reshape(2, 2, columns)
        conv_lines = 3 * TAPS // 4
        conv_sums = small_sums[:, :, 3 * across : 3 * across + conv_lines].reshape(2, 3, TAPS, HD)
        head_sums = small_sums[:, 0, 3 * across + conv_lines]
    else:
        every = jnp.concatenate([grad_pair, grad_down[None]], axis=0)
        every = every.reshape(3, depth, hidden_half, chips, lines).transpose(3, 1, 0, 2, 4)
        sums = reduce_parts(every.reshape(chips, depth, 3 * hidden_half, lines), chips, depth)
        sums = sums.reshape(chips, 2, 3, hidden_half, lines).transpose(2, 1, 3, 0, 4)
        sums = sums.reshape(3, 2 * hidden_half, width)
        grad_pair_out, grad_down_out = sums[:2], sums[2]
        grad_out = jnp.einsum("td,te->de", grad_mix, gated, preferred_element_type=f32).astype(bf16)
        grad_proj = jnp.einsum("td,te->de", normed, grad_pre, preferred_element_type=f32)
        grad_gain_in = jnp.sum(grad_proj * proj.astype(f32), axis=1) / gains[0]
        gain_parts = jnp.stack([grad_gain_in, grad_gain_mid]).reshape(2, depth, columns)
        small_terms = jnp.concatenate(
            [
                jnp.swapaxes(gain_parts, 0, 1).reshape(depth, -1),
                grad_proj[:, kinds * heads_wide : kinds * heads_wide + depth].T,
                grad_conv.reshape(3 * TAPS, depth, HD).transpose(1, 0, 2).reshape(depth, -1),
                jnp.broadcast_to(grad_head, (depth, HD)),
            ],
            axis=1,
        )
        small_count = small_terms.shape[1]
        small_lines = chips * -(-small_count // (chips * HD))
        small_terms = jnp.pad(small_terms, ((0, 0), (0, small_lines * HD - small_count)))
        small_terms = jnp.swapaxes(small_terms.reshape(depth, small_lines, HD), 0, 1).astype(bf16)
        grad_proj = grad_proj.astype(bf16)
        every = [
            grad_proj[:, : kinds * heads_wide].reshape(chips, lines, kinds, depth, HD).transpose(0, 3, 2, 1, 4),
            grad_out.reshape(chips, lines, 1, depth, HD).transpose(0, 3, 2, 1, 4),
            small_terms.reshape(chips, -1, 1, depth, HD).transpose(0, 3, 2, 1, 4),
        ]
        every = jnp.concatenate([e.reshape(chips, depth, -1, HD) for e in every], axis=2)
        sums = reduce_parts(every, chips, depth)
        many = sums[:, :, : (kinds + 1) * lines].reshape(chips, 2, kinds + 1, lines, HD)
        many = many.transpose(2, 0, 3, 1, 4).reshape(kinds + 1, width, 2 * HD)
        grad_proj_out, grad_out_out = many[:kinds], many[kinds].T
        small_sums = jnp.swapaxes(sums[:, :, (kinds + 1) * lines :], 0, 1).reshape(2, -1)
        gains_at, beta_at, conv_at = 2 * columns, 2 * columns + width, 2 * columns + width + 3 * TAPS * HD
        gain_sums = small_sums[:, :gains_at].reshape(2, 2, columns)
        beta_sums = small_sums[:, gains_at:beta_at]
        conv_sums = small_sums[:, beta_at:conv_at].reshape(2, 3, TAPS, HD)
        head_sums = small_sums[:, conv_at : conv_at + HD]
    grad_mlp_out = jnp.swapaxes(grad_pair_out, 1, 2)

    grad_gains = gain_sums[0] + gain_sums[1]
    grad_beta_out = beta_sums.T
    grad_conv_out = conv_sums.transpose(1, 2, 0, 3).reshape(3, TAPS, 2 * HD)
    grad_head_out = head_sums[0] + head_sums[1]
    return (
        layer_output,
        input_grad,
        grad_gains,
        grad_proj_out,
        grad_beta_out,
        grad_conv_out,
        grad_head_out,
        grad_out_out,
        grad_mlp_out,
        grad_down_out,
    )


def solution(mesh):
    devices = mesh.devices
    chips = devices.shape[0] // 2
    fine = Mesh(devices.reshape(chips, 2, devices.shape[1]), EVERY)
    return jax.shard_map(
        on_device,
        mesh=fine,
        in_specs=(
            P(GROUPS, "tensor"),
            P(GROUPS, "tensor"),
            P(None, "tensor"),
            P(None, None, "tensor"),
            P(None, "tensor"),
            P(None, None, "tensor"),
            P(),
            P("tensor", None),
            P(None, None, "tensor"),
            P("tensor", None),
            P(),
            P(),
        ),
        out_specs=(
            P(GROUPS, "tensor"),
            P(GROUPS, "tensor"),
            P(None, "tensor"),
            P(None, None, "tensor"),
            P(None, "tensor"),
            P(None, None, "tensor"),
            P(),
            P("tensor", None),
            P(None, None, "tensor"),
            P("tensor", None),
        ),
        check_vma=False,
    )
```

```python
import functools

import jax
import jax.numpy as jnp
from jax import lax
from jax.experimental import pallas as pl
from jax.experimental.pallas import tpu as pltpu
from jax.sharding import Mesh, PartitionSpec as P

CH = 128
SUB = 4
STEP = CH * SUB
HALF = 64
HD = 128
TAPS = 4
EPS = 1e-6
f32, bf16 = jnp.float32, jnp.bfloat16


def mm(a, b, ca=1, cb=0):
    return lax.dot_general(
        a.astype(bf16), b.astype(bf16), (((ca,), (cb,)), ((), ())), preferred_element_type=f32
    )


def nt(a, b):
    return mm(a, b, 1, 1)


def grid_ids():
    row = lax.broadcasted_iota(jnp.int32, (CH, CH), 0)
    col = lax.broadcasted_iota(jnp.int32, (CH, CH), 1)
    return row, col


def inverse(systems):
    row, col = grid_ids()
    eye = jnp.where(row == col, 1.0, 0.0)
    pair = (row // 2 == col // 2) & (row > col)
    found = [eye - jnp.where(pair, a, 0.0) for a in systems]
    size = 2
    while size < CH:
        inside = (
            (row // (2 * size) == col // (2 * size))
            & ((row // size) % 2 == 1)
            & ((col // size) % 2 == 0)
        )
        right = [mm(jnp.where(inside, a, 0.0), t) for a, t in zip(systems, found)]
        found = [t - mm(t, r) for t, r in zip(found, right)]
        size *= 2
    return found


def run(*parts):
    parts = list(parts)
    while parts:
        parts = [part for part in parts if next(part, parts) is not parts]


def in_order(*parts):
    for part in parts:
        yield from part


def behind(rows, before, opens):
    halves = []
    for n, is_open in enumerate(opens):
        prior = before if n == 0 else rows[n * HALF - 8 : n * HALF]
        halves.append(jnp.concatenate([prior * is_open, rows[n * HALF : (n + 1) * HALF]], axis=0))
    return halves


def ahead(rows, after, opens):
    halves = []
    for n in range(len(opens) - 1):
        next_rows = after if n == len(opens) - 2 else rows[(n + 1) * HALF : (n + 1) * HALF + 8]
        halves.append(
            jnp.concatenate([rows[n * HALF : (n + 1) * HALF], next_rows * opens[n + 1]], axis=0)
        )
    return halves


def shift_down(halves, s):
    return jnp.concatenate([h[8 - s : 8 - s + HALF] for h in halves], axis=0)


def shift_up(halves, s):
    return jnp.concatenate([h[s : s + HALF] for h in halves], axis=0)


def head(x, h):
    return x[:, h * HD : (h + 1) * HD]


def convolve(rows, halves, taps):
    mixed = taps[TAPS - 1 : TAPS] * rows
    for s in range(1, TAPS):
        mixed = mixed + taps[TAPS - 1 - s : TAPS - s] * shift_down(halves, s)
    return mixed


def unit(z):
    return lax.rsqrt(jnp.sum(z * z, axis=1, keepdims=True) + EPS)


def chunk_masks(open1):
    row, col = grid_ids()
    r1 = lax.broadcasted_iota(jnp.int32, (CH, 1), 0)
    sees = jnp.where(r1 < HALF, 1.0, open1)
    lasts = jnp.where(r1 < HALF, open1, 1.0)
    joined = jnp.where((row >= HALF) & (col < HALF), open1, 1.0)
    return row, col, sees, lasts, joined


def forward_kernel(
    starts, proj, before, conv, gain, gated_out, s_out, t_out, e_out, o_out, state, *, heads
):
    i = pl.program_id(0)
    width = heads * HD

    @pl.when(i == 0)
    def _():
        state[...] = jnp.zeros_like(state)

    opens = [1.0 - starts[2 * SUB * i + n].astype(f32) for n in range(2 * SUB)]
    acts = []
    for k in range(3):
        rows = proj[:, k * width : (k + 1) * width]
        mixed = convolve(rows, behind(rows, before[:, k * width : (k + 1) * width], opens), conv[k])
        acts.append(mixed * jax.nn.sigmoid(mixed))
    beta = jax.nn.sigmoid(proj[:, 4 * width : 4 * width + heads])

    pairs = [(c, h) for c in range(SUB) for h in range(heads)]
    masks = [chunk_masks(opens[2 * c + 1]) for c in range(SUB)]
    q, k, v, b, grams, scores = {}, {}, {}, {}, {}, {}
    for h in range(heads):
        qa, ka, va = (head(acts[n], h) for n in range(3))
        qa = qa * (unit(qa) * HD**-0.5)
        ka = ka * unit(ka)
        for c in range(SUB):
            lines = slice(c * CH, (c + 1) * CH)
            q[c, h], k[c, h], v[c, h] = qa[lines], ka[lines], va[lines]
            b[c, h] = beta[lines, h : h + 1]
            row, col, sees, lasts, joined = masks[c]
            both = nt(jnp.concatenate([k[c, h], q[c, h]], axis=0), k[c, h])
            grams[c, h] = jnp.where(row > col, joined, 0.0) * both[:CH]
            scores[c, h] = jnp.where(row >= col, joined, 0.0) * both[CH:]
    solved = dict(zip(pairs, inverse([b[p] * grams[p] for p in pairs])))
    every = range(heads)
    carried = [state[h] for h in every]
    for c in range(SUB):
        row, col, sees, lasts, joined = masks[c]
        begun = [carried[h] * opens[2 * c] for h in every]
        seen = [mm(jnp.concatenate([sees * k[c, h], sees * q[c, h]], axis=0), begun[h]) for h in every]
        rest = [v[c, h] - seen[h][:CH] for h in every]
        delta = [mm(solved[c, h], b[c, h] * rest[h]) for h in every]
        err = [rest[h] - mm(grams[c, h], delta[h]) for h in every]
        delta = [b[c, h] * err[h] for h in every]
        added = [mm(jnp.transpose(lasts * k[c, h]), delta[h]) for h in every]
        carried = [opens[2 * c + 1] * begun[h] + added[h] for h in every]
        outs = [seen[h][CH:] + mm(scores[c, h], delta[h]) for h in every]
        lines = slice(c * CH, (c + 1) * CH)
        for h in every:
            out = outs[h]
            s_out[c, h] = begun[h].astype(s_out.dtype)
            t_out[c, h] = jnp.transpose(solved[c, h]).astype(t_out.dtype)
            at = (lines, slice(h * HD, (h + 1) * HD))
            e_out[at] = err[h].astype(e_out.dtype)
            o_out[at] = out.astype(o_out.dtype)
            rho = lax.rsqrt(jnp.mean(out * out, axis=1, keepdims=True) + EPS)
            gate = proj[lines, 3 * width + h * HD : 3 * width + (h + 1) * HD]
            gate = gate * jax.nn.sigmoid(gate)
            gated_out[at] = (out * rho * gain[...] * gate).astype(gated_out.dtype)
    for h in every:
        state[h] = carried[h]


def backward_kernel(
    starts,
    proj,
    before,
    conv,
    gain,
    s_in,
    t_in,
    e_in,
    o_in,
    gg_in,
    gpre,
    gconv,
    ggain,
    dstate,
    after,
    *,
    heads,
    blocks,
):
    step = pl.program_id(0)
    i = blocks - 1 - step
    width = heads * HD

    @pl.when(step == 0)
    def _():
        dstate[...] = jnp.zeros_like(dstate)
        after[...] = jnp.zeros_like(after)
        gconv[...] = jnp.zeros_like(gconv)
        ggain[...] = jnp.zeros_like(ggain)

    opens = [1.0 - starts[2 * SUB * i + n].astype(f32) for n in range(2 * SUB + 1)]
    mixed, acts, sig, halves = [], [], [], []
    for k in range(3):
        rows = proj[:, k * width : (k + 1) * width]
        halves.append(behind(rows, before[:, k * width : (k + 1) * width], opens[:-1]))
        mixed.append(convolve(rows, halves[k], conv[k]))
        sig.append(jax.nn.sigmoid(mixed[k]))
        acts.append(mixed[k] * sig[k])
    beta = jax.nn.sigmoid(proj[:, 4 * width : 4 * width + heads])
    gain_row = gain[...]

    every = range(heads)
    dos, grads, dbetas = {}, {}, {}
    out = [o_in[:, h * HD : (h + 1) * HD].astype(f32) for h in every]
    gg = [gg_in[:, h * HD : (h + 1) * HD].astype(f32) for h in every]
    wide = [slice(3 * width + h * HD, 3 * width + (h + 1) * HD) for h in every]
    rho = [lax.rsqrt(jnp.mean(x * x, axis=1, keepdims=True) + EPS) for x in out]
    unit_out = [out[h] * rho[h] for h in every]
    gate = [proj[:, wide[h]] for h in every]
    gate_sig = [jax.nn.sigmoid(g) for g in gate]
    for h in every:
        g, s = gate[h], gate_sig[h]
        gpre[:, wide[h]] = (gg[h] * (unit_out[h] * gain_row) * s * (1.0 + g * (1.0 - s))).astype(gpre.dtype)
    dn = [gg[h] * (gate[h] * gate_sig[h]) for h in every]
    ggain[...] += sum(jnp.sum(dn[h] * unit_out[h], axis=0, keepdims=True) for h in every)
    dn = [x * gain_row for x in dn]
    means = [jnp.mean(dn[h] * unit_out[h], axis=1, keepdims=True) for h in every]
    dos = [rho[h] * (dn[h] - unit_out[h] * means[h]) for h in every]

    carried = [dstate[h] for h in every]
    made = {}

    def prepare(c):
        row, col, sees, lasts, joined = chunk_masks(opens[2 * c + 1])
        joined_t = jnp.where((col >= HALF) & (row < HALF), opens[2 * c + 1], 1.0)
        m = made[c] = {}
        m["causal"] = jnp.where(row >= col, joined, 0.0)
        m["strict"] = jnp.where(row > col, joined, 0.0)
        m["causal_t"] = jnp.where(col >= row, joined_t, 0.0)
        m["strict_t"] = jnp.where(col > row, joined_t, 0.0)
        m["sees"], m["lasts"] = sees, lasts
        lines = slice(c * CH, (c + 1) * CH)
        lanes = [slice(h * HD, (h + 1) * HD) for h in every]
        qa = m["qa"] = [acts[0][lines, lanes[h]] for h in every]
        ka = m["ka"] = [acts[1][lines, lanes[h]] for h in every]
        m["rq"], m["rk"] = [unit(x) for x in qa], [unit(x) for x in ka]
        q = m["q"] = [qa[h] * (m["rq"][h] * HD**-0.5) for h in every]
        k = m["k"] = [ka[h] * m["rk"][h] for h in every]
        b = m["b"] = [beta[lines, h : h + 1] for h in every]
        yield
        m["do"] = [dos[h][lines] for h in every]
        m["err"] = [e_in[lines, lanes[h]].astype(f32) for h in every]
        m["delta"] = [b[h] * m["err"][h] for h in every]
        scores_t = [m["causal_t"] * nt(k[h], q[h]) for h in every]
        yield
        m["partial"] = [mm(scores_t[h], m["do"][h]) for h in every]
        m["turned"] = [jnp.transpose(jnp.concatenate([sees * q[h], -sees * k[h]], axis=0)) for h in every]
        yield

    def retreat(c):
        m = made[c]
        ds = m["ds"] = list(carried)
        ddelta = [m["partial"][h] + mm(m["lasts"] * m["k"][h], ds[h]) for h in every]
        yield
        dx = m["dx"] = [mm(t_in[c, h], ddelta[h]) for h in every]
        yield
        m["dr"] = [m["b"][h] * dx[h] for h in every]
        m["both"] = [jnp.concatenate([m["do"][h], m["dr"][h]], axis=0) for h in every]
        for h in every:
            carried[h] = opens[2 * c] * (opens[2 * c + 1] * ds[h] + mm(m["turned"][h], m["both"][h]))
        yield

    def finish(c):
        m = made[c]
        both, delta = m["both"], m["delta"]
        pair = [nt(both[h], delta[h]) for h in every]
        pair_t = [nt(delta[h], both[h]) for h in every]
        yield
        through = [nt(both[h], s_in[c, h]) for h in every]
        from_s = [nt(delta[h], m["ds"][h]) for h in every]
        yield
        dp = [m["causal"] * pair[h][:CH] for h in every]
        dp_t = [m["causal_t"] * pair_t[h][:, :CH] for h in every]
        w = [m["strict"] * pair[h][CH:] + m["strict_t"] * pair_t[h][:, CH:] for h in every]
        from_k = [mm(jnp.concatenate([dp[h], w[h]], axis=0), m["k"][h]) for h in every]
        from_q = [mm(dp_t[h], m["q"][h]) for h in every]
        yield
        qa, ka, rq, rk = m["qa"], m["ka"], m["rq"], m["rk"]
        sees, lasts = m["sees"], m["lasts"]
        dq = [(sees * through[h][:CH] + from_k[h][:CH]) * HD**-0.5 for h in every]
        dk = [lasts * from_s[h] - sees * through[h][CH:] + from_q[h] - from_k[h][CH:] for h in every]
        along_q = [jnp.sum(qa[h] * dq[h], axis=1, keepdims=True) for h in every]
        along_k = [jnp.sum(ka[h] * dk[h], axis=1, keepdims=True) for h in every]
        sums = [jnp.sum(m["dx"][h] * m["err"][h], axis=1, keepdims=True) for h in every]
        yield
        for h in every:
            dbetas[c, h] = sums[h]
            grads[0, c, h] = rq[h] * dq[h] - qa[h] * (rq[h] * rq[h] * rq[h] * along_q[h])
            grads[1, c, h] = rk[h] * dk[h] - ka[h] * (rk[h] * rk[h] * rk[h] * along_k[h])
            grads[2, c, h] = m["dr"][h]
        yield

    last = SUB - 1
    run(prepare(last))
    for c in range(last, -1, -1):
        run(retreat(c), in_order(*([prepare(c - 1)] if c else []), *([finish(c + 1)] if c < last else [])))
    run(finish(0))
    for h in every:
        dstate[h] = carried[h]
    dbeta = jnp.concatenate(
        [jnp.concatenate([dbetas[c, h] for h in range(heads)], axis=1) for c in range(SUB)], axis=0
    )
    dbeta = dbeta * beta * (1.0 - beta)
    dbeta = jnp.concatenate([dbeta, jnp.zeros((STEP, HD - heads), f32)], axis=1)
    gpre[:, 4 * width :] = dbeta.astype(gpre.dtype)
    for k in range(3):
        dact = jnp.concatenate(
            [jnp.concatenate([grads[k, c, h] for h in range(heads)], axis=1) for c in range(SUB)], axis=0
        )
        dmix = dact * sig[k] * (1.0 + mixed[k] * (1.0 - sig[k]))
        nxt = ahead(dmix, after[k], opens)
        dpre = conv[k, TAPS - 1 : TAPS] * dmix
        gconv[k, TAPS - 1 : TAPS] += jnp.sum(
            dmix * proj[:, k * width : (k + 1) * width], axis=0, keepdims=True
        )
        for s in range(1, TAPS):
            dpre = dpre + conv[k, TAPS - 1 - s : TAPS - s] * shift_up(nxt, s)
            gconv[k, TAPS - 1 - s : TAPS - s] += jnp.sum(
                dmix * shift_down(halves[k], s), axis=0, keepdims=True
            )
        after[k] = dmix[:8]
        gpre[:, k * width : (k + 1) * width] = dpre.astype(gpre.dtype)


def core_work(rows, width):
    return pl.CostEstimate(
        flops=60_000 * rows * width, transcendentals=8 * rows * width, bytes_accessed=200 * rows * width
    )


def mixer_forward(starts, proj, conv, gain):
    rows, full = proj.shape
    width = conv.shape[2]
    heads = width // HD
    blocks = rows // STEP
    chunks = blocks * SUB
    per = STEP // 8
    at = lambda i, s: lax.rem(i + s[2 * chunks + 1] * (blocks // 2), blocks)
    prior = lambda i, s: at(jnp.maximum(i - 1, 0), s) * per + per - 1
    return pl.pallas_call(
        functools.partial(forward_kernel, heads=heads),
        grid_spec=pltpu.PrefetchScalarGridSpec(
            num_scalar_prefetch=1,
            grid=(blocks,),
            in_specs=[
                pl.BlockSpec((STEP, full), lambda i, s: (at(i, s), 0)),
                pl.BlockSpec((8, 3 * width), lambda i, s: (prior(i, s), 0)),
                pl.BlockSpec((3, TAPS, width), lambda i, s: (0, 0, 0)),
                pl.BlockSpec((1, HD), lambda i, s: (0, 0)),
            ],
            out_specs=[
                pl.BlockSpec((STEP, width), lambda i, s: (at(i, s), 0)),
                pl.BlockSpec((SUB, heads, HD, HD), lambda i, s: (i, 0, 0, 0)),
                pl.BlockSpec((SUB, heads, CH, CH), lambda i, s: (i, 0, 0, 0)),
                pl.BlockSpec((STEP, width), lambda i, s: (i, 0)),
                pl.BlockSpec((STEP, width), lambda i, s: (i, 0)),
            ],
            scratch_shapes=[pltpu.VMEM((heads, HD, HD), f32)],
        ),
        out_shape=[
            jax.ShapeDtypeStruct((rows, width), bf16),
            jax.ShapeDtypeStruct((chunks, heads, HD, HD), bf16),
            jax.ShapeDtypeStruct((chunks, heads, CH, CH), bf16),
            jax.ShapeDtypeStruct((rows, width), f32),
            jax.ShapeDtypeStruct((rows, width), f32),
        ],
        compiler_params=pltpu.CompilerParams(vmem_limit_bytes=56 * 1024 * 1024),
        cost_estimate=core_work(rows, width),
    )(starts, proj, proj, conv, gain)


def mixer_backward(starts, proj, conv, gain, saved, grad_gated):
    rows, full = proj.shape
    width = conv.shape[2]
    heads = width // HD
    blocks = rows // STEP
    chunks = blocks * SUB
    per = STEP // 8
    back = lambda i: blocks - 1 - i
    at = lambda i, s: lax.rem(back(i) + s[2 * chunks + 1] * (blocks // 2), blocks)
    prior = lambda i, s: at(jnp.minimum(i + 1, blocks - 1), s) * per + per - 1
    return pl.pallas_call(
        functools.partial(backward_kernel, heads=heads, blocks=blocks),
        grid_spec=pltpu.PrefetchScalarGridSpec(
            num_scalar_prefetch=1,
            grid=(blocks,),
            in_specs=[
                pl.BlockSpec((STEP, full), lambda i, s: (at(i, s), 0)),
                pl.BlockSpec((8, 3 * width), lambda i, s: (prior(i, s), 0)),
                pl.BlockSpec((3, TAPS, width), lambda i, s: (0, 0, 0)),
                pl.BlockSpec((1, HD), lambda i, s: (0, 0)),
                pl.BlockSpec((SUB, heads, HD, HD), lambda i, s: (back(i), 0, 0, 0)),
                pl.BlockSpec((SUB, heads, CH, CH), lambda i, s: (back(i), 0, 0, 0)),
                pl.BlockSpec((STEP, width), lambda i, s: (back(i), 0)),
                pl.BlockSpec((STEP, width), lambda i, s: (back(i), 0)),
                pl.BlockSpec((STEP, width), lambda i, s: (at(i, s), 0)),
            ],
            out_specs=[
                pl.BlockSpec((STEP, full), lambda i, s: (at(i, s), 0)),
                pl.BlockSpec((3, TAPS, width), lambda i, s: (0, 0, 0)),
                pl.BlockSpec((1, HD), lambda i, s: (0, 0)),
            ],
            scratch_shapes=[pltpu.VMEM((heads, HD, HD), f32), pltpu.VMEM((3, 8, width), f32)],
        ),
        out_shape=[
            jax.ShapeDtypeStruct((rows, full), bf16),
            jax.ShapeDtypeStruct((3, TAPS, width), f32),
            jax.ShapeDtypeStruct((1, HD), f32),
        ],
        compiler_params=pltpu.CompilerParams(vmem_limit_bytes=56 * 1024 * 1024),
        cost_estimate=core_work(rows, width),
    )(starts, proj, proj, conv, gain, *saved, grad_gated)


BLOCK = 64
EVERY = ("chip", "core", "tensor")
GROUPS = ("chip", "core")


def per_match(places, starts, lengths, values):
    inside = (places[:, None] >= starts[None, :]) & (places[:, None] < (starts + lengths)[None, :])
    return jnp.sum(jnp.where(inside, values[None, :], 0), axis=1)


def total_before(counts):
    size = counts.shape[-1]
    earlier = jnp.tri(size, k=-1, dtype=jnp.int32)
    return jnp.sum(counts[..., None, :] * earlier, axis=-1)


def gather_kernel(index, source, target):
    def move(j, carried):
        target[j] = source[index[j]]
        return carried

    lax.fori_loop(0, target.shape[0], move, 0, unroll=8)


def reorder(blocks, index):
    count, unit, _ = blocks.shape
    if unit % 8:
        chosen = (index[:, None] == jnp.arange(count, dtype=jnp.int32)[None, :]).astype(blocks.dtype)
        return jnp.einsum("ab,buc->auc", chosen, blocks)
    whole = pl.BlockSpec(blocks.shape, lambda i, s: (0, 0, 0))
    return pl.pallas_call(
        gather_kernel,
        grid_spec=pltpu.PrefetchScalarGridSpec(
            num_scalar_prefetch=1, grid=(1,), in_specs=[whole], out_specs=whole
        ),
        out_shape=jax.ShapeDtypeStruct(blocks.shape, blocks.dtype),
        compiler_params=pltpu.CompilerParams(vmem_limit_bytes=32 * 1024 * 1024),
    )(index, blocks)


def routing(seq_lengths, seq_order, groups, rows, depth):
    count = seq_lengths.shape[0]
    per_group = count // groups
    half = rows // (2 * BLOCK)
    part = half // 2
    total = groups * rows // BLOCK
    lengths = seq_lengths // BLOCK
    given = total_before(lengths)
    chosen = seq_order[:, None] == jnp.arange(count, dtype=jnp.int32)[None, :]
    dealt_len = jnp.sum(jnp.where(chosen, lengths[None, :], 0), axis=1)
    dealt_src = jnp.sum(jnp.where(chosen, given[None, :], 0), axis=1)
    by_group = dealt_len.reshape(groups, per_group)
    is_long = by_group == half
    short = jnp.where(is_long, 0, by_group)
    inner = jnp.where(is_long, 0, half + total_before(short))
    base = jnp.arange(groups, dtype=jnp.int32)[:, None] * (2 * half)
    placed = (base + inner).reshape(-1)
    order = jnp.arange(total, dtype=jnp.int32)
    piece, offset = order // part, order % part
    chip, core, plane = piece // (2 * depth), (piece // depth) % 2, piece % depth
    places = (chip * depth + plane) * half + core * part + offset
    take = places + per_match(places, placed, dealt_len, dealt_src - placed)
    goes = order + per_match(order, dealt_src, dealt_len, placed - dealt_src)
    unit, within = goes // half, goes % half
    back = (((unit // depth) * 2 + within // part) * depth + unit % depth) * part + within % part
    own = lax.axis_index("chip") * depth + lax.axis_index("tensor")
    own_places = own * half + jnp.arange(half, dtype=jnp.int32)
    begins = jnp.any(own_places[:, None] == placed[None, :], axis=1).astype(jnp.int32)
    core = lax.axis_index("core").astype(jnp.int32)
    marks = jnp.concatenate([begins, jnp.ones((1,), jnp.int32), core[None]])
    return take, back, marks


def deal(values, groups):
    rows, columns = values.shape
    blocks, unit = rows // BLOCK, BLOCK // groups
    return jnp.swapaxes(values.reshape(blocks, groups, unit, columns), 0, 1)


def spread(dealt):
    groups, blocks, unit, columns = dealt.shape
    dealt = lax.all_to_all(dealt, GROUPS, 0, 0, tiled=True)
    return dealt.reshape(blocks * groups, unit, columns)


def deliver(picked):
    blocks, unit, columns = picked.shape
    depth = lax.axis_size("tensor")
    groups = lax.axis_size("core") * lax.axis_size("chip")
    part = blocks // (groups * depth)
    routed = lax.all_to_all(picked.reshape(groups * depth, part, unit, columns), EVERY, 0, 0, tiled=True)
    routed = routed.reshape(groups, depth, part, unit, columns).transpose(2, 0, 3, 1, 4)
    return routed.reshape(part * BLOCK, depth * columns)


def collect(values, groups):
    rows, width = values.shape
    depth = lax.axis_size("tensor")
    part, unit, columns = rows // BLOCK, BLOCK // groups, width // depth
    parted = values.reshape(part, groups, unit, depth, columns).transpose(1, 3, 0, 2, 4)
    held = lax.all_to_all(parted.reshape(groups * depth, part, unit, columns), EVERY, 0, 0, tiled=True)
    return held.reshape(groups * depth * part, unit, columns)


def bring_home(held, groups):
    count, unit, columns = held.shape
    blocks = count // groups
    home = lax.all_to_all(held.reshape(groups, blocks, unit, columns), GROUPS, 0, 0, tiled=True)
    return jnp.swapaxes(home, 0, 1).reshape(blocks * BLOCK, columns)


def tie(*values):
    return lax.optimization_barrier(values)


def swap(values):
    return lax.ppermute(values, "core", [(0, 1), (1, 0)])


def dot(a, b):
    return jnp.dot(a, b, preferred_element_type=f32)


def norm_back(values, scale, gain, grad_normed, width):
    weighted = gain * grad_normed
    along = jnp.sum(weighted * values, axis=1, keepdims=True)
    grad_values = scale * weighted - values * (scale * scale * scale) * along / width
    return grad_values, jnp.sum(grad_normed * values * scale, axis=0)


ROOM = pltpu.CompilerParams(vmem_limit_bytes=48 * 1024 * 1024)


def moved(*arrays):
    size = sum(a.size * a.dtype.itemsize for a in arrays)
    return pl.CostEstimate(flops=0, transcendentals=0, bytes_accessed=size)


def shape_of(shape, dtype=bf16):
    return jax.ShapeDtypeStruct(shape, dtype)


def whole(shape):
    return pl.BlockSpec(shape, lambda *i: (0,) * len(shape))


def columns_at(place, size):
    return pl.ds(pl.multiple_of(place * size, 128), size)


def mixer_weights_kernel(source, beta, target, out):
    depth, _, width = source.shape[1:]
    lines = target.shape[0]
    kinds = (target.shape[1] - width) // (depth * width)
    for z in range(depth):
        for k in range(kinds):
            lane = (k * depth + z) * width
            target[:, lane : lane + width] = source[0, z, k * lines : (k + 1) * lines]
        for n in range(lines // width):
            line = kinds * lines + n * width
            out[z * width : (z + 1) * width, n * width : (n + 1) * width] = source[0, z, line : line + width]
    target[:, kinds * depth * width :] = beta[...]


def mixer_weights(parts, beta, kinds):
    chips, depth, _, width = parts.shape
    rows = beta.shape[0]
    lines = rows // chips
    wide = kinds * depth * width + width
    out_lines = max(lines, width)
    return pl.pallas_call(
        mixer_weights_kernel,
        grid=(chips,),
        in_specs=[
            pl.BlockSpec((1, depth, (kinds + 1) * lines, width), lambda i: (i, 0, 0, 0)),
            pl.BlockSpec((lines, width), lambda i: (i, 0)),
        ],
        out_specs=[
            pl.BlockSpec((lines, wide), lambda i: (i, 0)),
            pl.BlockSpec((depth * width, out_lines), lambda i: (0, i)),
        ],
        out_shape=[shape_of((rows, wide)), shape_of((depth * width, chips * out_lines))],
        compiler_params=ROOM,
        cost_estimate=moved(parts, parts),
    )(parts, beta)


def ff_weights_kernel(source, target):
    depth = source.shape[1]
    kinds, lines = target.shape[0], target.shape[1] // depth
    for z in range(depth):
        for k in range(kinds):
            target[k, z * lines : (z + 1) * lines] = source[0, z, k * lines : (k + 1) * lines]


def ff_weights(parts, kinds):
    chips, depth, lines, width = parts.shape
    lines = lines // kinds
    if chips != 4:
        apart = parts.reshape(chips, depth, kinds, lines, width)
        return apart.transpose(2, 1, 3, 0, 4).reshape(kinds, depth * lines, chips * width)
    return pl.pallas_call(
        ff_weights_kernel,
        grid=(chips,),
        in_specs=[pl.BlockSpec((1, depth, kinds * lines, width), lambda i: (i, 0, 0, 0))],
        out_specs=pl.BlockSpec((kinds, depth * lines, width), lambda i: (0, 0, i)),
        out_shape=shape_of((kinds, depth * lines, chips * width)),
        compiler_params=ROOM,
        cost_estimate=moved(parts, parts),
    )(parts)


def place_kernel(order, *refs):
    target = refs[-1]
    for k, slot in enumerate(refs[:-1]):
        target[order[k]] = slot[...]


def place(slots, order):
    count, (rows, width) = len(slots), slots[0].shape
    return pl.pallas_call(
        place_kernel,
        grid_spec=pltpu.PrefetchScalarGridSpec(
            num_scalar_prefetch=1,
            grid=(1,),
            in_specs=[whole((rows, width))] * count,
            out_specs=whole((count, rows, width)),
        ),
        out_shape=shape_of((count, rows, width)),
        compiler_params=ROOM,
        cost_estimate=moved(*slots, *slots),
    )(order, *slots)


def place_columns_kernel(order, *refs):
    target = refs[-1]
    for k, slot in enumerate(refs[:-1]):
        target[:, columns_at(order[k], slot.shape[1])] = slot[...]


def place_columns(slots, order):
    count, (rows, width) = len(slots), slots[0].shape
    return pl.pallas_call(
        place_columns_kernel,
        grid_spec=pltpu.PrefetchScalarGridSpec(
            num_scalar_prefetch=1,
            grid=(1,),
            in_specs=[whole((rows, width))] * count,
            out_specs=whole((rows, count * width)),
        ),
        out_shape=shape_of((rows, count * width)),
        compiler_params=ROOM,
        cost_estimate=moved(*slots, *slots),
    )(order, *slots)


def split_ff_kernel(pair, single, target):
    depth = target.shape[1]
    lines = single.shape[0] // depth
    for z in range(depth):
        part = slice(z * lines, (z + 1) * lines)
        target[0, z, :lines] = pair[0, part]
        target[0, z, lines : 2 * lines] = pair[1, part]
        target[0, z, 2 * lines :] = single[part]


def split_ff(pair, single, depth):
    rows, width = single.shape[0], single.shape[1] // 4
    shape = (depth, 3 * rows // depth, width)
    return pl.pallas_call(
        split_ff_kernel,
        grid=(4,),
        in_specs=[
            pl.BlockSpec((2, rows, width), lambda i: (0, 0, i)),
            pl.BlockSpec((rows, width), lambda i: (0, i)),
        ],
        out_specs=pl.BlockSpec((1,) + shape, lambda i: (i, 0, 0, 0)),
        out_shape=shape_of((4,) + shape),
        compiler_params=ROOM,
        cost_estimate=moved(pair, pair, single, single),
    )(pair, single)


def tn(a, b):
    return mm(a, b, 0, 0)


FREE = pl.CostEstimate(flops=0, transcendentals=0, bytes_accessed=0)
WIDE_ROOM = pltpu.CompilerParams(vmem_limit_bytes=56 * 1024 * 1024)


def mixer_grads_kernel(
    near, normed, grad_pre, grad_mix, gated, proj, gains, gain_mid, conv, grad_head, *targets, kinds
):
    step = pl.program_id(0)
    chip = near[step]
    depth, _, width = targets[0].shape
    lines = normed.shape[1]
    wide = depth * width
    total = jnp.zeros((lines, 1), f32)
    parts = []
    for n in range(kinds + 1):
        lanes = slice(n * wide, n * wide + (wide if n < kinds else width))
        part = tn(normed[...], grad_pre[:, lanes])
        total = total + jnp.sum(part * proj[:, lanes].astype(f32), axis=1, keepdims=True)
        parts.append(part)
    out = tn(grad_mix[...], gated[...])
    lane = lax.broadcasted_iota(jnp.int32, (lines, width), 1)
    turned = jnp.transpose(jnp.where(lane == depth, total, parts[kinds]))
    gain_in = turned[depth : depth + 1] / gains[0:1]
    blank = jnp.zeros((1, width), f32)

    def in_lines(row, keep):
        row = row * keep
        return [row[:, n * width : (n + 1) * width] for n in range(lines // width)]

    for k, target in enumerate(targets):

        @pl.when(step == k)
        def _():
            for z in range(depth):
                lanes = slice(z * width, (z + 1) * width)
                for n in range(kinds):
                    target[z, n * lines : (n + 1) * lines] = parts[n][:, lanes].astype(bf16)
                target[z, kinds * lines : (kinds + 1) * lines] = out[:, lanes].astype(bf16)
                here = jnp.where(chip == z, 1.0, 0.0)
                small = in_lines(turned[z : z + 1], 1.0) + in_lines(gain_in, here) + in_lines(gain_mid[0:1], here)
                small.append(conv[chip, :, lanes])
                small.append(grad_head[...] * jnp.where(chip == 0, 1.0, 0.0))
                count = 3 * (lines // width) + conv.shape[1] + 1
                small += [blank] * (16 - count)
                target[z, (kinds + 1) * lines :] = jnp.concatenate(small, axis=0).astype(bf16)


def mixer_grads(normed, grad_pre, grad_mix, gated, proj, gains, gain_mid, conv, grad_head, near, depth, kinds):
    rows, width = normed.shape
    lines = width // 4
    shape = (depth, (kinds + 1) * lines + 16, HD)
    column = lambda a: pl.BlockSpec((a.shape[0], lines), lambda i, s: (0, s[i]))
    conv = conv.reshape(4, -1, depth * HD)
    return pl.pallas_call(
        functools.partial(mixer_grads_kernel, kinds=kinds),
        grid_spec=pltpu.PrefetchScalarGridSpec(
            num_scalar_prefetch=1,
            grid=(4,),
            in_specs=[
                column(normed),
                whole(grad_pre.shape),
                column(grad_mix),
                whole(gated.shape),
                pl.BlockSpec((lines, proj.shape[1]), lambda i, s: (s[i], 0)),
                column(gains),
                column(gain_mid),
                whole(conv.shape),
                whole(grad_head.shape),
            ],
            out_specs=[whole(shape)] * 4,
        ),
        out_shape=[shape_of(shape)] * 4,
        compiler_params=WIDE_ROOM,
        cost_estimate=pl.CostEstimate(flops=40_000_000_000, transcendentals=0, bytes_accessed=100_000_000),
    )(near, normed, grad_pre, grad_mix, gated, proj, gains, gain_mid, conv, grad_head)


def send_back_kernel(grad_pre, proj, target):
    target[...] = nt(grad_pre[...], proj[...]).astype(target.dtype)


def send_back(grad_pre, proj):
    rows, wide = grad_pre.shape
    width = proj.shape[0]
    block, steps = 256, rows // 512
    return pl.pallas_call(
        send_back_kernel,
        grid=(steps,),
        in_specs=[pl.BlockSpec((block, wide), lambda i: (steps + i, 0)), whole(proj.shape)],
        out_specs=pl.BlockSpec((block, width), lambda i: (i, 0)),
        out_shape=shape_of((rows // 2, width)),
        compiler_params=WIDE_ROOM,
        cost_estimate=FREE,
    )(grad_pre, proj)


def keep_back_kernel(grad_pre, proj, came, values, gain, grad_middle, target):
    grad_normed = nt(grad_pre[...], proj[...]) + came[...].astype(f32)
    rows = values[...].astype(f32)
    scale = lax.rsqrt(jnp.mean(rows * rows, axis=1, keepdims=True) + EPS)
    weighted = gain[...] * grad_normed
    along = jnp.mean(weighted * rows, axis=1, keepdims=True)
    grad = scale * weighted - rows * (scale * scale * scale * along)
    target[...] = (grad_middle[...] + grad).astype(target.dtype)


def keep_back(grad_pre, proj, came, values, gain, grad_middle):
    rows, wide = grad_pre.shape
    width = proj.shape[0]
    block = 256
    line = lambda w: pl.BlockSpec((block, w), lambda i: (i, 0))
    return pl.pallas_call(
        keep_back_kernel,
        grid=(rows // 512,),
        in_specs=[
            line(wide),
            whole(proj.shape),
            line(width),
            line(width),
            whole(gain.shape),
            line(width),
        ],
        out_specs=line(width),
        out_shape=shape_of((rows // 2, width)),
        compiler_params=WIDE_ROOM,
        cost_estimate=FREE,
    )(grad_pre, proj, came, values, gain, grad_middle)


def add_kernel(ahead, *refs):
    for j, target in enumerate(refs[-4:]):
        total = refs[0][ahead[j]].astype(f32)
        for source in refs[1:-4]:
            total = total + source[ahead[j]].astype(f32)
        target[...] = total.astype(bf16)


def add_parts(parts, ahead):
    depth, rows, width = parts[0].shape
    steps = 2
    block = rows // steps
    return pl.pallas_call(
        add_kernel,
        grid_spec=pltpu.PrefetchScalarGridSpec(
            num_scalar_prefetch=1,
            grid=(steps,),
            in_specs=[pl.BlockSpec((depth, block, width), lambda i, s: (0, i, 0))] * len(parts),
            out_specs=[pl.BlockSpec((block, width), lambda i, s: (i, 0))] * 4,
        ),
        out_shape=[shape_of((rows, width))] * 4,
        compiler_params=ROOM,
        cost_estimate=moved(*parts, parts[0]),
    )(ahead, *parts)


def join_ff_kernel(where, own, other, pair, single):
    lines = single.shape[0] // 2
    for side, slot in enumerate((own, other)):
        core = where[4] if side == 0 else 1 - where[4]
        rows = pl.ds(pl.multiple_of(core * lines, 8), lines)
        pair[0, rows] = slot[0, :lines].astype(f32)
        pair[1, rows] = slot[0, lines : 2 * lines].astype(f32)
        single[rows] = slot[0, 2 * lines :].astype(f32)


def join_ff(own, other, where):
    _, lines, width = own.shape
    rows = 2 * lines // 3
    piece = pl.BlockSpec((1, lines, width), lambda i, s: (i, 0, 0))
    return pl.pallas_call(
        join_ff_kernel,
        grid_spec=pltpu.PrefetchScalarGridSpec(
            num_scalar_prefetch=1,
            grid=(4,),
            in_specs=[piece, piece],
            out_specs=[
                pl.BlockSpec((2, rows, width), lambda i, s: (0, 0, i)),
                pl.BlockSpec((rows, width), lambda i, s: (0, i)),
            ],
        ),
        out_shape=[shape_of((2, rows, 4 * width), f32), shape_of((rows, 4 * width), f32)],
        compiler_params=ROOM,
        cost_estimate=moved(*[own] * 6),
    )(where, own, other)


def join_mixer_kernel(where, *refs):
    proj, out, small = refs[-3:]
    kinds = proj.shape[0]
    lines, width = proj.shape[1] // 4, proj.shape[2] // 2
    for k in range(4):
        mine, theirs = refs[k][...].astype(f32), refs[4 + k][...].astype(f32)
        first = jnp.where(where[4] == 0, mine, theirs)
        second = jnp.where(where[4] == 0, theirs, mine)
        rows = pl.ds(pl.multiple_of(where[k] * lines, 128), lines)
        for n in range(kinds):
            proj[n, rows, :width] = first[n * lines : (n + 1) * lines]
            proj[n, rows, width:] = second[n * lines : (n + 1) * lines]
        line = kinds * lines
        out[:width, columns_at(where[k], lines)] = jnp.transpose(first[line : line + lines])
        out[width:, columns_at(where[k], lines)] = jnp.transpose(second[line : line + lines])
        small[0, where[k]] = first[line + lines :]
        small[1, where[k]] = second[line + lines :]


def join_mixer(own, other, where, kinds, lines):
    rows, width = own[0].shape
    rest = rows - (kinds + 1) * lines
    outs = [(kinds, 4 * lines, 2 * width), (2 * width, 4 * lines), (2, 4, rest, width)]
    return pl.pallas_call(
        join_mixer_kernel,
        grid_spec=pltpu.PrefetchScalarGridSpec(
            num_scalar_prefetch=1,
            grid=(1,),
            in_specs=[whole((rows, width))] * 8,
            out_specs=[whole(o) for o in outs],
        ),
        out_shape=[shape_of(o, f32) for o in outs],
        compiler_params=ROOM,
        cost_estimate=moved(*[*own] * 6),
    )(where, *own, *other)


def ff_kernel(rows, cot, pair, down, hidden, grads):
    size = down.shape[0]
    for start in range(0, size, 512):
        part = slice(start, min(start + 512, size))
        gate = nt(rows[...], pair[0, part])
        up = nt(rows[...], pair[1, part])
        back = nt(cot[...], down[part])
        sig = jax.nn.sigmoid(gate)
        act = gate * sig
        hidden[:, part] = (act * up).astype(hidden.dtype)
        grads[0, :, part] = (back * up * (sig * (1.0 + gate * (1.0 - sig)))).astype(grads.dtype)
        grads[1, :, part] = (back * act).astype(grads.dtype)


def feed_forward(rows, cot, pair, down):
    count, width = rows.shape
    size = down.shape[0]
    block = 256
    line = lambda w: pl.BlockSpec((block, w), lambda i: (i, 0))
    return pl.pallas_call(
        ff_kernel,
        grid=(count // block,),
        in_specs=[line(width), line(width), whole(pair.shape), whole(down.shape)],
        out_specs=[line(size), pl.BlockSpec((2, block, size), lambda i: (0, i, 0))],
        out_shape=[shape_of((count, size)), shape_of((2, count, size))],
        compiler_params=pltpu.CompilerParams(vmem_limit_bytes=56 * 1024 * 1024),
        cost_estimate=pl.CostEstimate(
            flops=6 * count * width * size, transcendentals=count * size, bytes_accessed=40_000_000
        ),
    )(rows, cot, pair, down)


def to_near(slots):
    return [slots[0]] + [
        lax.ppermute(slots[k], "chip", [(i, i ^ k) for i in range(4)]) for k in range(1, len(slots))
    ]


def to_ahead(slots):
    count = len(slots)
    return [slots[0]] + [
        lax.ppermute(slots[j], "tensor", [(i, (i + j) % count) for i in range(count)])
        for j in range(1, count)
    ]


def total_of(sums):
    return sum(s.astype(f32) for s in sums).astype(bf16)


def sum_scattered(parts, chips, depth):
    flat = parts.reshape(-1, parts.shape[-1])
    summed = lax.psum_scatter(flat, "chip", scatter_dimension=0, tiled=True)
    return lax.psum_scatter(summed, "tensor", scatter_dimension=0, tiled=True)


def reduce_parts(parts, chips, depth):
    _, _, rows, columns = parts.shape
    full = lax.all_gather(sum_scattered(parts, chips, depth), GROUPS, axis=0)
    return full.reshape(chips, 2, rows, columns).astype(f32)


def cut(array, chips, axis):
    size = array.shape[axis] // chips
    return lax.dynamic_slice_in_dim(array, lax.axis_index("chip") * size, size, axis)


def on_device(
    layer_input,
    out_cotangent,
    norm_gains,
    proj_weight,
    beta_weight,
    conv_weight,
    head_gain,
    out_weight,
    mlp_weight,
    down_weight,
    seq_lengths,
    seq_order,
):
    rows, columns = layer_input.shape
    depth = lax.axis_size("tensor")
    chips = lax.axis_size("chip")
    groups = 2 * chips
    width = columns * depth
    own_rows = rows // 4
    core = lax.axis_index("core")

    def mine(array, axis):
        size = array.shape[axis] // 2
        return jnp.where(
            core == 0,
            lax.slice_in_dim(array, 0, size, axis=axis),
            lax.slice_in_dim(array, size, 2 * size, axis=axis),
        )

    chip, plane = lax.axis_index("chip"), lax.axis_index("tensor")
    few = chips == 4
    planes_behind = lax.rem(plane + depth - jnp.arange(depth, dtype=jnp.int32), depth)
    planes_ahead = lax.rem(plane + jnp.arange(depth, dtype=jnp.int32), depth)
    near = chip ^ jnp.arange(4, dtype=jnp.int32)
    where = jnp.concatenate([near, core[None]])
    everywhere = ("chip", "tensor")
    kinds = proj_weight.shape[0]
    heads_wide = depth * HD
    lines = width // chips
    hidden_half = down_weight.shape[0] // 2

    take, back, marks = routing(seq_lengths, seq_order, groups, rows, depth)
    layer_input, proj_weight = tie(deal(layer_input, groups), proj_weight)
    dealt_in = spread(layer_input)
    out_half = cut(mine(out_weight, 0), chips, 1)
    out_half = jnp.swapaxes(out_half.reshape(HD, -1, min(HD, lines)), 0, 1).reshape(-1, min(HD, lines))
    out_half = out_half.reshape(-1, HD)
    mixer_half = [cut(mine(proj_weight, 2), chips, 1).reshape(-1, HD), out_half]
    small_wide = jnp.concatenate([norm_gains.reshape(-1), mine(conv_weight, 2).reshape(-1)])
    high = lax.reduce_precision(small_wide, 8, 7)
    middle_term = lax.reduce_precision(small_wide - high, 8, 7)
    low_term = small_wide - high - middle_term
    small = [mine(beta_weight, 1).reshape(-1)] + [t.astype(bf16) for t in (high, middle_term, low_term)]
    small = jnp.concatenate(small).reshape(-1, HD)
    small_rows = small.shape[0]
    small_piece = -(-small_rows // (16 * chips)) * 16
    small = jnp.pad(small, ((0, small_piece * chips - small_rows), (0, 0)))
    mixer_half = jnp.concatenate(mixer_half + [cut(small, chips, 0)], axis=0)
    mixer_parts = lax.all_gather(mixer_half, everywhere, axis=0).reshape(chips, depth, -1, HD)
    small = jnp.swapaxes(mixer_parts[:, :, -small_piece:], 0, 1).reshape(depth, -1)
    wide_size = small_wide.shape[0]
    beta_proj = jnp.pad(small[:, :width].T, ((0, 0), (0, HD - depth)))
    high, middle_term, low_term = (
        small[:, width + n * wide_size : width + (n + 1) * wide_size].astype(f32) for n in range(3)
    )
    small_wide = high + (middle_term + low_term)
    gains = small_wide[:, : 2 * columns].reshape(depth, 2, columns)
    gains = jnp.swapaxes(gains, 0, 1).reshape(2, width)
    conv = small_wide[:, 2 * columns :].reshape(depth, 3, TAPS, HD)
    conv = conv.transpose(1, 2, 0, 3).reshape(3, TAPS, heads_wide)
    if few:
        proj, out_proj = mixer_weights(mixer_parts, beta_proj, kinds)
    else:
        proj = mixer_weights(mixer_parts, beta_proj, kinds)[0]
        out_proj = mixer_parts[:, :, kinds * lines : (kinds + 1) * lines].reshape(chips, depth, HD, lines)
        out_proj = out_proj.transpose(1, 2, 0, 3).reshape(heads_wide, width)
    down_half = cut(mine(down_weight, 0), chips, 1)
    down_slots = to_ahead([down_half] * depth) if few else [down_half]
    pair_half = cut(mine(jnp.swapaxes(mlp_weight, 1, 2), 1), chips, 2)
    dealt_in, down_slots, pair_half, dealt_cot = tie(dealt_in, down_slots, pair_half, deal(out_cotangent, groups))
    rows_own = deliver(reorder(dealt_in, take))
    rows_own, dealt_cot = tie(rows_own, dealt_cot)
    dealt_cot = spread(dealt_cot)
    pair_parts = lax.all_gather(pair_half.reshape(2 * hidden_half, -1), everywhere, axis=0)

    low = jnp.concatenate([rows_own, swap(rows_own)], axis=0)
    all_rows = low.astype(f32)
    scale_all = lax.rsqrt(jnp.mean(jnp.square(all_rows), axis=1, keepdims=True) + EPS)
    normed = (all_rows * scale_all * gains[0]).astype(bf16)
    projected = dot(normed, proj)
    gain_row = head_gain[None, :]

    projected, dealt_cot = tie(projected, dealt_cot)
    picked_cot = reorder(dealt_cot, take)
    down_plane = place(down_slots, planes_behind) if few else down_slots[0]
    projected, picked_cot, down_plane = tie(projected, picked_cot, down_plane)
    cot_own = deliver(picked_cot)
    if few:
        down_slots = to_near([down_plane.reshape(depth * hidden_half, -1)] * 4)
    else:
        down_slots = lax.all_gather(down_plane, everywhere, axis=0)
    gated, *saved = mixer_forward(marks, projected, conv, gain_row)

    rows_f = rows_own.astype(f32)
    scale_in = scale_all[:own_rows]
    out_of = lambda part: dot(part, out_proj)
    mixed = swap(out_of(gated[own_rows:]).astype(bf16))
    middle = rows_f + out_of(gated[:own_rows]) + mixed.astype(f32)
    scale_mid = lax.rsqrt(jnp.mean(jnp.square(middle), axis=1, keepdims=True) + EPS)
    normed_mid_own = (middle * scale_mid * gains[1]).astype(bf16)
    normed_mid_own, cot_own, down_slots = tie(normed_mid_own, cot_own, down_slots)
    if few:
        down = place_columns(down_slots, near)
    else:
        down = down_slots.reshape(chips, depth * hidden_half, -1).transpose(1, 0, 2).reshape(-1, width)
    cot = jnp.concatenate([cot_own, swap(cot_own)], axis=0)
    normed_mid = jnp.concatenate([normed_mid_own, swap(normed_mid_own)], axis=0)

    pair = ff_weights(pair_parts.reshape(chips, depth, 2 * hidden_half, -1), 2)
    hidden, grad_gate_up = feed_forward(normed_mid, cot, pair, down)

    grad_pair = jnp.einsum("ktf,td->kfd", grad_gate_up, normed_mid, preferred_element_type=f32).astype(bf16)
    grad_down = jnp.einsum("tf,td->fd", hidden, cot, preferred_element_type=f32).astype(bf16)
    if few:
        ff_terms = split_ff(grad_pair, grad_down, depth)
        grad_gate_up, hidden, ff_terms = tie(grad_gate_up, hidden, ff_terms)
        ff_chip = lax.psum_scatter(ff_terms.reshape(-1, lines), "chip", scatter_dimension=0, tiled=True)

    lower = swap(dot(hidden[own_rows:], down).astype(bf16))
    total = middle + dot(hidden[:own_rows], down) + lower.astype(f32)
    total_low, grad_gate_up = tie(total.astype(bf16), grad_gate_up)
    held_out = collect(total_low, groups)
    from_mlp = lambda part: jnp.einsum("ktf,kfd->td", part, pair, preferred_element_type=f32)
    came = swap(from_mlp(grad_gate_up[:, own_rows:]).astype(bf16))
    grad_normed_mid = from_mlp(grad_gate_up[:, :own_rows]) + came.astype(f32)
    mid_back, grad_gain_mid = norm_back(middle, scale_mid, gains[1], grad_normed_mid, width)
    grad_middle = cot_own.astype(f32) + mid_back
    grad_mix_own = grad_middle.astype(bf16)
    (grad_mix,) = tie(jnp.concatenate([grad_mix_own, swap(grad_mix_own)], axis=0))
    grad_gated = jnp.einsum("td,ed->te", grad_mix, out_proj, preferred_element_type=f32)
    grad_pre, grad_conv, grad_head = mixer_backward(marks, projected, conv, gain_row, saved, grad_gated)
    if few:
        grad_pre, held_out = tie(grad_pre, held_out)

    sent = send_back(grad_pre, proj)
    if few:
        sent, ff_chip = tie(sent, ff_chip)
        ff_own = lax.psum_scatter(ff_chip, "tensor", scatter_dimension=0, tiled=True)
    came = swap(sent)
    grad_input = keep_back(grad_pre, proj, came, rows_own, gains[0:1], grad_middle)
    grad_input, grad_pre, grad_mix = tie(grad_input, grad_pre, grad_mix)
    held_grad = collect(grad_input, groups)

    if few:
        mixer_terms = mixer_grads(
            normed,
            grad_pre,
            grad_mix,
            gated,
            proj,
            gains,
            grad_gain_mid[None],
            grad_conv,
            grad_head,
            near,
            depth,
            kinds,
        )
        _, ff_own = tie(mixer_terms[0], ff_own)
        mixer_terms, ff_own = tie(to_near(mixer_terms), lax.all_gather(ff_own, "chip", axis=0))
        sums, ff_other = tie(to_ahead(add_parts(mixer_terms, planes_ahead)), swap(ff_own))
        mixer_own = to_near([total_of(sums)] * 4)
        mixer_sums = mixer_own, [swap(s) for s in mixer_own]
        grad_pair_out, grad_down_out = join_ff(ff_own, ff_other, where)
    held_grad, held_out = tie(held_grad, held_out)
    both = jnp.concatenate([reorder(held_out, back), reorder(held_grad, back)], axis=2)
    both = bring_home(both, groups)
    layer_output, input_grad = both[:, :columns], both[:, columns:]
    if few:
        grad_proj_out, grad_out_out, small_sums = join_mixer(*mixer_sums, where, kinds, lines)
        across = lines // HD
        beta_sums = small_sums[:, :, :across].reshape(2, width)
        gain_sums = jnp.sum(small_sums[:, :, across : 3 * across], axis=1).reshape(2, 2, columns)
        conv_lines = 3 * TAPS // 4
        conv_sums = small_sums[:, :, 3 * across : 3 * across + conv_lines].reshape(2, 3, TAPS, HD)
        head_sums = small_sums[:, 0, 3 * across + conv_lines]
    else:
        every = jnp.concatenate([grad_pair, grad_down[None]], axis=0)
        every = every.reshape(3, depth, hidden_half, chips, lines).transpose(3, 1, 0, 2, 4)
        sums = reduce_parts(every.reshape(chips, depth, 3 * hidden_half, lines), chips, depth)
        sums = sums.reshape(chips, 2, 3, hidden_half, lines).transpose(2, 1, 3, 0, 4)
        sums = sums.reshape(3, 2 * hidden_half, width)
        grad_pair_out, grad_down_out = sums[:2], sums[2]
        grad_out = jnp.einsum("td,te->de", grad_mix, gated, preferred_element_type=f32).astype(bf16)
        grad_proj = jnp.einsum("td,te->de", normed, grad_pre, preferred_element_type=f32)
        grad_gain_in = jnp.sum(grad_proj * proj.astype(f32), axis=1) / gains[0]
        gain_parts = jnp.stack([grad_gain_in, grad_gain_mid]).reshape(2, depth, columns)
        small_terms = jnp.concatenate(
            [
                jnp.swapaxes(gain_parts, 0, 1).reshape(depth, -1),
                grad_proj[:, kinds * heads_wide : kinds * heads_wide + depth].T,
                grad_conv.reshape(3 * TAPS, depth, HD).transpose(1, 0, 2).reshape(depth, -1),
                jnp.broadcast_to(grad_head, (depth, HD)),
            ],
            axis=1,
        )
        small_count = small_terms.shape[1]
        small_lines = chips * -(-small_count // (chips * HD))
        small_terms = jnp.pad(small_terms, ((0, 0), (0, small_lines * HD - small_count)))
        small_terms = jnp.swapaxes(small_terms.reshape(depth, small_lines, HD), 0, 1).astype(bf16)
        grad_proj = grad_proj.astype(bf16)
        every = [
            grad_proj[:, : kinds * heads_wide].reshape(chips, lines, kinds, depth, HD).transpose(0, 3, 2, 1, 4),
            grad_out.reshape(chips, lines, 1, depth, HD).transpose(0, 3, 2, 1, 4),
            small_terms.reshape(chips, -1, 1, depth, HD).transpose(0, 3, 2, 1, 4),
        ]
        every = jnp.concatenate([e.reshape(chips, depth, -1, HD) for e in every], axis=2)
        sums = reduce_parts(every, chips, depth)
        many = sums[:, :, : (kinds + 1) * lines].reshape(chips, 2, kinds + 1, lines, HD)
        many = many.transpose(2, 0, 3, 1, 4).reshape(kinds + 1, width, 2 * HD)
        grad_proj_out, grad_out_out = many[:kinds], many[kinds].T
        small_sums = jnp.swapaxes(sums[:, :, (kinds + 1) * lines :], 0, 1).reshape(2, -1)
        gains_at, beta_at, conv_at = 2 * columns, 2 * columns + width, 2 * columns + width + 3 * TAPS * HD
        gain_sums = small_sums[:, :gains_at].reshape(2, 2, columns)
        beta_sums = small_sums[:, gains_at:beta_at]
        conv_sums = small_sums[:, beta_at:conv_at].reshape(2, 3, TAPS, HD)
        head_sums = small_sums[:, conv_at : conv_at + HD]
    grad_mlp_out = jnp.swapaxes(grad_pair_out, 1, 2)

    grad_gains = gain_sums[0] + gain_sums[1]
    grad_beta_out = beta_sums.T
    grad_conv_out = conv_sums.transpose(1, 2, 0, 3).reshape(3, TAPS, 2 * HD)
    grad_head_out = head_sums[0] + head_sums[1]
    return (
        layer_output,
        input_grad,
        grad_gains,
        grad_proj_out,
        grad_beta_out,
        grad_conv_out,
        grad_head_out,
        grad_out_out,
        grad_mlp_out,
        grad_down_out,
    )


def solution(mesh):
    devices = mesh.devices
    chips = devices.shape[0] // 2
    fine = Mesh(devices.reshape(chips, 2, devices.shape[1]), EVERY)
    return jax.shard_map(
        on_device,
        mesh=fine,
        in_specs=(
            P(GROUPS, "tensor"),
            P(GROUPS, "tensor"),
            P(None, "tensor"),
            P(None, None, "tensor"),
            P(None, "tensor"),
            P(None, None, "tensor"),
            P(),
            P("tensor", None),
            P(None, None, "tensor"),
            P("tensor", None),
            P(),
            P(),
        ),
        out_specs=(
            P(GROUPS, "tensor"),
            P(GROUPS, "tensor"),
            P(None, "tensor"),
            P(None, None, "tensor"),
            P(None, "tensor"),
            P(None, None, "tensor"),
            P(),
            P("tensor", None),
            P(None, None, "tensor"),
            P("tensor", None),
        ),
        check_vma=False,
    )
```

```python
import functools

import jax
import jax.numpy as jnp
from jax import lax
from jax.experimental import pallas as pl
from jax.experimental.pallas import tpu as pltpu
from jax.sharding import Mesh, PartitionSpec as P

CH = 128
SUB = 4
STEP = CH * SUB
HALF = 64
HD = 128
TAPS = 4
EPS = 1e-6
f32, bf16 = jnp.float32, jnp.bfloat16


def mm(a, b, ca=1, cb=0):
    return lax.dot_general(
        a.astype(bf16), b.astype(bf16), (((ca,), (cb,)), ((), ())), preferred_element_type=f32
    )


def nt(a, b):
    return mm(a, b, 1, 1)


def grid_ids():
    row = lax.broadcasted_iota(jnp.int32, (CH, CH), 0)
    col = lax.broadcasted_iota(jnp.int32, (CH, CH), 1)
    return row, col


def inverse(systems):
    row, col = grid_ids()
    eye = jnp.where(row == col, 1.0, 0.0)
    pair = (row // 2 == col // 2) & (row > col)
    found = [eye - jnp.where(pair, a, 0.0) for a in systems]
    size = 2
    while size < CH:
        inside = (
            (row // (2 * size) == col // (2 * size))
            & ((row // size) % 2 == 1)
            & ((col // size) % 2 == 0)
        )
        right = [mm(jnp.where(inside, a, 0.0), t) for a, t in zip(systems, found)]
        found = [t - mm(t, r) for t, r in zip(found, right)]
        size *= 2
    return found


def run(*parts):
    parts = list(parts)
    while parts:
        parts = [part for part in parts if next(part, parts) is not parts]


def in_order(*parts):
    for part in parts:
        yield from part


def behind(rows, before, opens):
    halves = []
    for n, is_open in enumerate(opens):
        prior = before if n == 0 else rows[n * HALF - 8 : n * HALF]
        halves.append(jnp.concatenate([prior * is_open, rows[n * HALF : (n + 1) * HALF]], axis=0))
    return halves


def ahead(rows, after, opens):
    halves = []
    for n in range(len(opens) - 1):
        next_rows = after if n == len(opens) - 2 else rows[(n + 1) * HALF : (n + 1) * HALF + 8]
        halves.append(
            jnp.concatenate([rows[n * HALF : (n + 1) * HALF], next_rows * opens[n + 1]], axis=0)
        )
    return halves


def shift_down(halves, s):
    return jnp.concatenate([h[8 - s : 8 - s + HALF] for h in halves], axis=0)


def shift_up(halves, s):
    return jnp.concatenate([h[s : s + HALF] for h in halves], axis=0)


def head(x, h):
    return x[:, h * HD : (h + 1) * HD]


def convolve(rows, halves, taps):
    mixed = taps[TAPS - 1 : TAPS] * rows
    for s in range(1, TAPS):
        mixed = mixed + taps[TAPS - 1 - s : TAPS - s] * shift_down(halves, s)
    return mixed


def unit(z):
    return lax.rsqrt(jnp.sum(z * z, axis=1, keepdims=True) + EPS)


def chunk_masks(open1):
    row, col = grid_ids()
    r1 = lax.broadcasted_iota(jnp.int32, (CH, 1), 0)
    sees = jnp.where(r1 < HALF, 1.0, open1)
    lasts = jnp.where(r1 < HALF, open1, 1.0)
    joined = jnp.where((row >= HALF) & (col < HALF), open1, 1.0)
    return row, col, sees, lasts, joined


def forward_kernel(
    starts, proj, before, conv, gain, gated_out, s_out, t_out, e_out, o_out, state, *, heads
):
    i = pl.program_id(0)
    width = heads * HD

    @pl.when(i == 0)
    def _():
        state[...] = jnp.zeros_like(state)

    opens = [1.0 - starts[2 * SUB * i + n].astype(f32) for n in range(2 * SUB)]
    acts = []
    for k in range(3):
        rows = proj[:, k * width : (k + 1) * width]
        mixed = convolve(rows, behind(rows, before[:, k * width : (k + 1) * width], opens), conv[k])
        acts.append(mixed * jax.nn.sigmoid(mixed))
    beta = jax.nn.sigmoid(proj[:, 4 * width : 4 * width + heads])

    pairs = [(c, h) for c in range(SUB) for h in range(heads)]
    masks = [chunk_masks(opens[2 * c + 1]) for c in range(SUB)]
    q, k, v, b, grams, scores = {}, {}, {}, {}, {}, {}
    for h in range(heads):
        qa, ka, va = (head(acts[n], h) for n in range(3))
        qa = qa * (unit(qa) * HD**-0.5)
        ka = ka * unit(ka)
        for c in range(SUB):
            lines = slice(c * CH, (c + 1) * CH)
            q[c, h], k[c, h], v[c, h] = qa[lines], ka[lines], va[lines]
            b[c, h] = beta[lines, h : h + 1]
            row, col, sees, lasts, joined = masks[c]
            both = nt(jnp.concatenate([k[c, h], q[c, h]], axis=0), k[c, h])
            grams[c, h] = jnp.where(row > col, joined, 0.0) * both[:CH]
            scores[c, h] = jnp.where(row >= col, joined, 0.0) * both[CH:]
    solved = dict(zip(pairs, inverse([b[p] * grams[p] for p in pairs])))
    every = range(heads)
    carried = [state[h] for h in every]
    for c in range(SUB):
        row, col, sees, lasts, joined = masks[c]
        begun = [carried[h] * opens[2 * c] for h in every]
        seen = [mm(jnp.concatenate([sees * k[c, h], sees * q[c, h]], axis=0), begun[h]) for h in every]
        rest = [v[c, h] - seen[h][:CH] for h in every]
        delta = [mm(solved[c, h], b[c, h] * rest[h]) for h in every]
        err = [rest[h] - mm(grams[c, h], delta[h]) for h in every]
        delta = [b[c, h] * err[h] for h in every]
        added = [mm(jnp.transpose(lasts * k[c, h]), delta[h]) for h in every]
        carried = [opens[2 * c + 1] * begun[h] + added[h] for h in every]
        outs = [seen[h][CH:] + mm(scores[c, h], delta[h]) for h in every]
        lines = slice(c * CH, (c + 1) * CH)
        for h in every:
            out = outs[h]
            s_out[c, h] = begun[h].astype(s_out.dtype)
            t_out[c, h] = jnp.transpose(solved[c, h]).astype(t_out.dtype)
            at = (lines, slice(h * HD, (h + 1) * HD))
            e_out[at] = err[h].astype(e_out.dtype)
            o_out[at] = out.astype(o_out.dtype)
            rho = lax.rsqrt(jnp.mean(out * out, axis=1, keepdims=True) + EPS)
            gate = proj[lines, 3 * width + h * HD : 3 * width + (h + 1) * HD]
            gate = gate * jax.nn.sigmoid(gate)
            gated_out[at] = (out * rho * gain[...] * gate).astype(gated_out.dtype)
    for h in every:
        state[h] = carried[h]


def backward_kernel(
    starts,
    proj,
    before,
    conv,
    gain,
    s_in,
    t_in,
    e_in,
    o_in,
    gg_in,
    gpre,
    gconv,
    ggain,
    dstate,
    after,
    *,
    heads,
    blocks,
):
    step = pl.program_id(0)
    i = blocks - 1 - step
    width = heads * HD

    @pl.when(step == 0)
    def _():
        dstate[...] = jnp.zeros_like(dstate)
        after[...] = jnp.zeros_like(after)
        gconv[...] = jnp.zeros_like(gconv)
        ggain[...] = jnp.zeros_like(ggain)

    opens = [1.0 - starts[2 * SUB * i + n].astype(f32) for n in range(2 * SUB + 1)]
    mixed, acts, sig, halves = [], [], [], []
    for k in range(3):
        rows = proj[:, k * width : (k + 1) * width]
        halves.append(behind(rows, before[:, k * width : (k + 1) * width], opens[:-1]))
        mixed.append(convolve(rows, halves[k], conv[k]))
        sig.append(jax.nn.sigmoid(mixed[k]))
        acts.append(mixed[k] * sig[k])
    beta = jax.nn.sigmoid(proj[:, 4 * width : 4 * width + heads])
    gain_row = gain[...]

    every = range(heads)
    dos, grads, dbetas = {}, {}, {}
    out = [o_in[:, h * HD : (h + 1) * HD].astype(f32) for h in every]
    gg = [gg_in[:, h * HD : (h + 1) * HD].astype(f32) for h in every]
    wide = [slice(3 * width + h * HD, 3 * width + (h + 1) * HD) for h in every]
    rho = [lax.rsqrt(jnp.mean(x * x, axis=1, keepdims=True) + EPS) for x in out]
    unit_out = [out[h] * rho[h] for h in every]
    gate = [proj[:, wide[h]] for h in every]
    gate_sig = [jax.nn.sigmoid(g) for g in gate]
    for h in every:
        g, s = gate[h], gate_sig[h]
        gpre[:, wide[h]] = (gg[h] * (unit_out[h] * gain_row) * s * (1.0 + g * (1.0 - s))).astype(gpre.dtype)
    dn = [gg[h] * (gate[h] * gate_sig[h]) for h in every]
    ggain[...] += sum(jnp.sum(dn[h] * unit_out[h], axis=0, keepdims=True) for h in every)
    dn = [x * gain_row for x in dn]
    means = [jnp.mean(dn[h] * unit_out[h], axis=1, keepdims=True) for h in every]
    dos = [rho[h] * (dn[h] - unit_out[h] * means[h]) for h in every]

    carried = [dstate[h] for h in every]
    made = {}

    def prepare(c):
        row, col, sees, lasts, joined = chunk_masks(opens[2 * c + 1])
        joined_t = jnp.where((col >= HALF) & (row < HALF), opens[2 * c + 1], 1.0)
        m = made[c] = {}
        m["causal"] = jnp.where(row >= col, joined, 0.0)
        m["strict"] = jnp.where(row > col, joined, 0.0)
        m["causal_t"] = jnp.where(col >= row, joined_t, 0.0)
        m["strict_t"] = jnp.where(col > row, joined_t, 0.0)
        m["sees"], m["lasts"] = sees, lasts
        lines = slice(c * CH, (c + 1) * CH)
        lanes = [slice(h * HD, (h + 1) * HD) for h in every]
        qa = m["qa"] = [acts[0][lines, lanes[h]] for h in every]
        ka = m["ka"] = [acts[1][lines, lanes[h]] for h in every]
        m["rq"], m["rk"] = [unit(x) for x in qa], [unit(x) for x in ka]
        q = m["q"] = [qa[h] * (m["rq"][h] * HD**-0.5) for h in every]
        k = m["k"] = [ka[h] * m["rk"][h] for h in every]
        b = m["b"] = [beta[lines, h : h + 1] for h in every]
        yield
        m["do"] = [dos[h][lines] for h in every]
        m["err"] = [e_in[lines, lanes[h]].astype(f32) for h in every]
        m["delta"] = [b[h] * m["err"][h] for h in every]
        scores_t = [m["causal_t"] * nt(k[h], q[h]) for h in every]
        yield
        m["partial"] = [mm(scores_t[h], m["do"][h]) for h in every]
        m["turned"] = [jnp.transpose(jnp.concatenate([sees * q[h], -sees * k[h]], axis=0)) for h in every]
        yield

    def retreat(c):
        m = made[c]
        ds = m["ds"] = list(carried)
        ddelta = [m["partial"][h] + mm(m["lasts"] * m["k"][h], ds[h]) for h in every]
        yield
        dx = m["dx"] = [mm(t_in[c, h], ddelta[h]) for h in every]
        yield
        m["dr"] = [m["b"][h] * dx[h] for h in every]
        m["both"] = [jnp.concatenate([m["do"][h], m["dr"][h]], axis=0) for h in every]
        for h in every:
            carried[h] = opens[2 * c] * (opens[2 * c + 1] * ds[h] + mm(m["turned"][h], m["both"][h]))
        yield

    def finish(c):
        m = made[c]
        both, delta = m["both"], m["delta"]
        pair = [nt(both[h], delta[h]) for h in every]
        pair_t = [nt(delta[h], both[h]) for h in every]
        yield
        through = [nt(both[h], s_in[c, h]) for h in every]
        from_s = [nt(delta[h], m["ds"][h]) for h in every]
        yield
        dp = [m["causal"] * pair[h][:CH] for h in every]
        dp_t = [m["causal_t"] * pair_t[h][:, :CH] for h in every]
        w = [m["strict"] * pair[h][CH:] + m["strict_t"] * pair_t[h][:, CH:] for h in every]
        from_k = [mm(jnp.concatenate([dp[h], w[h]], axis=0), m["k"][h]) for h in every]
        from_q = [mm(dp_t[h], m["q"][h]) for h in every]
        yield
        qa, ka, rq, rk = m["qa"], m["ka"], m["rq"], m["rk"]
        sees, lasts = m["sees"], m["lasts"]
        dq = [(sees * through[h][:CH] + from_k[h][:CH]) * HD**-0.5 for h in every]
        dk = [lasts * from_s[h] - sees * through[h][CH:] + from_q[h] - from_k[h][CH:] for h in every]
        along_q = [jnp.sum(qa[h] * dq[h], axis=1, keepdims=True) for h in every]
        along_k = [jnp.sum(ka[h] * dk[h], axis=1, keepdims=True) for h in every]
        sums = [jnp.sum(m["dx"][h] * m["err"][h], axis=1, keepdims=True) for h in every]
        yield
        for h in every:
            dbetas[c, h] = sums[h]
            grads[0, c, h] = rq[h] * dq[h] - qa[h] * (rq[h] * rq[h] * rq[h] * along_q[h])
            grads[1, c, h] = rk[h] * dk[h] - ka[h] * (rk[h] * rk[h] * rk[h] * along_k[h])
            grads[2, c, h] = m["dr"][h]
        yield

    last = SUB - 1
    run(prepare(last))
    for c in range(last, -1, -1):
        run(retreat(c), in_order(*([prepare(c - 1)] if c else []), *([finish(c + 1)] if c < last else [])))
    run(finish(0))
    for h in every:
        dstate[h] = carried[h]
    dbeta = jnp.concatenate(
        [jnp.concatenate([dbetas[c, h] for h in range(heads)], axis=1) for c in range(SUB)], axis=0
    )
    dbeta = dbeta * beta * (1.0 - beta)
    dbeta = jnp.concatenate([dbeta, jnp.zeros((STEP, HD - heads), f32)], axis=1)
    gpre[:, 4 * width :] = dbeta.astype(gpre.dtype)
    for k in range(3):
        dact = jnp.concatenate(
            [jnp.concatenate([grads[k, c, h] for h in range(heads)], axis=1) for c in range(SUB)], axis=0
        )
        dmix = dact * sig[k] * (1.0 + mixed[k] * (1.0 - sig[k]))
        nxt = ahead(dmix, after[k], opens)
        dpre = conv[k, TAPS - 1 : TAPS] * dmix
        gconv[k, TAPS - 1 : TAPS] += jnp.sum(
            dmix * proj[:, k * width : (k + 1) * width], axis=0, keepdims=True
        )
        for s in range(1, TAPS):
            dpre = dpre + conv[k, TAPS - 1 - s : TAPS - s] * shift_up(nxt, s)
            gconv[k, TAPS - 1 - s : TAPS - s] += jnp.sum(
                dmix * shift_down(halves[k], s), axis=0, keepdims=True
            )
        after[k] = dmix[:8]
        gpre[:, k * width : (k + 1) * width] = dpre.astype(gpre.dtype)


def core_work(rows, width):
    return pl.CostEstimate(
        flops=60_000 * rows * width, transcendentals=8 * rows * width, bytes_accessed=200 * rows * width
    )


def mixer_forward(starts, proj, conv, gain):
    rows, full = proj.shape
    width = conv.shape[2]
    heads = width // HD
    blocks = rows // STEP
    chunks = blocks * SUB
    per = STEP // 8
    at = lambda i, s: lax.rem(i + s[2 * chunks + 1] * (blocks // 2), blocks)
    prior = lambda i, s: at(jnp.maximum(i - 1, 0), s) * per + per - 1
    return pl.pallas_call(
        functools.partial(forward_kernel, heads=heads),
        grid_spec=pltpu.PrefetchScalarGridSpec(
            num_scalar_prefetch=1,
            grid=(blocks,),
            in_specs=[
                pl.BlockSpec((STEP, full), lambda i, s: (at(i, s), 0)),
                pl.BlockSpec((8, 3 * width), lambda i, s: (prior(i, s), 0)),
                pl.BlockSpec((3, TAPS, width), lambda i, s: (0, 0, 0)),
                pl.BlockSpec((1, HD), lambda i, s: (0, 0)),
            ],
            out_specs=[
                pl.BlockSpec((STEP, width), lambda i, s: (at(i, s), 0)),
                pl.BlockSpec((SUB, heads, HD, HD), lambda i, s: (i, 0, 0, 0)),
                pl.BlockSpec((SUB, heads, CH, CH), lambda i, s: (i, 0, 0, 0)),
                pl.BlockSpec((STEP, width), lambda i, s: (i, 0)),
                pl.BlockSpec((STEP, width), lambda i, s: (i, 0)),
            ],
            scratch_shapes=[pltpu.VMEM((heads, HD, HD), f32)],
        ),
        out_shape=[
            jax.ShapeDtypeStruct((rows, width), bf16),
            jax.ShapeDtypeStruct((chunks, heads, HD, HD), bf16),
            jax.ShapeDtypeStruct((chunks, heads, CH, CH), bf16),
            jax.ShapeDtypeStruct((rows, width), f32),
            jax.ShapeDtypeStruct((rows, width), f32),
        ],
        compiler_params=pltpu.CompilerParams(vmem_limit_bytes=56 * 1024 * 1024),
        cost_estimate=core_work(rows, width),
    )(starts, proj, proj, conv, gain)


def mixer_backward(starts, proj, conv, gain, saved, grad_gated):
    rows, full = proj.shape
    width = conv.shape[2]
    heads = width // HD
    blocks = rows // STEP
    chunks = blocks * SUB
    per = STEP // 8
    back = lambda i: blocks - 1 - i
    at = lambda i, s: lax.rem(back(i) + s[2 * chunks + 1] * (blocks // 2), blocks)
    prior = lambda i, s: at(jnp.minimum(i + 1, blocks - 1), s) * per + per - 1
    return pl.pallas_call(
        functools.partial(backward_kernel, heads=heads, blocks=blocks),
        grid_spec=pltpu.PrefetchScalarGridSpec(
            num_scalar_prefetch=1,
            grid=(blocks,),
            in_specs=[
                pl.BlockSpec((STEP, full), lambda i, s: (at(i, s), 0)),
                pl.BlockSpec((8, 3 * width), lambda i, s: (prior(i, s), 0)),
                pl.BlockSpec((3, TAPS, width), lambda i, s: (0, 0, 0)),
                pl.BlockSpec((1, HD), lambda i, s: (0, 0)),
                pl.BlockSpec((SUB, heads, HD, HD), lambda i, s: (back(i), 0, 0, 0)),
                pl.BlockSpec((SUB, heads, CH, CH), lambda i, s: (back(i), 0, 0, 0)),
                pl.BlockSpec((STEP, width), lambda i, s: (back(i), 0)),
                pl.BlockSpec((STEP, width), lambda i, s: (back(i), 0)),
                pl.BlockSpec((STEP, width), lambda i, s: (at(i, s), 0)),
            ],
            out_specs=[
                pl.BlockSpec((STEP, full), lambda i, s: (at(i, s), 0)),
                pl.BlockSpec((3, TAPS, width), lambda i, s: (0, 0, 0)),
                pl.BlockSpec((1, HD), lambda i, s: (0, 0)),
            ],
            scratch_shapes=[pltpu.VMEM((heads, HD, HD), f32), pltpu.VMEM((3, 8, width), f32)],
        ),
        out_shape=[
            jax.ShapeDtypeStruct((rows, full), bf16),
            jax.ShapeDtypeStruct((3, TAPS, width), f32),
            jax.ShapeDtypeStruct((1, HD), f32),
        ],
        compiler_params=pltpu.CompilerParams(vmem_limit_bytes=56 * 1024 * 1024),
        cost_estimate=core_work(rows, width),
    )(starts, proj, proj, conv, gain, *saved, grad_gated)


BLOCK = 64
EVERY = ("chip", "core", "tensor")
GROUPS = ("chip", "core")


def per_match(places, starts, lengths, values):
    inside = (places[:, None] >= starts[None, :]) & (places[:, None] < (starts + lengths)[None, :])
    return jnp.sum(jnp.where(inside, values[None, :], 0), axis=1)


def total_before(counts):
    size = counts.shape[-1]
    earlier = jnp.tri(size, k=-1, dtype=jnp.int32)
    return jnp.sum(counts[..., None, :] * earlier, axis=-1)


def gather_kernel(index, source, target):
    def move(j, carried):
        target[j] = source[index[j]]
        return carried

    lax.fori_loop(0, target.shape[0], move, 0, unroll=8)


def reorder(blocks, index):
    count, unit, _ = blocks.shape
    if unit % 8:
        chosen = (index[:, None] == jnp.arange(count, dtype=jnp.int32)[None, :]).astype(blocks.dtype)
        return jnp.einsum("ab,buc->auc", chosen, blocks)
    whole = pl.BlockSpec(blocks.shape, lambda i, s: (0, 0, 0))
    return pl.pallas_call(
        gather_kernel,
        grid_spec=pltpu.PrefetchScalarGridSpec(
            num_scalar_prefetch=1, grid=(1,), in_specs=[whole], out_specs=whole
        ),
        out_shape=jax.ShapeDtypeStruct(blocks.shape, blocks.dtype),
        compiler_params=pltpu.CompilerParams(vmem_limit_bytes=32 * 1024 * 1024),
    )(index, blocks)


def routing(seq_lengths, seq_order, groups, rows, depth):
    count = seq_lengths.shape[0]
    per_group = count // groups
    half = rows // (2 * BLOCK)
    part = half // 2
    total = groups * rows // BLOCK
    lengths = seq_lengths // BLOCK
    given = total_before(lengths)
    chosen = seq_order[:, None] == jnp.arange(count, dtype=jnp.int32)[None, :]
    dealt_len = jnp.sum(jnp.where(chosen, lengths[None, :], 0), axis=1)
    dealt_src = jnp.sum(jnp.where(chosen, given[None, :], 0), axis=1)
    by_group = dealt_len.reshape(groups, per_group)
    is_long = by_group == half
    short = jnp.where(is_long, 0, by_group)
    inner = jnp.where(is_long, 0, half + total_before(short))
    base = jnp.arange(groups, dtype=jnp.int32)[:, None] * (2 * half)
    placed = (base + inner).reshape(-1)
    order = jnp.arange(total, dtype=jnp.int32)
    piece, offset = order // part, order % part
    chip, core, plane = piece // (2 * depth), (piece // depth) % 2, piece % depth
    places = (chip * depth + plane) * half + core * part + offset
    take = places + per_match(places, placed, dealt_len, dealt_src - placed)
    goes = order + per_match(order, dealt_src, dealt_len, placed - dealt_src)
    unit, within = goes // half, goes % half
    back = (((unit // depth) * 2 + within // part) * depth + unit % depth) * part + within % part
    own = lax.axis_index("chip") * depth + lax.axis_index("tensor")
    own_places = own * half + jnp.arange(half, dtype=jnp.int32)
    begins = jnp.any(own_places[:, None] == placed[None, :], axis=1).astype(jnp.int32)
    core = lax.axis_index("core").astype(jnp.int32)
    marks = jnp.concatenate([begins, jnp.ones((1,), jnp.int32), core[None]])
    return take, back, marks


def deal(values, groups):
    rows, columns = values.shape
    blocks, unit = rows // BLOCK, BLOCK // groups
    return jnp.swapaxes(values.reshape(blocks, groups, unit, columns), 0, 1)


def spread(dealt):
    groups, blocks, unit, columns = dealt.shape
    dealt = lax.all_to_all(dealt, GROUPS, 0, 0, tiled=True)
    return dealt.reshape(blocks * groups, unit, columns)


def deliver(picked):
    blocks, unit, columns = picked.shape
    depth = lax.axis_size("tensor")
    groups = lax.axis_size("core") * lax.axis_size("chip")
    part = blocks // (groups * depth)
    routed = lax.all_to_all(picked.reshape(groups * depth, part, unit, columns), EVERY, 0, 0, tiled=True)
    routed = routed.reshape(groups, depth, part, unit, columns).transpose(2, 0, 3, 1, 4)
    return routed.reshape(part * BLOCK, depth * columns)


def collect(values, groups):
    rows, width = values.shape
    depth = lax.axis_size("tensor")
    part, unit, columns = rows // BLOCK, BLOCK // groups, width // depth
    parted = values.reshape(part, groups, unit, depth, columns).transpose(1, 3, 0, 2, 4)
    held = lax.all_to_all(parted.reshape(groups * depth, part, unit, columns), EVERY, 0, 0, tiled=True)
    return held.reshape(groups * depth * part, unit, columns)


def bring_home(held, groups):
    count, unit, columns = held.shape
    blocks = count // groups
    home = lax.all_to_all(held.reshape(groups, blocks, unit, columns), GROUPS, 0, 0, tiled=True)
    return jnp.swapaxes(home, 0, 1).reshape(blocks * BLOCK, columns)


def tie(*values):
    return lax.optimization_barrier(values)


def swap(values):
    return lax.ppermute(values, "core", [(0, 1), (1, 0)])


def dot(a, b):
    return jnp.dot(a, b, preferred_element_type=f32)


def norm_back(values, scale, gain, grad_normed, width):
    weighted = gain * grad_normed
    along = jnp.sum(weighted * values, axis=1, keepdims=True)
    grad_values = scale * weighted - values * (scale * scale * scale) * along / width
    return grad_values, jnp.sum(grad_normed * values * scale, axis=0)


ROOM = pltpu.CompilerParams(vmem_limit_bytes=48 * 1024 * 1024)


def moved(*arrays):
    size = sum(a.size * a.dtype.itemsize for a in arrays)
    return pl.CostEstimate(flops=0, transcendentals=0, bytes_accessed=size)


def shape_of(shape, dtype=bf16):
    return jax.ShapeDtypeStruct(shape, dtype)


def whole(shape):
    return pl.BlockSpec(shape, lambda *i: (0,) * len(shape))


def columns_at(place, size):
    return pl.ds(pl.multiple_of(place * size, 128), size)


def mixer_weights_kernel(source, beta, target, out):
    depth, _, width = source.shape[1:]
    lines = target.shape[0]
    kinds = (target.shape[1] - width) // (depth * width)
    for z in range(depth):
        for k in range(kinds):
            lane = (k * depth + z) * width
            target[:, lane : lane + width] = source[0, z, k * lines : (k + 1) * lines]
        for n in range(lines // width):
            line = kinds * lines + n * width
            out[z * width : (z + 1) * width, n * width : (n + 1) * width] = source[0, z, line : line + width]
    target[:, kinds * depth * width :] = beta[...]


def mixer_weights(parts, beta, kinds):
    chips, depth, _, width = parts.shape
    rows = beta.shape[0]
    lines = rows // chips
    wide = kinds * depth * width + width
    out_lines = max(lines, width)
    return pl.pallas_call(
        mixer_weights_kernel,
        grid=(chips,),
        in_specs=[
            pl.BlockSpec((1, depth, (kinds + 1) * lines, width), lambda i: (i, 0, 0, 0)),
            pl.BlockSpec((lines, width), lambda i: (i, 0)),
        ],
        out_specs=[
            pl.BlockSpec((lines, wide), lambda i: (i, 0)),
            pl.BlockSpec((depth * width, out_lines), lambda i: (0, i)),
        ],
        out_shape=[shape_of((rows, wide)), shape_of((depth * width, chips * out_lines))],
        compiler_params=ROOM,
        cost_estimate=moved(parts, parts),
    )(parts, beta)


def ff_weights_kernel(source, target):
    depth = source.shape[1]
    kinds, lines = target.shape[0], target.shape[1] // depth
    for z in range(depth):
        for k in range(kinds):
            target[k, z * lines : (z + 1) * lines] = source[0, z, k * lines : (k + 1) * lines]


def ff_weights(parts, kinds):
    chips, depth, lines, width = parts.shape
    lines = lines // kinds
    if chips != 4:
        apart = parts.reshape(chips, depth, kinds, lines, width)
        return apart.transpose(2, 1, 3, 0, 4).reshape(kinds, depth * lines, chips * width)
    return pl.pallas_call(
        ff_weights_kernel,
        grid=(chips,),
        in_specs=[pl.BlockSpec((1, depth, kinds * lines, width), lambda i: (i, 0, 0, 0))],
        out_specs=pl.BlockSpec((kinds, depth * lines, width), lambda i: (0, 0, i)),
        out_shape=shape_of((kinds, depth * lines, chips * width)),
        compiler_params=ROOM,
        cost_estimate=moved(parts, parts),
    )(parts)


def place_kernel(order, *refs):
    target = refs[-1]
    for k, slot in enumerate(refs[:-1]):
        target[order[k]] = slot[...]


def place(slots, order):
    count, (rows, width) = len(slots), slots[0].shape
    return pl.pallas_call(
        place_kernel,
        grid_spec=pltpu.PrefetchScalarGridSpec(
            num_scalar_prefetch=1,
            grid=(1,),
            in_specs=[whole((rows, width))] * count,
            out_specs=whole((count, rows, width)),
        ),
        out_shape=shape_of((count, rows, width)),
        compiler_params=ROOM,
        cost_estimate=moved(*slots, *slots),
    )(order, *slots)


def place_columns_kernel(order, *refs):
    target = refs[-1]
    for k, slot in enumerate(refs[:-1]):
        target[:, columns_at(order[k], slot.shape[1])] = slot[...]


def place_columns(slots, order):
    count, (rows, width) = len(slots), slots[0].shape
    return pl.pallas_call(
        place_columns_kernel,
        grid_spec=pltpu.PrefetchScalarGridSpec(
            num_scalar_prefetch=1,
            grid=(1,),
            in_specs=[whole((rows, width))] * count,
            out_specs=whole((rows, count * width)),
        ),
        out_shape=shape_of((rows, count * width)),
        compiler_params=ROOM,
        cost_estimate=moved(*slots, *slots),
    )(order, *slots)


def split_ff_kernel(pair, single, target):
    depth = target.shape[1]
    lines = single.shape[0] // depth
    for z in range(depth):
        part = slice(z * lines, (z + 1) * lines)
        target[0, z, :lines] = pair[0, part]
        target[0, z, lines : 2 * lines] = pair[1, part]
        target[0, z, 2 * lines :] = single[part]


def split_ff(pair, single, depth):
    rows, width = single.shape[0], single.shape[1] // 4
    shape = (depth, 3 * rows // depth, width)
    return pl.pallas_call(
        split_ff_kernel,
        grid=(4,),
        in_specs=[
            pl.BlockSpec((2, rows, width), lambda i: (0, 0, i)),
            pl.BlockSpec((rows, width), lambda i: (0, i)),
        ],
        out_specs=pl.BlockSpec((1,) + shape, lambda i: (i, 0, 0, 0)),
        out_shape=shape_of((4,) + shape),
        compiler_params=ROOM,
        cost_estimate=moved(pair, pair, single, single),
    )(pair, single)


def tn(a, b):
    return mm(a, b, 0, 0)


FREE = pl.CostEstimate(flops=0, transcendentals=0, bytes_accessed=0)
WIDE_ROOM = pltpu.CompilerParams(vmem_limit_bytes=56 * 1024 * 1024)


def mixer_grads_kernel(
    near, normed, grad_pre, grad_mix, gated, proj, gains, gain_mid, conv, grad_head, *targets, kinds
):
    step = pl.program_id(0)
    chip = near[step]
    depth, _, width = targets[0].shape
    lines = normed.shape[1]
    wide = depth * width
    total = jnp.zeros((lines, 1), f32)
    parts = []
    for n in range(kinds + 1):
        lanes = slice(n * wide, n * wide + (wide if n < kinds else width))
        part = tn(normed[...], grad_pre[:, lanes])
        total = total + jnp.sum(part * proj[:, lanes].astype(f32), axis=1, keepdims=True)
        parts.append(part)
    out = tn(grad_mix[...], gated[...])
    lane = lax.broadcasted_iota(jnp.int32, (lines, width), 1)
    turned = jnp.transpose(jnp.where(lane == depth, total, parts[kinds]))
    gain_in = turned[depth : depth + 1] / gains[0:1]
    blank = jnp.zeros((1, width), f32)

    def in_lines(row, keep):
        row = row * keep
        return [row[:, n * width : (n + 1) * width] for n in range(lines // width)]

    for k, target in enumerate(targets):

        @pl.when(step == k)
        def _():
            for z in range(depth):
                lanes = slice(z * width, (z + 1) * width)
                for n in range(kinds):
                    target[z, n * lines : (n + 1) * lines] = parts[n][:, lanes].astype(bf16)
                target[z, kinds * lines : (kinds + 1) * lines] = out[:, lanes].astype(bf16)
                here = jnp.where(chip == z, 1.0, 0.0)
                small = in_lines(turned[z : z + 1], 1.0) + in_lines(gain_in, here) + in_lines(gain_mid[0:1], here)
                small.append(conv[chip, :, lanes])
                small.append(grad_head[...] * jnp.where(chip == 0, 1.0, 0.0))
                count = 3 * (lines // width) + conv.shape[1] + 1
                small += [blank] * (16 - count)
                target[z, (kinds + 1) * lines :] = jnp.concatenate(small, axis=0).astype(bf16)


def mixer_grads(normed, grad_pre, grad_mix, gated, proj, gains, gain_mid, conv, grad_head, near, depth, kinds):
    rows, width = normed.shape
    lines = width // 4
    shape = (depth, (kinds + 1) * lines + 16, HD)
    column = lambda a: pl.BlockSpec((a.shape[0], lines), lambda i, s: (0, s[i]))
    conv = conv.reshape(4, -1, depth * HD)
    return pl.pallas_call(
        functools.partial(mixer_grads_kernel, kinds=kinds),
        grid_spec=pltpu.PrefetchScalarGridSpec(
            num_scalar_prefetch=1,
            grid=(4,),
            in_specs=[
                column(normed),
                whole(grad_pre.shape),
                column(grad_mix),
                whole(gated.shape),
                pl.BlockSpec((lines, proj.shape[1]), lambda i, s: (s[i], 0)),
                column(gains),
                column(gain_mid),
                whole(conv.shape),
                whole(grad_head.shape),
            ],
            out_specs=[whole(shape)] * 4,
        ),
        out_shape=[shape_of(shape)] * 4,
        compiler_params=WIDE_ROOM,
        cost_estimate=pl.CostEstimate(flops=40_000_000_000, transcendentals=0, bytes_accessed=100_000_000),
    )(near, normed, grad_pre, grad_mix, gated, proj, gains, gain_mid, conv, grad_head)


def send_back_kernel(grad_pre, proj, target):
    target[...] = nt(grad_pre[...], proj[...]).astype(target.dtype)


def send_back(grad_pre, proj):
    rows, wide = grad_pre.shape
    width = proj.shape[0]
    block, steps = 256, rows // 512
    return pl.pallas_call(
        send_back_kernel,
        grid=(steps,),
        in_specs=[pl.BlockSpec((block, wide), lambda i: (steps + i, 0)), whole(proj.shape)],
        out_specs=pl.BlockSpec((block, width), lambda i: (i, 0)),
        out_shape=shape_of((rows // 2, width)),
        compiler_params=WIDE_ROOM,
        cost_estimate=FREE,
    )(grad_pre, proj)


def keep_back_kernel(grad_pre, proj, came, values, gain, grad_middle, target):
    grad_normed = nt(grad_pre[...], proj[...]) + came[...].astype(f32)
    rows = values[...].astype(f32)
    scale = lax.rsqrt(jnp.mean(rows * rows, axis=1, keepdims=True) + EPS)
    weighted = gain[...] * grad_normed
    along = jnp.mean(weighted * rows, axis=1, keepdims=True)
    grad = scale * weighted - rows * (scale * scale * scale * along)
    target[...] = (grad_middle[...] + grad).astype(target.dtype)


def keep_back(grad_pre, proj, came, values, gain, grad_middle):
    rows, wide = grad_pre.shape
    width = proj.shape[0]
    block = 256
    line = lambda w: pl.BlockSpec((block, w), lambda i: (i, 0))
    return pl.pallas_call(
        keep_back_kernel,
        grid=(rows // 512,),
        in_specs=[
            line(wide),
            whole(proj.shape),
            line(width),
            line(width),
            whole(gain.shape),
            line(width),
        ],
        out_specs=line(width),
        out_shape=shape_of((rows // 2, width)),
        compiler_params=WIDE_ROOM,
        cost_estimate=FREE,
    )(grad_pre, proj, came, values, gain, grad_middle)


def add_kernel(ahead, *refs):
    for j, target in enumerate(refs[-4:]):
        total = refs[0][ahead[j]].astype(f32)
        for source in refs[1:-4]:
            total = total + source[ahead[j]].astype(f32)
        target[...] = total.astype(bf16)


def add_parts(parts, ahead):
    depth, rows, width = parts[0].shape
    steps = 2
    block = rows // steps
    return pl.pallas_call(
        add_kernel,
        grid_spec=pltpu.PrefetchScalarGridSpec(
            num_scalar_prefetch=1,
            grid=(steps,),
            in_specs=[pl.BlockSpec((depth, block, width), lambda i, s: (0, i, 0))] * len(parts),
            out_specs=[pl.BlockSpec((block, width), lambda i, s: (i, 0))] * 4,
        ),
        out_shape=[shape_of((rows, width))] * 4,
        compiler_params=ROOM,
        cost_estimate=moved(*parts, parts[0]),
    )(ahead, *parts)


def join_ff_kernel(where, own, other, pair, single):
    lines = single.shape[0] // 2
    for side, slot in enumerate((own, other)):
        core = where[4] if side == 0 else 1 - where[4]
        rows = pl.ds(pl.multiple_of(core * lines, 8), lines)
        pair[0, rows] = slot[0, :lines].astype(f32)
        pair[1, rows] = slot[0, lines : 2 * lines].astype(f32)
        single[rows] = slot[0, 2 * lines :].astype(f32)


def join_ff(own, other, where):
    _, lines, width = own.shape
    rows = 2 * lines // 3
    piece = pl.BlockSpec((1, lines, width), lambda i, s: (i, 0, 0))
    return pl.pallas_call(
        join_ff_kernel,
        grid_spec=pltpu.PrefetchScalarGridSpec(
            num_scalar_prefetch=1,
            grid=(4,),
            in_specs=[piece, piece],
            out_specs=[
                pl.BlockSpec((2, rows, width), lambda i, s: (0, 0, i)),
                pl.BlockSpec((rows, width), lambda i, s: (0, i)),
            ],
        ),
        out_shape=[shape_of((2, rows, 4 * width), f32), shape_of((rows, 4 * width), f32)],
        compiler_params=ROOM,
        cost_estimate=moved(*[own] * 6),
    )(where, own, other)


def join_mixer_kernel(where, *refs):
    proj, out, small = refs[-3:]
    kinds = proj.shape[0]
    lines, width = proj.shape[1] // 4, proj.shape[2] // 2
    for k in range(4):
        mine, theirs = refs[k][...].astype(f32), refs[4 + k][...].astype(f32)
        first = jnp.where(where[4] == 0, mine, theirs)
        second = jnp.where(where[4] == 0, theirs, mine)
        rows = pl.ds(pl.multiple_of(where[k] * lines, 128), lines)
        for n in range(kinds):
            proj[n, rows, :width] = first[n * lines : (n + 1) * lines]
            proj[n, rows, width:] = second[n * lines : (n + 1) * lines]
        line = kinds * lines
        out[:width, columns_at(where[k], lines)] = jnp.transpose(first[line : line + lines])
        out[width:, columns_at(where[k], lines)] = jnp.transpose(second[line : line + lines])
        small[0, where[k]] = first[line + lines :]
        small[1, where[k]] = second[line + lines :]


def join_mixer(own, other, where, kinds, lines):
    rows, width = own[0].shape
    rest = rows - (kinds + 1) * lines
    outs = [(kinds, 4 * lines, 2 * width), (2 * width, 4 * lines), (2, 4, rest, width)]
    return pl.pallas_call(
        join_mixer_kernel,
        grid_spec=pltpu.PrefetchScalarGridSpec(
            num_scalar_prefetch=1,
            grid=(1,),
            in_specs=[whole((rows, width))] * 8,
            out_specs=[whole(o) for o in outs],
        ),
        out_shape=[shape_of(o, f32) for o in outs],
        compiler_params=ROOM,
        cost_estimate=moved(*[*own] * 6),
    )(where, *own, *other)


def ff_kernel(rows, cot, pair, down, hidden, grads):
    size = down.shape[0]
    for start in range(0, size, 512):
        part = slice(start, min(start + 512, size))
        gate = nt(rows[...], pair[0, part])
        up = nt(rows[...], pair[1, part])
        back = nt(cot[...], down[part])
        sig = jax.nn.sigmoid(gate)
        act = gate * sig
        hidden[:, part] = (act * up).astype(hidden.dtype)
        grads[0, :, part] = (back * up * (sig * (1.0 + gate * (1.0 - sig)))).astype(grads.dtype)
        grads[1, :, part] = (back * act).astype(grads.dtype)


def feed_forward(rows, cot, pair, down):
    count, width = rows.shape
    size = down.shape[0]
    block = 256
    line = lambda w: pl.BlockSpec((block, w), lambda i: (i, 0))
    return pl.pallas_call(
        ff_kernel,
        grid=(count // block,),
        in_specs=[line(width), line(width), whole(pair.shape), whole(down.shape)],
        out_specs=[line(size), pl.BlockSpec((2, block, size), lambda i: (0, i, 0))],
        out_shape=[shape_of((count, size)), shape_of((2, count, size))],
        compiler_params=pltpu.CompilerParams(vmem_limit_bytes=56 * 1024 * 1024),
        cost_estimate=pl.CostEstimate(
            flops=6 * count * width * size, transcendentals=count * size, bytes_accessed=40_000_000
        ),
    )(rows, cot, pair, down)


def to_near(slots):
    return [slots[0]] + [
        lax.ppermute(slots[k], "chip", [(i, i ^ k) for i in range(4)]) for k in range(1, len(slots))
    ]


def to_ahead(slots):
    count = len(slots)
    return [slots[0]] + [
        lax.ppermute(slots[j], "tensor", [(i, (i + j) % count) for i in range(count)])
        for j in range(1, count)
    ]


def total_of(sums):
    return sum(s.astype(f32) for s in sums).astype(bf16)


def sum_scattered(parts, chips, depth):
    flat = parts.reshape(-1, parts.shape[-1])
    summed = lax.psum_scatter(flat, "chip", scatter_dimension=0, tiled=True)
    return lax.psum_scatter(summed, "tensor", scatter_dimension=0, tiled=True)


def reduce_parts(parts, chips, depth):
    _, _, rows, columns = parts.shape
    full = lax.all_gather(sum_scattered(parts, chips, depth), GROUPS, axis=0)
    return full.reshape(chips, 2, rows, columns).astype(f32)


def cut(array, chips, axis):
    size = array.shape[axis] // chips
    return lax.dynamic_slice_in_dim(array, lax.axis_index("chip") * size, size, axis)


def on_device(
    layer_input,
    out_cotangent,
    norm_gains,
    proj_weight,
    beta_weight,
    conv_weight,
    head_gain,
    out_weight,
    mlp_weight,
    down_weight,
    seq_lengths,
    seq_order,
):
    rows, columns = layer_input.shape
    depth = lax.axis_size("tensor")
    chips = lax.axis_size("chip")
    groups = 2 * chips
    width = columns * depth
    own_rows = rows // 4
    core = lax.axis_index("core")

    def mine(array, axis):
        size = array.shape[axis] // 2
        return jnp.where(
            core == 0,
            lax.slice_in_dim(array, 0, size, axis=axis),
            lax.slice_in_dim(array, size, 2 * size, axis=axis),
        )

    chip, plane = lax.axis_index("chip"), lax.axis_index("tensor")
    few = chips == 4
    planes_behind = lax.rem(plane + depth - jnp.arange(depth, dtype=jnp.int32), depth)
    planes_ahead = lax.rem(plane + jnp.arange(depth, dtype=jnp.int32), depth)
    near = chip ^ jnp.arange(4, dtype=jnp.int32)
    where = jnp.concatenate([near, core[None]])
    everywhere = ("chip", "tensor")
    kinds = proj_weight.shape[0]
    heads_wide = depth * HD
    lines = width // chips
    hidden_half = down_weight.shape[0] // 2

    take, back, marks = routing(seq_lengths, seq_order, groups, rows, depth)
    layer_input, proj_weight = tie(deal(layer_input, groups), proj_weight)
    dealt_in = spread(layer_input)
    out_half = cut(mine(out_weight, 0), chips, 1)
    out_half = jnp.swapaxes(out_half.reshape(HD, -1, min(HD, lines)), 0, 1).reshape(-1, min(HD, lines))
    out_half = out_half.reshape(-1, HD)
    mixer_half = [cut(mine(proj_weight, 2), chips, 1).reshape(-1, HD), out_half]
    small_wide = jnp.concatenate([norm_gains.reshape(-1), mine(conv_weight, 2).reshape(-1)])
    high = lax.reduce_precision(small_wide, 8, 7)
    middle_term = lax.reduce_precision(small_wide - high, 8, 7)
    low_term = small_wide - high - middle_term
    small = [mine(beta_weight, 1).reshape(-1)] + [t.astype(bf16) for t in (high, middle_term, low_term)]
    small = jnp.concatenate(small).reshape(-1, HD)
    small_rows = small.shape[0]
    small_piece = -(-small_rows // (16 * chips)) * 16
    small = jnp.pad(small, ((0, small_piece * chips - small_rows), (0, 0)))
    mixer_half = jnp.concatenate(mixer_half + [cut(small, chips, 0)], axis=0)
    mixer_parts = lax.all_gather(mixer_half, everywhere, axis=0).reshape(chips, depth, -1, HD)
    small = jnp.swapaxes(mixer_parts[:, :, -small_piece:], 0, 1).reshape(depth, -1)
    wide_size = small_wide.shape[0]
    beta_proj = jnp.pad(small[:, :width].T, ((0, 0), (0, HD - depth)))
    high, middle_term, low_term = (
        small[:, width + n * wide_size : width + (n + 1) * wide_size].astype(f32) for n in range(3)
    )
    small_wide = high + (middle_term + low_term)
    gains = small_wide[:, : 2 * columns].reshape(depth, 2, columns)
    gains = jnp.swapaxes(gains, 0, 1).reshape(2, width)
    conv = small_wide[:, 2 * columns :].reshape(depth, 3, TAPS, HD)
    conv = conv.transpose(1, 2, 0, 3).reshape(3, TAPS, heads_wide)
    if few:
        proj, out_proj = mixer_weights(mixer_parts, beta_proj, kinds)
    else:
        proj = mixer_weights(mixer_parts, beta_proj, kinds)[0]
        out_proj = mixer_parts[:, :, kinds * lines : (kinds + 1) * lines].reshape(chips, depth, HD, lines)
        out_proj = out_proj.transpose(1, 2, 0, 3).reshape(heads_wide, width)
    down_half = cut(mine(down_weight, 0), chips, 1)
    down_slots = to_ahead([down_half] * depth) if few else [down_half]
    pair_half = cut(mine(jnp.swapaxes(mlp_weight, 1, 2), 1), chips, 2)
    dealt_in, down_slots, pair_half, dealt_cot = tie(dealt_in, down_slots, pair_half, deal(out_cotangent, groups))
    rows_own = deliver(reorder(dealt_in, take))
    rows_own, dealt_cot = tie(rows_own, dealt_cot)
    dealt_cot = spread(dealt_cot)
    pair_parts = lax.all_gather(pair_half.reshape(2 * hidden_half, -1), everywhere, axis=0)

    low = jnp.concatenate([rows_own, swap(rows_own)], axis=0)
    all_rows = low.astype(f32)
    scale_all = lax.rsqrt(jnp.mean(jnp.square(all_rows), axis=1, keepdims=True) + EPS)
    normed = (all_rows * scale_all * gains[0]).astype(bf16)
    projected = dot(normed, proj)
    gain_row = head_gain[None, :]

    projected, dealt_cot = tie(projected, dealt_cot)
    picked_cot = reorder(dealt_cot, take)
    down_plane = place(down_slots, planes_behind) if few else down_slots[0]
    projected, picked_cot, down_plane = tie(projected, picked_cot, down_plane)
    cot_own = deliver(picked_cot)
    if few:
        down_slots = to_near([down_plane.reshape(depth * hidden_half, -1)] * 4)
    else:
        down_slots = lax.all_gather(down_plane, everywhere, axis=0)
    gated, *saved = mixer_forward(marks, projected, conv, gain_row)

    rows_f = rows_own.astype(f32)
    scale_in = scale_all[:own_rows]
    out_of = lambda part: dot(part, out_proj)
    mixed = swap(out_of(gated[own_rows:]).astype(bf16))
    middle = rows_f + out_of(gated[:own_rows]) + mixed.astype(f32)
    scale_mid = lax.rsqrt(jnp.mean(jnp.square(middle), axis=1, keepdims=True) + EPS)
    normed_mid_own = (middle * scale_mid * gains[1]).astype(bf16)
    normed_mid_own, cot_own, down_slots = tie(normed_mid_own, cot_own, down_slots)
    if few:
        down = place_columns(down_slots, near)
    else:
        down = down_slots.reshape(chips, depth * hidden_half, -1).transpose(1, 0, 2).reshape(-1, width)
    cot = jnp.concatenate([cot_own, swap(cot_own)], axis=0)
    normed_mid = jnp.concatenate([normed_mid_own, swap(normed_mid_own)], axis=0)

    pair = ff_weights(pair_parts.reshape(chips, depth, 2 * hidden_half, -1), 2)
    hidden, grad_gate_up = feed_forward(normed_mid, cot, pair, down)

    grad_pair = jnp.einsum("ktf,td->kfd", grad_gate_up, normed_mid, preferred_element_type=f32).astype(bf16)
    grad_down = jnp.einsum("tf,td->fd", hidden, cot, preferred_element_type=f32).astype(bf16)
    if few:
        ff_terms = split_ff(grad_pair, grad_down, depth)
        grad_gate_up, hidden, ff_terms = tie(grad_gate_up, hidden, ff_terms)
        ff_chip = lax.psum_scatter(ff_terms.reshape(-1, lines), "chip", scatter_dimension=0, tiled=True)

    lower = swap(dot(hidden[own_rows:], down).astype(bf16))
    total = middle + dot(hidden[:own_rows], down) + lower.astype(f32)
    total_low, grad_gate_up = tie(total.astype(bf16), grad_gate_up)
    held_out = collect(total_low, groups)
    from_mlp = lambda part: jnp.einsum("ktf,kfd->td", part, pair, preferred_element_type=f32)
    came = swap(from_mlp(grad_gate_up[:, own_rows:]).astype(bf16))
    grad_normed_mid = from_mlp(grad_gate_up[:, :own_rows]) + came.astype(f32)
    mid_back, grad_gain_mid = norm_back(middle, scale_mid, gains[1], grad_normed_mid, width)
    grad_middle = cot_own.astype(f32) + mid_back
    grad_mix_own = grad_middle.astype(bf16)
    (grad_mix,) = tie(jnp.concatenate([grad_mix_own, swap(grad_mix_own)], axis=0))
    grad_gated = jnp.einsum("td,ed->te", grad_mix, out_proj, preferred_element_type=f32)
    grad_pre, grad_conv, grad_head = mixer_backward(marks, projected, conv, gain_row, saved, grad_gated)
    if few:
        grad_pre, held_out = tie(grad_pre, held_out)

    sent = send_back(grad_pre, proj)
    if few:
        sent, ff_chip = tie(sent, ff_chip)
        ff_own = lax.psum_scatter(ff_chip, "tensor", scatter_dimension=0, tiled=True)
    came = swap(sent)
    grad_input = keep_back(grad_pre, proj, came, rows_own, gains[0:1], grad_middle)
    grad_input, grad_pre, grad_mix = tie(grad_input, grad_pre, grad_mix)
    held_grad = collect(grad_input, groups)

    if few:
        mixer_terms = mixer_grads(
            normed,
            grad_pre,
            grad_mix,
            gated,
            proj,
            gains,
            grad_gain_mid[None],
            grad_conv,
            grad_head,
            near,
            depth,
            kinds,
        )
        _, ff_own = tie(mixer_terms[0], ff_own)
        sums = to_ahead(add_parts(to_near(mixer_terms), planes_ahead))
        sums, ff_own = tie(sums, lax.all_gather(ff_own, "chip", axis=0))
        ff_other = swap(ff_own)
        mixer_own = to_near([total_of(sums)] * 4)
        grad_pair_out, grad_down_out = join_ff(ff_own, ff_other, where)
    held_grad, held_out = tie(held_grad, held_out)
    both = jnp.concatenate([reorder(held_out, back), reorder(held_grad, back)], axis=2)
    both = bring_home(both, groups)
    layer_output, input_grad = both[:, :columns], both[:, columns:]
    if few:
        mixer_own, grad_pair_out, grad_down_out, layer_output, input_grad = tie(
            mixer_own, grad_pair_out, grad_down_out, layer_output, input_grad
        )
        mixer_sums = mixer_own, [swap(s) for s in mixer_own]
    if few:
        grad_proj_out, grad_out_out, small_sums = join_mixer(*mixer_sums, where, kinds, lines)
        across = lines // HD
        beta_sums = small_sums[:, :, :across].reshape(2, width)
        gain_sums = jnp.sum(small_sums[:, :, across : 3 * across], axis=1).reshape(2, 2, columns)
        conv_lines = 3 * TAPS // 4
        conv_sums = small_sums[:, :, 3 * across : 3 * across + conv_lines].reshape(2, 3, TAPS, HD)
        head_sums = small_sums[:, 0, 3 * across + conv_lines]
    else:
        every = jnp.concatenate([grad_pair, grad_down[None]], axis=0)
        every = every.reshape(3, depth, hidden_half, chips, lines).transpose(3, 1, 0, 2, 4)
        sums = reduce_parts(every.reshape(chips, depth, 3 * hidden_half, lines), chips, depth)
        sums = sums.reshape(chips, 2, 3, hidden_half, lines).transpose(2, 1, 3, 0, 4)
        sums = sums.reshape(3, 2 * hidden_half, width)
        grad_pair_out, grad_down_out = sums[:2], sums[2]
        grad_out = jnp.einsum("td,te->de", grad_mix, gated, preferred_element_type=f32).astype(bf16)
        grad_proj = jnp.einsum("td,te->de", normed, grad_pre, preferred_element_type=f32)
        grad_gain_in = jnp.sum(grad_proj * proj.astype(f32), axis=1) / gains[0]
        gain_parts = jnp.stack([grad_gain_in, grad_gain_mid]).reshape(2, depth, columns)
        small_terms = jnp.concatenate(
            [
                jnp.swapaxes(gain_parts, 0, 1).reshape(depth, -1),
                grad_proj[:, kinds * heads_wide : kinds * heads_wide + depth].T,
                grad_conv.reshape(3 * TAPS, depth, HD).transpose(1, 0, 2).reshape(depth, -1),
                jnp.broadcast_to(grad_head, (depth, HD)),
            ],
            axis=1,
        )
        small_count = small_terms.shape[1]
        small_lines = chips * -(-small_count // (chips * HD))
        small_terms = jnp.pad(small_terms, ((0, 0), (0, small_lines * HD - small_count)))
        small_terms = jnp.swapaxes(small_terms.reshape(depth, small_lines, HD), 0, 1).astype(bf16)
        grad_proj = grad_proj.astype(bf16)
        every = [
            grad_proj[:, : kinds * heads_wide].reshape(chips, lines, kinds, depth, HD).transpose(0, 3, 2, 1, 4),
            grad_out.reshape(chips, lines, 1, depth, HD).transpose(0, 3, 2, 1, 4),
            small_terms.reshape(chips, -1, 1, depth, HD).transpose(0, 3, 2, 1, 4),
        ]
        every = jnp.concatenate([e.reshape(chips, depth, -1, HD) for e in every], axis=2)
        sums = reduce_parts(every, chips, depth)
        many = sums[:, :, : (kinds + 1) * lines].reshape(chips, 2, kinds + 1, lines, HD)
        many = many.transpose(2, 0, 3, 1, 4).reshape(kinds + 1, width, 2 * HD)
        grad_proj_out, grad_out_out = many[:kinds], many[kinds].T
        small_sums = jnp.swapaxes(sums[:, :, (kinds + 1) * lines :], 0, 1).reshape(2, -1)
        gains_at, beta_at, conv_at = 2 * columns, 2 * columns + width, 2 * columns + width + 3 * TAPS * HD
        gain_sums = small_sums[:, :gains_at].reshape(2, 2, columns)
        beta_sums = small_sums[:, gains_at:beta_at]
        conv_sums = small_sums[:, beta_at:conv_at].reshape(2, 3, TAPS, HD)
        head_sums = small_sums[:, conv_at : conv_at + HD]
    grad_mlp_out = jnp.swapaxes(grad_pair_out, 1, 2)

    grad_gains = gain_sums[0] + gain_sums[1]
    grad_beta_out = beta_sums.T
    grad_conv_out = conv_sums.transpose(1, 2, 0, 3).reshape(3, TAPS, 2 * HD)
    grad_head_out = head_sums[0] + head_sums[1]
    return (
        layer_output,
        input_grad,
        grad_gains,
        grad_proj_out,
        grad_beta_out,
        grad_conv_out,
        grad_head_out,
        grad_out_out,
        grad_mlp_out,
        grad_down_out,
    )


def solution(mesh):
    devices = mesh.devices
    chips = devices.shape[0] // 2
    fine = Mesh(devices.reshape(chips, 2, devices.shape[1]), EVERY)
    return jax.shard_map(
        on_device,
        mesh=fine,
        in_specs=(
            P(GROUPS, "tensor"),
            P(GROUPS, "tensor"),
            P(None, "tensor"),
            P(None, None, "tensor"),
            P(None, "tensor"),
            P(None, None, "tensor"),
            P(),
            P("tensor", None),
            P(None, None, "tensor"),
            P("tensor", None),
            P(),
            P(),
        ),
        out_specs=(
            P(GROUPS, "tensor"),
            P(GROUPS, "tensor"),
            P(None, "tensor"),
            P(None, None, "tensor"),
            P(None, "tensor"),
            P(None, None, "tensor"),
            P(),
            P("tensor", None),
            P(None, None, "tensor"),
            P("tensor", None),
        ),
        check_vma=False,
    )
```
